128 devices in a mesh: lon: 32 (over z, x, y_hi), lat: 4 (over y_lo, core).
Axes of the slice: x: 4, y: 4 (y_hi: 2, y_lo: 2; y = y_hi * 2 + y_lo), z: 4, core: 2. Of those that a mesh axis runs over, the one named last changes fastest.
Arguments:
- field_in: bfloat16 [384, 1792, 128], P('lat', 'lon'), may hold values from -6 to 6
- conv_out: bfloat16 [384, 1792, 128], P('lat', 'lon'), may hold values from -6 to 6
- cotangent: bfloat16 [384, 1792, 128], P('lat', 'lon'), may hold values from -6 to 6
- kernel: float32 [49, 128], replicated, may hold values from -0.875 to 0.875
- ln_gain: float32 [128], replicated, may hold values from 0.5 to 1.5
- ln_bias: float32 [128], replicated, may hold values from -3 to 3
- w_in: bfloat16 [128, 512], replicated, may hold values from -0.5 to 0.5
- b_in: float32 [512], replicated, may hold values from -3 to 3
- w_out: bfloat16 [512, 128], replicated, may hold values from -0.25 to 0.25
- b_out: float32 [128], replicated, may hold values from -3 to 3
- layer_scale: float32 [128], replicated, may hold values from 0.5 to 1.5
Outputs:
- d_field: bfloat16 [384, 1792, 128], P('lat', 'lon')
- d_kernel: float32 [49, 128], replicated
- d_conv_bias: float32 [128], replicated
- d_ln_gain: float32 [128], replicated
- d_ln_bias: float32 [128], replicated
- d_w_in: float32 [128, 512], replicated
- d_b_in: float32 [512], replicated
- d_w_out: float32 [512, 128], replicated
- d_b_out: float32 [128], replicated
- d_layer_scale: float32 [128], replicated
- grad_norm: float32 [], replicated
The draws below stay inside these ranges and needn't reach their ends.
All inputs are finite; a program needn't handle non-finite values.
Results may differ from the reference program's by a relative error of at most 0.0075.
Values may be sent and summed in bfloat16 or wider, within the bound.
A program may use at most 64 MiB of HBM per device.

```python
import math
import jax
import jax.numpy as jnp
from jax import lax

C = 128
HID = 512
TAPS = 49
NLAT = 384
NLON = 1792


def levels(own_key, dims, shards, least, largest):
    gain = 1.0
    for position, blocks in shards:
        steps = jax.random.uniform(jax.random.fold_in(jax.random.fold_in(own_key, 6), position), (blocks,), jnp.float32, least / len(shards), largest / len(shards))
        gain = gain * jnp.repeat(jnp.exp(steps), dims[position] // blocks).reshape((-1,) + (1,) * (len(dims) - 1 - position))
    return gain


def scatter_about(own_key, shape, spread, reach, pieces=(), held_as=jnp.bfloat16):
    result = jax.random.normal(own_key, shape, jnp.float32) * spread
    if len(pieces) > 0:
        result = levels(own_key, shape, pieces, -0.22, 0.18) * result
    return jnp.clip(result, min=-reach, max=reach).astype(held_as)


def setup_inputs(seed: int = 0) -> dict:
    key_list = jax.random.split(jax.random.key(seed), 12)
    field_in = scatter_about(key_list[0], (NLAT, NLON, C), 1.0, 6.0, ((0, 4), (1, 32)))
    conv_out = scatter_about(key_list[1], (NLAT, NLON, C), 1.0, 6.0, ((0, 4), (1, 32)))
    cotangent = scatter_about(key_list[2], (NLAT, NLON, C), 1.0, 6.0, ((0, 4), (1, 32)))
    kernel = scatter_about(key_list[3], (TAPS, C), TAPS ** -0.5, 0.875, (), jnp.float32)
    ln_gain = jnp.clip(1.0 + 0.1 * jax.random.normal(key_list[4], (C,), jnp.float32), 0.5, 1.5)
    ln_bias = scatter_about(key_list[5], (C,), 0.5, 3.0, (), jnp.float32)
    w_in = scatter_about(key_list[6], (C, HID), C ** -0.5, 0.5)
    b_in = scatter_about(key_list[7], (HID,), 0.5, 3.0, (), jnp.float32)
    w_out = scatter_about(key_list[8], (HID, C), HID ** -0.5, 0.25)
    b_out = scatter_about(key_list[9], (C,), 0.5, 3.0, (), jnp.float32)
    layer_scale = jnp.clip(jax.random.uniform(key_list[10], (C,), jnp.float32, 0.5, 1.5), 0.5, 1.5)
    return {"field_in": field_in, "conv_out": conv_out, "cotangent": cotangent, "kernel": kernel, "ln_gain": ln_gain, "ln_bias": ln_bias, "w_in": w_in, "b_in": b_in, "w_out": w_out, "b_out": b_out, "layer_scale": layer_scale}


norm_eps = 1e-06
gelu_coef = 0.044715
gelu_root = math.sqrt(2.0 / math.pi)

def latitude_weight(row_ids, total_rows):
    place = (row_ids.astype(jnp.float32) + 0.5) / jnp.float32(total_rows) - 0.5
    return jnp.cos(jnp.float32(math.pi) * place)

def gelu_parts(pre):
    inner = gelu_root * (pre + gelu_coef * pre * pre * pre)
    tangent = jnp.tanh(inner)
    value = 0.5 * pre * (1.0 + tangent)
    slope = 0.5 * (1.0 + tangent) + 0.5 * pre * (1.0 - tangent * tangent) * gelu_root * (1.0 + 3.0 * gelu_coef * pre * pre)
    return (value, slope)

def channel_backward(conv_rows, dy_rows, ln_gain, ln_bias, w_in, b_in, w_out, b_out, layer_scale):
    values = conv_rows.astype(jnp.float32)
    center = values - lax.optimization_barrier(jnp.mean(values, -1, keepdims=True))
    rstd = lax.rsqrt(lax.optimization_barrier(jnp.mean(center * center, -1, keepdims=True)) + norm_eps)
    normed = center * rstd
    zed = (normed * ln_gain + ln_bias).astype(jnp.bfloat16)
    pre = jnp.dot(zed, w_in, preferred_element_type=jnp.float32) + b_in
    act_value, slope = gelu_parts(pre)
    act = act_value.astype(jnp.bfloat16)
    out = jnp.dot(act, w_out, preferred_element_type=jnp.float32) + b_out
    dy_values = dy_rows.astype(jnp.float32)
    g_scale = lax.optimization_barrier(jnp.sum(dy_values * out, 0))
    d_out = (layer_scale * dy_values).astype(jnp.bfloat16)
    g_b_out = lax.optimization_barrier(jnp.sum(d_out.astype(jnp.float32), 0))
    g_w_out = jnp.dot(act.T, d_out, preferred_element_type=jnp.float32)
    d_act = jnp.dot(d_out, w_out.T, preferred_element_type=jnp.float32)
    d_pre = (d_act * slope).astype(jnp.bfloat16)
    g_b_in = lax.optimization_barrier(jnp.sum(d_pre.astype(jnp.float32), 0))
    g_w_in = jnp.dot(zed.T, d_pre, preferred_element_type=jnp.float32)
    d_zed = jnp.dot(d_pre, w_in.T, preferred_element_type=jnp.float32)
    g_ln_gain = lax.optimization_barrier(jnp.sum(d_zed * normed, 0))
    g_ln_bias = lax.optimization_barrier(jnp.sum(d_zed, 0))
    d_norm = d_zed * ln_gain
    du_value = rstd * (d_norm - lax.optimization_barrier(jnp.mean(d_norm, -1, keepdims=True)) - normed * lax.optimization_barrier(jnp.mean(d_norm * normed, -1, keepdims=True)))
    du_rows = du_value.astype(jnp.bfloat16)
    g_conv_bias = lax.optimization_barrier(jnp.sum(du_rows.astype(jnp.float32), 0))
    return (du_rows, (g_conv_bias, g_ln_gain, g_ln_bias, g_w_in, g_b_in, g_w_out, g_b_out, g_scale))

def pad_grid(field):
    wrapped = jnp.concatenate([field[:, -3:], field, field[:, :3]], 1)
    return jnp.pad(wrapped, ((3, 3), (0, 0), (0, 0)))

def reference(field_in, conv_out, cotangent, kernel, ln_gain, ln_bias, w_in, b_in, w_out, b_out, layer_scale):
    blocks = NLAT // 8
    starts = jnp.arange(blocks, dtype=jnp.int32) * 8

    def first(carry, start):
        conv_rows = lax.dynamic_slice_in_dim(conv_out, start, 8, 0).reshape(8 * NLON, C)
        dy_rows = lax.dynamic_slice_in_dim(cotangent, start, 8, 0).reshape(8 * NLON, C)
        du_rows, parts = channel_backward(conv_rows, dy_rows, ln_gain, ln_bias, w_in, b_in, w_out, b_out, layer_scale)
        carry = tuple((total + part for total, part in zip(carry, parts)))
        return (carry, du_rows.reshape(8, NLON, C))
    zero_c = jnp.zeros((C,), jnp.float32)
    zero_h = jnp.zeros((HID,), jnp.float32)
    init = (zero_c, zero_c, zero_c, jnp.zeros((C, HID), jnp.float32), zero_h, jnp.zeros((HID, C), jnp.float32), zero_c, zero_c)
    sums, du_blocks = lax.scan(first, init, starts)
    du_full = du_blocks.reshape(NLAT, NLON, C)
    du_pad = pad_grid(du_full)
    field_pad = pad_grid(field_in)

    def second(carry, start):
        du_rows = lax.dynamic_slice_in_dim(du_pad, start, 14, 0).astype(jnp.float32)
        field_rows = lax.dynamic_slice_in_dim(field_pad, start, 14, 0).astype(jnp.float32)
        pad_cos = latitude_weight(start - 3 + jnp.arange(14, dtype=jnp.int32), NLAT)
        weighted = pad_cos[:, None, None] * field_rows
        inner = du_rows[3:11, 3:3 + NLON]
        conv_sum = jnp.zeros((8, NLON, C), jnp.float32)
        kernel_terms = []
        for lat_off in range(-3, 4):
            for lon_off in range(-3, 4):
                tap = (lat_off + 3) * 7 + lon_off + 3
                conv_sum = conv_sum + kernel[tap] * du_rows[3 - lat_off:11 - lat_off, 3 - lon_off:3 - lon_off + NLON]
                kernel_terms.append(lax.optimization_barrier(jnp.sum(inner * weighted[3 + lat_off:11 + lat_off, 3 + lon_off:3 + lon_off + NLON], (0, 1))))
        dy_rows = lax.dynamic_slice_in_dim(cotangent, start, 8, 0).astype(jnp.float32)
        row_cos = latitude_weight(start + jnp.arange(8, dtype=jnp.int32), NLAT)
        d_rows = (dy_rows + row_cos[:, None, None] * conv_sum).astype(jnp.bfloat16)
        return (carry + jnp.stack(kernel_terms), d_rows)
    kernel_sum, d_blocks = lax.scan(second, jnp.zeros((TAPS, C), jnp.float32), starts)
    d_field = d_blocks.reshape(NLAT, NLON, C)
    factor = jnp.float32(float(NLAT * NLON) ** (-0.5))
    scaled = tuple((part * factor for part in (kernel_sum,) + sums))
    grad_norm = jnp.sqrt(sum((jnp.sum(part * part) for part in scaled)))
    d_kernel, d_conv_bias, d_ln_gain, d_ln_bias, d_w_in, d_b_in, d_w_out, d_b_out, d_layer_scale = scaled
    return (d_field, d_kernel, d_conv_bias, d_ln_gain, d_ln_bias, d_w_in, d_b_in, d_w_out, d_b_out, d_layer_scale, grad_norm)
```

```python
import math

import jax
import jax.numpy as jnp
import ml_dtypes
import numpy as np
from jax import lax
from jax.experimental import pallas as pl
from jax.experimental.pallas import tpu as pltpu
from jax.sharding import PartitionSpec as P

MESH = pl.DeviceIdType.MESH
f32, bf16 = jnp.float32, jnp.bfloat16
EPS = 1e-06
COEF = 0.044715
ROOT = math.sqrt(2.0 / math.pi)

N = 14
OUT = 8
PAIRS = 104
FREQ = 2 * PAIRS
SCALE = 1.828125
LAT_ROWS, COLS, CH, HID, TAPS = 96, 56, 128, 512, 49
TL, TC = LAT_ROWS // OUT, COLS // OUT
CHUNK = 32
SUB = 896
SMALL = 64


def tables():
    own = [(0, 0), (0, 7), (7, 0), (7, 7)]
    seen, pairs = set(own), []
    for k in range(N):
        for l in range(N):
            if (k, l) not in seen:
                seen.add((k, l))
                seen.add(((-k) % N, (-l) % N))
                pairs.append((k, l))
    freq = np.array(own + pairs)
    weight = np.array([1.0] * 4 + [2.0] * 96)[:, None] / (N * N)
    twin = np.array([0.0] * 4 + [1.0] * 96)[:, None]

    def angle(rows, cols, row_off, col_off):
        m, n = np.meshgrid(np.arange(rows) + row_off, np.arange(cols) + col_off, indexing="ij")
        m, n = m.ravel(), n.ravel()
        return 2 * np.pi * ((np.outer(freq[:, 0], m) + np.outer(freq[:, 1], n)) % N) / N

    def interleave(re, im):
        fill = np.zeros((PAIRS - 100, re.shape[1]))
        re, im = np.concatenate([re, fill]), np.concatenate([im, fill])
        shape = (PAIRS // 8, 8, re.shape[1])
        return np.stack([re.reshape(shape), im.reshape(shape)], 1).reshape(FREQ, -1)

    inside = np.tile(np.array([0.0] + [1.0] * 14 + [0.0]), N)
    a = angle(N, 16, 0, -1)
    fwd = interleave(np.cos(a) * inside, -np.sin(a) * inside * twin)
    a = angle(OUT, OUT, 6, 6)
    fwd_tile = interleave(np.cos(a), -np.sin(a) * twin)
    inv = interleave(np.cos(a) * weight, -np.sin(a) * weight * twin).T
    a = angle(7, 7, 0, 0)
    taps = interleave(np.cos(a), -np.sin(a) * twin)
    taps_inv = interleave(np.cos(a) * weight, -np.sin(a) * weight * twin).T
    area = N * N
    return (
        (fwd * SCALE).astype(ml_dtypes.bfloat16),
        (fwd_tile * SCALE).astype(ml_dtypes.bfloat16),
        (inv * area * SCALE).astype(ml_dtypes.bfloat16),
        (np.pad(taps, ((0, 0), (0, 7))) / (area * SCALE * SCALE)).astype(np.float32),
        (np.pad(taps_inv, ((0, 7), (0, 0))) / (SCALE * SCALE)).astype(np.float32),
    )


def dot(a, b):
    return jnp.dot(a, b, preferred_element_type=f32)


def dot_exact(a, b):
    return jnp.dot(a, b, preferred_element_type=f32, precision=lax.Precision.HIGHEST)


def dot_last(a, b):
    return lax.dot_general(a, b, (((1,), (1,)), ((), ())), preferred_element_type=f32)


def dot_rows(a, b):
    return lax.dot_general(a, b, (((0,), (0,)), ((), ())), preferred_element_type=f32)


def rows8(v):
    return jnp.sum(v.reshape(v.shape[0] // 8, 8, v.shape[1]), 0)


def make_kernel(nz, nx, nyh, nyl, ncore, total_cells):
    nlon, nlat = nz * nx * nyh, nyl * ncore
    ny = nyh * nyl
    nb, na = nz * ny, nx * ncore
    wrows = 2 * CH // nb
    cells = LAT_ROWS * COLS
    step = CHUNK * COLS
    steps = LAT_ROWS // CHUNK
    factor = float(total_cells) ** (-0.5)

    def kernel(
        x_hbm, c_hbm, f_hbm, ker_ref, gain_ref, bias_ref, win_ref, bin_ref, wout_ref, bout_ref, ls_ref,
        cos_ref, mf_ref, mg_ref, mi_ref, mk_ref, md_ref,
        out_hbm, dk_ref, dcb_ref, dgain_ref, dbias_ref, dwin_ref, dbin_ref, dwout_ref, dbout_ref, dls_ref, norm_ref,
        xv, cv, fv, outv, dup, fs, yb, kpad, kh, acc, gw, gbin, small, sm32,
        hs, hr, vs, vr, ws, wr, w2, wf, s1, s2,
        in_sem, out_sem, h_send, h_recv, v_send, v_recv,
        w1_send, w1_recv, w2_send, w2_recv, w3_send, w3_recv, s1_send, s1_recv, s2_send, s2_recv,
    ):
        lon, lat = lax.axis_index("lon"), lax.axis_index("lat")
        z, x, yh = lax.div(lon, nx * nyh), lax.rem(lax.div(lon, nyh), nx), lax.rem(lon, nyh)
        yl, core = lax.div(lat, ncore), lax.rem(lat, ncore)
        b_me = z * ny + yh * nyl + yl
        a_me = x * ncore + core

        def b_peer(b):
            bz, by = lax.div(b, ny), lax.rem(b, ny)
            return (bz * (nx * nyh) + x * nyh + lax.div(by, nyl), lax.rem(by, nyl) * ncore + core)

        def a_peer(a):
            return (z * (nx * nyh) + lax.div(a, ncore) * nyh + yh, yl * ncore + lax.rem(a, ncore))

        right, left = lax.rem(lon + 1, nlon), lax.rem(lon + nlon - 1, nlon)
        down, up = lax.rem(lat + 1, nlat), lax.rem(lat + nlat - 1, nlat)

        def load(i, which):
            src, dst = ((x_hbm, xv), (c_hbm, cv), (f_hbm, fv))[which]
            rows = pl.ds(i * step, step)
            return pltpu.make_async_copy(src.at[rows], dst.at[rows], in_sem.at[which, i])

        for i in range(steps):
            for which in range(3):
                load(i, which).start()

        barrier = pltpu.get_barrier_semaphore()
        for peer in ((right, lat), (left, lat), (lon, down), (lon, up)):
            pl.semaphore_signal(barrier, inc=1, device_id=peer, device_id_type=MESH)

        def greet_b(d, carry):
            pl.semaphore_signal(barrier, inc=1, device_id=b_peer(lax.rem(b_me + d, nb)), device_id_type=MESH)
            return carry

        def greet_a(d, carry):
            pl.semaphore_signal(barrier, inc=1, device_id=a_peer(lax.rem(a_me + d, na)), device_id_type=MESH)
            return carry

        lax.fori_loop(1, nb, greet_b, 0)
        lax.fori_loop(1, na, greet_a, 0)

        third = jnp.full((CH, CH), 1.0 / CH, bf16)
        none = jnp.zeros((CH, CH), bf16)
        mean_two = jnp.concatenate(
            [jnp.concatenate([third, none], 1), jnp.concatenate([none, third], 1)], 0
        )
        gain, bias, scale = gain_ref[...], bias_ref[...], ls_ref[...]
        gw[...] = jnp.zeros_like(gw)
        gbin[...] = jnp.zeros_like(gbin)
        small[...] = jnp.zeros_like(small)
        acc[...] = jnp.zeros_like(acc)
        kpad[...] = jnp.zeros_like(kpad)
        kpad[0:TAPS] = ker_ref[...]
        kh[...] = dot_exact(mk_ref[...], kpad[...])

        def mlp(i, carry):
            for which in range(3):
                rows_hbm = pl.ds(pl.multiple_of(i * step, step), step)
                src, dst = ((x_hbm, xv), (c_hbm, cv), (f_hbm, fv))[which]
                pltpu.make_async_copy(src.at[rows_hbm], dst.at[rows_hbm], in_sem.at[which, i]).wait()
            rows = pl.ds(pl.multiple_of(i * step, step), step)
            xb, cb = xv[rows, :], cv[rows, :]
            center = xb.astype(f32) - dot(xb, third)
            rstd = lax.rsqrt(dot((center * center).astype(bf16), third) + EPS)
            normed = center * rstd
            zed = (normed * gain + bias).astype(bf16)
            cot = cb.astype(f32)
            d_out = (cot * scale).astype(bf16)
            acts, dpres = [], []
            g_bin = jnp.zeros((8, HID), f32)
            for s in range(0, step, SUB):
                h = dot(zed[s : s + SUB], win_ref[...]) + bin_ref[...]
                d_act = dot_last(d_out[s : s + SUB], wout_ref[...])
                h2 = h * h
                inner = h * (ROOT + (ROOT * COEF) * h2)
                wide = h * (2 * ROOT + (6 * ROOT * COEF) * h2)
                gate = 0.5 * jnp.tanh(inner) + 0.5
                d_pre = d_act * (gate * (1.0 + (1.0 - gate) * wide))
                g_bin = g_bin + rows8(d_pre)
                acts.append((h * gate).astype(bf16))
                dpres.append(d_pre.astype(bf16))
            act, d_pre = jnp.concatenate(acts, 0), jnp.concatenate(dpres, 0)
            gbin[...] += g_bin
            gw[CH:, :] += dot_rows(cb, act)
            gw[:CH, :] += dot_rows(zed, d_pre)
            d_zed = dot_last(d_pre, win_ref[...])
            d_gain = d_zed * normed
            d_norm = d_zed * gain
            means = dot(
                jnp.concatenate([d_norm.astype(bf16), (d_gain * gain).astype(bf16)], 1), mean_two
            )
            du = rstd * (d_norm - means[:, :CH] - normed * means[:, CH:])
            dup[pl.ds(3 + i * CHUNK, CHUNK), 4 : 4 + COLS, :] = du.reshape(CHUNK, COLS, CH)
            small[0] += rows8(d_gain)
            small[1] += rows8(d_zed)
            small[2] += rows8(du)
            small[3] += rows8(cot)
            field = fv[rows, :].astype(f32).reshape(CHUNK, COLS, CH)
            for r in range(CHUNK):
                fs[i * CHUNK + r] = field[r] * cos_ref[lat * LAT_ROWS + i * CHUNK + r]
            return carry

        lax.fori_loop(0, steps, mlp, 0)

        half = LAT_ROWS // 2
        low = lax.broadcasted_iota(jnp.int32, (half, 8, CH), 1) < 4

        def copy_h(side):
            return pltpu.make_async_remote_copy(
                src_ref=hs.at[side], dst_ref=hr.at[side], send_sem=h_send.at[side], recv_sem=h_recv.at[side],
                device_id=((right, lat), (left, lat))[side], device_id_type=MESH,
            )

        def copy_v(side):
            return pltpu.make_async_remote_copy(
                src_ref=vs.at[side], dst_ref=vr.at[side], send_sem=v_send.at[side], recv_sem=v_recv.at[side],
                device_id=((lon, down), (lon, up))[side], device_id_type=MESH,
            )

        pl.semaphore_wait(barrier, 4 + (nb - 1) + (na - 1))
        first, second = dup[3 : 3 + half, 56:64, :], dup[3 + half : 3 + LAT_ROWS, 56:64, :]
        hs[0] = jnp.where(low, first, pltpu.roll(second, 4, 1)).reshape(half * 8, CH).astype(bf16)
        copy_h(0).start()
        first, second = dup[3 : 3 + half, 0:8, :], dup[3 + half : 3 + LAT_ROWS, 0:8, :]
        hs[1] = jnp.where(low, pltpu.roll(second, 4, 1), first).reshape(half * 8, CH).astype(bf16)
        copy_h(1).start()

        def copy_w1(b_to, b_from):
            return pltpu.make_async_remote_copy(
                src_ref=ws.at[b_to], dst_ref=wr.at[b_from], send_sem=w1_send.at[b_to], recv_sem=w1_recv.at[b_from],
                device_id=b_peer(b_to), device_id_type=MESH,
            )

        ws[...] = gw[...].astype(bf16).reshape(nb, wrows, HID)

        def send_w1(d, carry):
            copy_w1(lax.rem(b_me + d, nb), b_me).start()
            return carry

        lax.fori_loop(1, nb, send_w1, 0)

        def tile_pair(slot, i0, i1, t):
            def window(i):
                return dup[pl.ds(i * OUT, N), 8 * t : 8 * t + 16, :].reshape(N * 16, CH).astype(bf16)

            def field(i):
                return fs[pl.ds(i * OUT, OUT), 8 * t : 8 * t + 8, :].reshape(OUT * OUT, CH).astype(bf16)

            shape = (PAIRS // 8, 2, 8, 2 * CH)
            w = dot(mf_ref[...], jnp.concatenate([window(i0), window(i1)], 1)).reshape(shape)
            g = dot(mg_ref[...], jnp.concatenate([field(i0), field(i1)], 1)).reshape(shape)
            k = kh[...].reshape(PAIRS // 8, 2, 8, CH)
            k = jnp.concatenate([k, k], -1)
            w_re, w_im, g_re, g_im, k_re, k_im = w[:, 0], w[:, 1], g[:, 0], g[:, 1], k[:, 0], k[:, 1]
            y = jnp.stack([k_re * w_re - k_im * w_im, k_re * w_im + k_im * w_re], 1)
            yb[slot] = y.reshape(FREQ, 2 * CH).astype(bf16)
            d = jnp.stack([g_re * w_re + g_im * w_im, g_im * w_re - g_re * w_im], 1).reshape(FREQ, 2 * CH)
            acc[...] += d[:, :CH] + d[:, CH:]

        def middle(j, carry):
            for t in range(1, TC - 1):
                tile_pair(j * TC + t, 1 + 2 * j, 2 + 2 * j, t)
            return carry

        def sides(j, carry):
            for t in (0, TC - 1):
                tile_pair(j * TC + t, 1 + 2 * j, 2 + 2 * j, t)
            return carry

        lax.fori_loop(0, 3, middle, 0)

        copy_h(0).wait_recv()
        copy_h(1).wait_recv()
        near = hr[0].astype(f32).reshape(half, 8, CH)
        dup[3 : 3 + half, 0:8, :] = jnp.where(low, near, dup[3 : 3 + half, 0:8, :])
        dup[3 + half : 3 + LAT_ROWS, 0:8, :] = jnp.where(
            low, pltpu.roll(near, 4, 1), dup[3 + half : 3 + LAT_ROWS, 0:8, :]
        )
        near = hr[1].astype(f32).reshape(half, 8, CH)
        dup[3 : 3 + half, 56:64, :] = jnp.where(low, dup[3 : 3 + half, 56:64, :], near)
        dup[3 + half : 3 + LAT_ROWS, 56:64, :] = jnp.where(
            low, dup[3 + half : 3 + LAT_ROWS, 56:64, :], pltpu.roll(near, 4, 1)
        )
        vs[0] = dup[LAT_ROWS : LAT_ROWS + 3].reshape(192, CH).astype(bf16)
        vs[1] = dup[3:6].reshape(192, CH).astype(bf16)
        copy_v(0).start()
        copy_v(1).start()

        lax.fori_loop(3, 5, middle, 0)

        def copy_w2(a_to, a_from):
            return pltpu.make_async_remote_copy(
                src_ref=w2.at[a_me], dst_ref=w2.at[a_from], send_sem=w2_send.at[a_to], recv_sem=w2_recv.at[a_from],
                device_id=a_peer(a_to), device_id_type=MESH,
            )

        wr[b_me] = ws[b_me]

        def wait_w1(d, carry):
            b = lax.rem(b_me + d, nb)
            copy_w1(b, b).wait_recv()
            return carry

        lax.fori_loop(1, nb, wait_w1, 0)
        w2[a_me] = jnp.sum(wr[...].astype(f32), 0).astype(bf16)

        def send_w2(d, carry):
            copy_w2(lax.rem(a_me + d, na), a_me).start()
            return carry

        lax.fori_loop(1, na, send_w2, 0)

        lax.fori_loop(0, 5, sides, 0)

        copy_v(0).wait_recv()
        copy_v(1).wait_recv()
        zero = jnp.zeros((3, 64, CH), f32)
        dup[0:3] = jnp.where(lat > 0, vr[0].astype(f32).reshape(3, 64, CH), zero)
        dup[LAT_ROWS + 3 : LAT_ROWS + 6] = jnp.where(lat < nlat - 1, vr[1].astype(f32).reshape(3, 64, CH), zero)
        for t in range(TC):
            tile_pair(5 * TC + t, 0, TL - 1, t)

        sm32[...] = jnp.zeros_like(sm32)
        sm32[0:56] = dot_exact(md_ref[...], acc[...])
        total = jnp.sum(gbin[...], 0, keepdims=True)
        for q in range(4):
            sm32[49 + q : 50 + q] = total[:, q * CH : (q + 1) * CH]
            sm32[53 + q : 54 + q] = jnp.sum(small[q], 0, keepdims=True)
        s1[a_me] = sm32[...].astype(bf16)

        def copy_s1(a_to, a_from):
            return pltpu.make_async_remote_copy(
                src_ref=s1.at[a_me], dst_ref=s1.at[a_from], send_sem=s1_send.at[a_to], recv_sem=s1_recv.at[a_from],
                device_id=a_peer(a_to), device_id_type=MESH,
            )

        def copy_s2(b_to, b_from):
            return pltpu.make_async_remote_copy(
                src_ref=s2.at[b_me], dst_ref=s2.at[b_from], send_sem=s2_send.at[b_to], recv_sem=s2_recv.at[b_from],
                device_id=b_peer(b_to), device_id_type=MESH,
            )

        def copy_w3(b_to, b_from):
            return pltpu.make_async_remote_copy(
                src_ref=wf.at[b_me], dst_ref=wf.at[b_from], send_sem=w3_send.at[b_to], recv_sem=w3_recv.at[b_from],
                device_id=b_peer(b_to), device_id_type=MESH,
            )

        def over_a(copy, act):
            def body(d, carry):
                peer = lax.rem(a_me + d, na)
                if act == "send":
                    copy(peer, a_me).start()
                elif act == "recv":
                    copy(peer, peer).wait_recv()
                else:
                    copy(peer, a_me).wait_send()
                return carry

            lax.fori_loop(1, na, body, 0)

        def over_b(copy, act):
            def body(d, carry):
                peer = lax.rem(b_me + d, nb)
                if act == "send":
                    copy(peer, b_me).start()
                elif act == "recv":
                    copy(peer, peer).wait_recv()
                else:
                    copy(peer, b_me).wait_send()
                return carry

            lax.fori_loop(1, nb, body, 0)

        over_a(copy_s1, "send")
        over_a(copy_w2, "recv")
        wf[b_me] = jnp.sum(w2[...].astype(f32), 0).astype(bf16)

        def store(i):
            rows = pl.ds(i * (OUT * COLS), OUT * COLS)
            return pltpu.make_async_copy(outv.at[rows], out_hbm.at[rows], out_sem.at[i])

        def finish_pair(j, i0, i1):
            tiles = [dot(mi_ref[...], yb[j * TC + t]).reshape(OUT, OUT, 2 * CH) for t in range(TC)]
            conv = jnp.concatenate(tiles, 1)
            for n, i in ((0, i0), (1, i1)):
                rows = pl.ds(pl.multiple_of(i * (OUT * COLS), OUT * COLS), OUT * COLS)
                cot = cv[rows, :].astype(f32).reshape(OUT, COLS, CH)
                part = conv[:, :, n * CH : (n + 1) * CH]
                value = [cot[r] + part[r] * cos_ref[lat * LAT_ROWS + i * OUT + r] for r in range(OUT)]
                outv[rows, :] = jnp.concatenate(value, 0).astype(bf16)
                store(i).start()

        def finish(j, carry):
            finish_pair(j, 1 + 2 * j, 2 + 2 * j)
            return carry

        over_a(copy_s1, "recv")
        s2[b_me] = jnp.sum(s1[...].astype(f32), 0).astype(bf16)
        over_b(copy_s2, "send")
        over_b(copy_w3, "send")
        lax.fori_loop(0, 5, finish, 0)
        finish_pair(5, 0, TL - 1)

        over_b(copy_w3, "recv")
        d_win = jnp.concatenate([wf[b].astype(f32) for b in range(nb // 2)], 0) * factor
        dwin_ref[...] = d_win
        g_out = jnp.concatenate([wf[b].astype(f32) for b in range(nb // 2, nb)], 0) * factor
        g_out = g_out.T
        d_wout = g_out * scale
        dwout_ref[...] = d_wout
        over_b(copy_s2, "recv")
        sums = jnp.sum(s2[...].astype(f32), 0) * factor
        sm32[...] = sums
        dk = sm32[0:TAPS]
        d_bin = jnp.concatenate([sm32[49 + q : 50 + q] for q in range(4)], 1)
        d_gain, d_bias, d_cb, s_cot = (sm32[53 + q : 54 + q] for q in range(4))
        d_bout = s_cot * scale
        d_ls = jnp.sum(g_out * wout_ref[...].astype(f32), 0, keepdims=True) + bout_ref[...] * s_cot
        dk_ref[...] = dk
        dbin_ref[...] = d_bin
        dgain_ref[...] = d_gain
        dbias_ref[...] = d_bias
        dcb_ref[...] = d_cb
        dbout_ref[...] = d_bout
        dls_ref[...] = d_ls
        squares = jnp.sum(d_win * d_win, 0, keepdims=True) + jnp.sum(d_bin * d_bin, 0, keepdims=True)
        squares = sum(squares[:, q * CH : (q + 1) * CH] for q in range(4))
        squares = squares + jnp.sum(d_wout * d_wout, 0, keepdims=True) + jnp.sum(dk * dk, 0, keepdims=True)
        for part in (d_gain, d_bias, d_cb, d_bout, d_ls):
            squares = squares + part * part
        norm_ref[...] = jnp.sqrt(jnp.sum(squares, 1, keepdims=True))

        for side in range(2):
            copy_h(side).wait_send()
            copy_v(side).wait_send()
        over_b(copy_w1, "done")
        over_a(copy_w2, "done")
        over_b(copy_w3, "done")
        over_a(copy_s1, "done")
        over_b(copy_s2, "done")

        def drain(i, carry):
            store(i).wait()
            return carry

        lax.fori_loop(0, TL, drain, 0)

    hbm, vmem, smem = (pl.BlockSpec(memory_space=m) for m in (pl.ANY, pltpu.VMEM, pltpu.SMEM))
    shape = jax.ShapeDtypeStruct
    dma = pltpu.SemaphoreType.DMA
    return pl.pallas_call(
        kernel,
        in_specs=[hbm] * 3 + [vmem] * 8 + [smem] + [vmem] * 5,
        out_specs=[hbm] + [vmem] * 10,
        out_shape=[
            shape((cells, CH), bf16),
            shape((TAPS, CH), f32),
            shape((1, CH), f32),
            shape((1, CH), f32),
            shape((1, CH), f32),
            shape((CH, HID), f32),
            shape((1, HID), f32),
            shape((HID, CH), f32),
            shape((1, CH), f32),
            shape((1, CH), f32),
            shape((1, 1), f32),
        ],
        scratch_shapes=[
            pltpu.VMEM((cells, CH), bf16),
            pltpu.VMEM((cells, CH), bf16),
            pltpu.VMEM((cells, CH), bf16),
            pltpu.VMEM((cells, CH), bf16),
            pltpu.VMEM((LAT_ROWS + 6, COLS + 8, CH), f32),
            pltpu.VMEM((LAT_ROWS, COLS, CH), f32),
            pltpu.VMEM((TL * TC // 2, FREQ, 2 * CH), bf16),
            pltpu.VMEM((56, CH), f32),
            pltpu.VMEM((FREQ, CH), f32),
            pltpu.VMEM((FREQ, CH), f32),
            pltpu.VMEM((2 * CH, HID), f32),
            pltpu.VMEM((8, HID), f32),
            pltpu.VMEM((4, 8, CH), f32),
            pltpu.VMEM((SMALL, CH), f32),
            pltpu.VMEM((2, LAT_ROWS * 4, CH), bf16),
            pltpu.VMEM((2, LAT_ROWS * 4, CH), bf16),
            pltpu.VMEM((2, 192, CH), bf16),
            pltpu.VMEM((2, 192, CH), bf16),
            pltpu.VMEM((nb, wrows, HID), bf16),
            pltpu.VMEM((nb, wrows, HID), bf16),
            pltpu.VMEM((na, wrows, HID), bf16),
            pltpu.VMEM((nb, wrows, HID), bf16),
            pltpu.VMEM((na, SMALL, CH), bf16),
            pltpu.VMEM((nb, SMALL, CH), bf16),
            dma((3, steps)),
            dma((TL,)),
            dma((2,)),
            dma((2,)),
            dma((2,)),
            dma((2,)),
            dma((nb,)),
            dma((nb,)),
            dma((na,)),
            dma((na,)),
            dma((nb,)),
            dma((nb,)),
            dma((na,)),
            dma((na,)),
            dma((nb,)),
            dma((nb,)),
        ],
        compiler_params=pltpu.CompilerParams(
            collective_id=0, has_side_effects=True, vmem_limit_bytes=60 * 2**20
        ),
        cost_estimate=pl.CostEstimate(flops=6 * 10**9, bytes_accessed=6 * 10**6, transcendentals=3 * 10**6),
        name="block_backward",
    )


def solution(mesh):
    nlon, nlat = mesh.shape["lon"], mesh.shape["lat"]
    nz, nx, nyh = (4, 4, 2) if nlon == 32 else (nlon, 1, 1)
    nyl, ncore = nlat // 2, 2
    total_rows, total_cols = LAT_ROWS * nlat, COLS * nlon
    call = make_kernel(nz, nx, nyh, nyl, ncore, total_rows * total_cols)
    fwd, fwd_tile, inv, taps, taps_inv = tables()
    place = (np.arange(total_rows, dtype=np.float32) + np.float32(0.5)) / np.float32(total_rows) - np.float32(0.5)
    weight = np.cos(np.float32(math.pi) * place).astype(np.float32)

    def on_device(field_in, conv_out, cotangent, kernel, ln_gain, ln_bias, w_in, b_in, w_out, b_out, layer_scale):
        rows, cols, width = conv_out.shape
        flat = lambda v: v.reshape(rows * cols, width)
        line = lambda v: v.reshape(1, -1)
        outs = call(
            flat(conv_out), flat(cotangent), flat(field_in), kernel, line(ln_gain), line(ln_bias), w_in, line(b_in),
            w_out, line(b_out), line(layer_scale), weight, fwd, fwd_tile, inv, taps, taps_inv,
        )
        d_field, d_kernel, d_cb, d_gain, d_bias, d_win, d_bin, d_wout, d_bout, d_ls, norm = outs
        wide = lambda v: v.reshape(-1)
        return (
            d_field.reshape(rows, cols, width), d_kernel, wide(d_cb), wide(d_gain), wide(d_bias), d_win, wide(d_bin),
            d_wout, wide(d_bout), wide(d_ls), norm.reshape(()),
        )

    grid = P("lat", "lon", None)
    return jax.shard_map(
        on_device,
        mesh=mesh,
        in_specs=(grid, grid, grid) + (P(),) * 8,
        out_specs=(grid,) + (P(),) * 10,
        check_vma=False,
    )
```

```python
import math

import jax
import jax.numpy as jnp
import ml_dtypes
import numpy as np
from jax import lax
from jax.experimental import pallas as pl
from jax.experimental.pallas import tpu as pltpu
from jax.sharding import PartitionSpec as P

MESH = pl.DeviceIdType.MESH
f32, bf16 = jnp.float32, jnp.bfloat16
EPS = 1e-06
COEF = 0.044715
ROOT = math.sqrt(2.0 / math.pi)

N = 14
OUT = 8
PAIRS = 104
FREQ = 2 * PAIRS
SCALE = 1.828125
LAT_ROWS, COLS, CH, HID, TAPS = 96, 56, 128, 512, 49
TL, TC = LAT_ROWS // OUT, COLS // OUT
SMALL = 64
RIM = ((0, 0, LAT_ROWS), (TC - 1, 0, LAT_ROWS))


def tables():
    own = [(0, 0), (0, 7), (7, 0), (7, 7)]
    seen, pairs = set(own), []
    for k in range(N):
        for l in range(N):
            if (k, l) not in seen:
                seen.add((k, l))
                seen.add(((-k) % N, (-l) % N))
                pairs.append((k, l))
    freq = np.array(own + pairs)
    weight = np.array([1.0] * 4 + [2.0] * 96)[:, None] / (N * N)
    twin = np.array([0.0] * 4 + [1.0] * 96)[:, None]

    def angle(rows, cols, row_off, col_off):
        m, n = np.meshgrid(np.arange(rows) + row_off, np.arange(cols) + col_off, indexing="ij")
        m, n = m.ravel(), n.ravel()
        return 2 * np.pi * ((np.outer(freq[:, 0], m) + np.outer(freq[:, 1], n)) % N) / N

    def interleave(re, im):
        fill = np.zeros((PAIRS - 100, re.shape[1]))
        re, im = np.concatenate([re, fill]), np.concatenate([im, fill])
        shape = (PAIRS // 8, 8, re.shape[1])
        return np.stack([re.reshape(shape), im.reshape(shape)], 1).reshape(FREQ, -1)

    inside = np.tile(np.array([0.0] + [1.0] * 14 + [0.0]), N)
    a = angle(N, 16, 0, -1)
    fwd = interleave(np.cos(a) * inside, -np.sin(a) * inside * twin)
    a = angle(OUT, OUT, 6, 6)
    fwd_tile = interleave(np.cos(a), -np.sin(a) * twin)
    inv = interleave(np.cos(a) * weight, -np.sin(a) * weight * twin).T
    a = angle(7, 7, 0, 0)
    taps = interleave(np.cos(a), -np.sin(a) * twin)
    taps_inv = interleave(np.cos(a) * weight, -np.sin(a) * weight * twin).T
    area = N * N
    return (
        (fwd * SCALE).astype(ml_dtypes.bfloat16),
        (fwd_tile * SCALE).astype(ml_dtypes.bfloat16),
        (inv * area * SCALE).astype(ml_dtypes.bfloat16),
        (np.pad(taps, ((0, 0), (0, 7))) / (area * SCALE * SCALE)).astype(np.float32),
        (np.pad(taps_inv, ((0, 7), (0, 0))) / (SCALE * SCALE)).astype(np.float32),
    )


def dot(a, b):
    return jnp.dot(a, b, preferred_element_type=f32)


def dot_exact(a, b):
    return jnp.dot(a, b, preferred_element_type=f32, precision=lax.Precision.HIGHEST)


def dot_last(a, b):
    return lax.dot_general(a, b, (((1,), (1,)), ((), ())), preferred_element_type=f32)


def dot_rows(a, b):
    return lax.dot_general(a, b, (((0,), (0,)), ((), ())), preferred_element_type=f32)


def rows8(v):
    return jnp.sum(v.reshape(v.shape[0] // 8, 8, v.shape[1]), 0)


def make_kernel(nz, nx, nyh, nyl, ncore, total_cells):
    nlon, nlat = nz * nx * nyh, nyl * ncore
    ny = nyh * nyl
    nb, na = nz * ny, nx * ncore
    wrows = 2 * CH // nb
    srows = SMALL // na
    factor = float(total_cells) ** (-0.5)

    def kernel(
        x_hbm, c_hbm, f_hbm, ker_hbm, gain_ref, bias_ref, win_ref, bin_ref, wout_ref, bout_ref, ls_ref,
        cos_ref, mf_hbm, mg_hbm, mi_hbm, mk_hbm, md_hbm,
        out_hbm, dk_ref, dcb_ref, dgain_ref, dbias_ref, dwin_ref, dbin_ref, dwout_ref, dbout_ref, dls_ref, norm_ref,
        xv, cv, fv, outv, dup, yb, mf, mg, mi, mk, md, ker, kpad, kh, acc, gw, gbin, small, sm32,
        hs, hr, vs, vr, ws, wr, w2, wf, s0, s1, s2, s3,
        in_sem, const_sem, out_sem, h_send, h_recv, v_send, v_recv,
        w1_send, w1_recv, w2_send, w2_recv, w3_send, w3_recv, s1_send, s1_recv, s2_send, s2_recv, s3_send, s3_recv,
    ):
        lon, lat = lax.axis_index("lon"), lax.axis_index("lat")
        z, x, yh = lax.div(lon, nx * nyh), lax.rem(lax.div(lon, nyh), nx), lax.rem(lon, nyh)
        yl, core = lax.div(lat, ncore), lax.rem(lat, ncore)
        b_me = z * ny + yh * nyl + yl
        a_me = x * ncore + core

        def b_peer(b):
            bz, by = lax.div(b, ny), lax.rem(b, ny)
            return (bz * (nx * nyh) + x * nyh + lax.div(by, nyl), lax.rem(by, nyl) * ncore + core)

        def a_peer(a):
            return (z * (nx * nyh) + lax.div(a, ncore) * nyh + yh, yl * ncore + lax.rem(a, ncore))

        right, left = lax.rem(lon + 1, nlon), lax.rem(lon + nlon - 1, nlon)
        down, up = lax.rem(lat + 1, nlat), lax.rem(lat + nlat - 1, nlat)

        def load(which, t):
            src, dst = ((x_hbm, xv), (c_hbm, cv), (f_hbm, fv))[which]
            return pltpu.make_async_copy(src.at[:, pl.ds(8 * t, 8), :], dst.at[t], in_sem.at[which, t])

        consts = ((mf_hbm, mf), (mg_hbm, mg), (mk_hbm, mk), (ker_hbm, ker), (md_hbm, md), (mi_hbm, mi))

        def load_const(i):
            return pltpu.make_async_copy(*consts[i], const_sem.at[i])

        for t in (0, TC - 1, *range(1, TC - 1)):
            load(0, t).start()
            load(1, t).start()
        for i in range(len(consts)):
            load_const(i).start()
        for t in range(TC):
            load(2, t).start()

        barrier = pltpu.get_barrier_semaphore()
        for peer in ((right, lat), (left, lat), (lon, down), (lon, up)):
            pl.semaphore_signal(barrier, inc=1, device_id=peer, device_id_type=MESH)

        def greet_b(d, carry):
            pl.semaphore_signal(barrier, inc=1, device_id=b_peer(lax.rem(b_me + d, nb)), device_id_type=MESH)
            return carry

        def greet_a(d, carry):
            pl.semaphore_signal(barrier, inc=1, device_id=a_peer(lax.rem(a_me + d, na)), device_id_type=MESH)
            return carry

        lax.fori_loop(1, nb, greet_b, 0)
        lax.fori_loop(1, na, greet_a, 0)

        third = jnp.full((CH, CH), 1.0 / CH, bf16)
        none = jnp.zeros((CH, CH), bf16)
        mean_two = jnp.concatenate(
            [jnp.concatenate([third, none], 1), jnp.concatenate([none, third], 1)], 0
        )
        gain, bias, scale = gain_ref[...], bias_ref[...], ls_ref[...]
        gw[...] = jnp.zeros_like(gw)
        gbin[...] = jnp.zeros_like(gbin)
        small[...] = jnp.zeros_like(small)
        acc[...] = jnp.zeros_like(acc)
        kpad[...] = jnp.zeros_like(kpad)

        def mlp(parts):
            def cells_of(ref):
                return jnp.concatenate(
                    [ref[t, pl.ds(r0, n)].astype(f32).reshape(n * 8, CH) for t, r0, n in parts], 0
                )

            value = cells_of(xv)
            center = value - dot(value.astype(bf16), third)
            rstd = lax.rsqrt(dot((center * center).astype(bf16), third) + EPS)
            normed = center * rstd
            zed = (normed * gain + bias).astype(bf16)
            cot = cells_of(cv)
            cb = cot.astype(bf16)
            d_out = (cot * scale).astype(bf16)
            acts, dpres = [], []
            g_bin = jnp.zeros((8, HID), f32)
            sub = value.shape[0] // 2
            for s in range(0, value.shape[0], sub):
                h = dot(zed[s : s + sub], win_ref[...]) + bin_ref[...]
                d_act = dot_last(d_out[s : s + sub], wout_ref[...])
                h2 = h * h
                inner = h * (ROOT + (ROOT * COEF) * h2)
                wide = h * (2 * ROOT + (6 * ROOT * COEF) * h2)
                gate = 0.5 * jnp.tanh(inner) + 0.5
                d_pre = d_act * (gate * (1.0 + (1.0 - gate) * wide))
                g_bin = g_bin + rows8(d_pre)
                acts.append((h * gate).astype(bf16))
                dpres.append(d_pre.astype(bf16))
            act, d_pre = jnp.concatenate(acts, 0), jnp.concatenate(dpres, 0)
            gbin[...] += g_bin
            gw[CH:, :] += dot_rows(cb, act)
            gw[:CH, :] += dot_rows(zed, d_pre)
            d_zed = dot_last(d_pre, win_ref[...])
            d_gain = d_zed * normed
            d_norm = d_zed * gain
            means = dot(
                jnp.concatenate([d_norm.astype(bf16), (d_gain * gain).astype(bf16)], 1), mean_two
            )
            du = rstd * (d_norm - means[:, :CH] - normed * means[:, CH:])
            at = 0
            for t, r0, n in parts:
                dup[pl.ds(3 + r0, n), 4 + 8 * t : 12 + 8 * t, :] = du[at : at + 8 * n].reshape(n, 8, CH)
                at += 8 * n
            small[0] += rows8(d_gain)
            small[1] += rows8(d_zed)
            small[2] += rows8(du)
            small[3] += rows8(cot)

        for t in (0, TC - 1):
            load(0, t).wait()
            load(1, t).wait()
        mlp(RIM)

        half = LAT_ROWS // 2
        low = lax.broadcasted_iota(jnp.int32, (half, 8, CH), 1) < 4

        def copy_h(side):
            return pltpu.make_async_remote_copy(
                src_ref=hs.at[side], dst_ref=hr.at[side], send_sem=h_send.at[side], recv_sem=h_recv.at[side],
                device_id=((right, lat), (left, lat))[side], device_id_type=MESH,
            )

        def copy_v(side):
            return pltpu.make_async_remote_copy(
                src_ref=vs.at[side], dst_ref=vr.at[side], send_sem=v_send.at[side], recv_sem=v_recv.at[side],
                device_id=((lon, down), (lon, up))[side], device_id_type=MESH,
            )

        pl.semaphore_wait(barrier, 4 + (nb - 1) + (na - 1))
        first, second = dup[3 : 3 + half, 56:64, :], dup[3 + half : 3 + LAT_ROWS, 56:64, :]
        hs[0] = jnp.where(low, first, pltpu.roll(second, 4, 1)).reshape(half * 8, CH).astype(bf16)
        copy_h(0).start()
        first, second = dup[3 : 3 + half, 0:8, :], dup[3 + half : 3 + LAT_ROWS, 0:8, :]
        hs[1] = jnp.where(low, pltpu.roll(second, 4, 1), first).reshape(half * 8, CH).astype(bf16)
        copy_h(1).start()

        for t in range(1, TC - 1):
            load(0, t).wait()
            load(1, t).wait()

        def mlp_middle(i, carry):
            mlp([(t, i * half, half) for t in range(1, TC - 1)])
            return carry

        lax.fori_loop(0, 2, mlp_middle, 0)

        def copy_w1(b_to, b_from):
            return pltpu.make_async_remote_copy(
                src_ref=ws.at[b_to], dst_ref=wr.at[b_from], send_sem=w1_send.at[b_to], recv_sem=w1_recv.at[b_from],
                device_id=b_peer(b_to), device_id_type=MESH,
            )

        def copy_w2(a_to, a_from):
            return pltpu.make_async_remote_copy(
                src_ref=w2.at[a_me], dst_ref=w2.at[a_from], send_sem=w2_send.at[a_to], recv_sem=w2_recv.at[a_from],
                device_id=a_peer(a_to), device_id_type=MESH,
            )

        def copy_w3(b_to, b_from):
            return pltpu.make_async_remote_copy(
                src_ref=wf.at[b_me], dst_ref=wf.at[b_from], send_sem=w3_send.at[b_to], recv_sem=w3_recv.at[b_from],
                device_id=b_peer(b_to), device_id_type=MESH,
            )

        def copy_s1(a_to, a_from):
            return pltpu.make_async_remote_copy(
                src_ref=s0.at[a_to], dst_ref=s1.at[a_from], send_sem=s1_send.at[a_to], recv_sem=s1_recv.at[a_from],
                device_id=a_peer(a_to), device_id_type=MESH,
            )

        def copy_s2(b_to, b_from):
            return pltpu.make_async_remote_copy(
                src_ref=s2.at[b_me], dst_ref=s2.at[b_from], send_sem=s2_send.at[b_to], recv_sem=s2_recv.at[b_from],
                device_id=b_peer(b_to), device_id_type=MESH,
            )

        def copy_s3(a_to, a_from):
            return pltpu.make_async_remote_copy(
                src_ref=s3.at[a_me], dst_ref=s3.at[a_from], send_sem=s3_send.at[a_to], recv_sem=s3_recv.at[a_from],
                device_id=a_peer(a_to), device_id_type=MESH,
            )

        def over(copy, act, me, size):
            def body(d, carry):
                peer = lax.rem(me + d, size)
                if act == "send":
                    copy(peer, me).start()
                elif act == "recv":
                    copy(peer, peer).wait_recv()
                else:
                    copy(peer, me).wait_send()
                return carry

            lax.fori_loop(1, size, body, 0)

        def over_a(copy, act):
            over(copy, act, a_me, na)

        def over_b(copy, act):
            over(copy, act, b_me, nb)

        ws[...] = gw[...].astype(bf16).reshape(nb, wrows, HID)
        over_b(copy_w1, "send")

        copy_h(0).wait_recv()
        copy_h(1).wait_recv()
        near = hr[0].astype(f32).reshape(half, 8, CH)
        dup[3 : 3 + half, 0:8, :] = jnp.where(low, near, dup[3 : 3 + half, 0:8, :])
        dup[3 + half : 3 + LAT_ROWS, 0:8, :] = jnp.where(
            low, pltpu.roll(near, 4, 1), dup[3 + half : 3 + LAT_ROWS, 0:8, :]
        )
        near = hr[1].astype(f32).reshape(half, 8, CH)
        dup[3 : 3 + half, 56:64, :] = jnp.where(low, dup[3 : 3 + half, 56:64, :], near)
        dup[3 + half : 3 + LAT_ROWS, 56:64, :] = jnp.where(
            low, dup[3 + half : 3 + LAT_ROWS, 56:64, :], pltpu.roll(near, 4, 1)
        )
        vs[0] = dup[LAT_ROWS : LAT_ROWS + 3].reshape(192, CH).astype(bf16)
        vs[1] = dup[3:6].reshape(192, CH).astype(bf16)
        copy_v(0).start()
        copy_v(1).start()

        for i in range(len(consts)):
            load_const(i).wait()
        for t in range(TC):
            load(2, t).wait()
        kpad[0:TAPS] = ker[...]
        kh[...] = dot_exact(mk[...], kpad[...])

        def tile_pair(slot, i0, i1, t):
            def window(i):
                return dup[pl.ds(i * OUT, N), 8 * t : 8 * t + 16, :].reshape(N * 16, CH).astype(bf16)

            def field(i):
                tile = fv[t, pl.ds(i * OUT, OUT)].astype(f32)
                tile = [tile[r] * cos_ref[lat * LAT_ROWS + i * OUT + r] for r in range(OUT)]
                return jnp.concatenate(tile, 0).astype(bf16)

            shape = (PAIRS // 8, 2, 8, 2 * CH)
            w = dot(mf[...], jnp.concatenate([window(i0), window(i1)], 1)).reshape(shape)
            g = dot(mg[...], jnp.concatenate([field(i0), field(i1)], 1)).reshape(shape)
            k = kh[...].reshape(PAIRS // 8, 2, 8, CH)
            k = jnp.concatenate([k, k], -1)
            w_re, w_im, g_re, g_im, k_re, k_im = w[:, 0], w[:, 1], g[:, 0], g[:, 1], k[:, 0], k[:, 1]
            y = jnp.stack([k_re * w_re - k_im * w_im, k_re * w_im + k_im * w_re], 1)
            yb[slot] = y.reshape(FREQ, 2 * CH).astype(bf16)
            d = jnp.stack([g_re * w_re + g_im * w_im, g_im * w_re - g_re * w_im], 1).reshape(FREQ, 2 * CH)
            acc[...] += d[:, :CH] + d[:, CH:]

        pairs = TL // 2

        def middle(j, carry):
            for t in range(1, TC - 1):
                tile_pair(t * pairs + j, 1 + 2 * j, 2 + 2 * j, t)
            return carry

        def sides(j, carry):
            for t in (0, TC - 1):
                tile_pair(t * pairs + j, 1 + 2 * j, 2 + 2 * j, t)
            return carry

        lax.fori_loop(0, pairs - 1, middle, 0)
        lax.fori_loop(0, pairs - 1, sides, 0)

        wr[b_me] = ws[b_me]
        over_b(copy_w1, "recv")
        w2[a_me] = jnp.sum(wr[...].astype(f32), 0).astype(bf16)
        over_a(copy_w2, "send")

        copy_v(0).wait_recv()
        copy_v(1).wait_recv()
        zero = jnp.zeros((3, 64, CH), f32)
        dup[0:3] = jnp.where(lat > 0, vr[0].astype(f32).reshape(3, 64, CH), zero)
        dup[LAT_ROWS + 3 : LAT_ROWS + 6] = jnp.where(lat < nlat - 1, vr[1].astype(f32).reshape(3, 64, CH), zero)
        for t in range(TC):
            tile_pair(t * pairs + pairs - 1, 0, TL - 1, t)

        sm32[...] = jnp.zeros_like(sm32)
        sm32[0:56] = dot_exact(md[...], acc[...])
        total = jnp.sum(gbin[...], 0, keepdims=True)
        for q in range(4):
            sm32[49 + q : 50 + q] = total[:, q * CH : (q + 1) * CH]
            sm32[53 + q : 54 + q] = jnp.sum(small[q], 0, keepdims=True)
        s0[...] = sm32[...].reshape(na, srows, CH)
        over_a(copy_s1, "send")

        def store(t):
            return pltpu.make_async_copy(outv.at[t], out_hbm.at[:, pl.ds(8 * t, 8), :], out_sem.at[t])

        def finish(t, carry):
            for j in range(pairs):
                conv = dot(mi[...], yb[t * pairs + j]).reshape(OUT, OUT, 2 * CH)
                ends = (0, TL - 1) if j == pairs - 1 else (1 + 2 * j, 2 + 2 * j)
                for n, i in enumerate(ends):
                    cot = cv[t, i * OUT : (i + 1) * OUT].astype(f32)
                    part = conv[:, :, n * CH : (n + 1) * CH]
                    value = [cot[r] + part[r] * cos_ref[lat * LAT_ROWS + i * OUT + r] for r in range(OUT)]
                    outv[t, i * OUT : (i + 1) * OUT] = jnp.stack(value, 0).astype(bf16)
            store(t).start()
            return carry

        lax.fori_loop(0, 4, finish, 0)
        s1[a_me] = s0[a_me]
        over_a(copy_s1, "recv")
        s2[b_me] = jnp.sum(s1[...], 0)
        over_b(copy_s2, "send")
        over_a(copy_w2, "recv")
        wf[b_me] = jnp.sum(w2[...].astype(f32), 0).astype(bf16)
        over_b(copy_w3, "send")
        lax.fori_loop(4, TC, finish, 0)
        over_b(copy_s2, "recv")
        s3[a_me] = jnp.sum(s2[...], 0)
        over_a(copy_s3, "send")

        over_b(copy_w3, "recv")
        d_win = jnp.concatenate([wf[b].astype(f32) for b in range(nb // 2)], 0) * factor
        dwin_ref[...] = d_win
        g_out = jnp.concatenate([wf[b].astype(f32) for b in range(nb // 2, nb)], 0) * factor
        g_out = g_out.T
        d_wout = g_out * scale
        dwout_ref[...] = d_wout
        over_a(copy_s3, "recv")
        sm32[...] = s3[...].reshape(SMALL, CH) * factor
        dk = sm32[0:TAPS]
        d_bin = jnp.concatenate([sm32[49 + q : 50 + q] for q in range(4)], 1)
        d_gain, d_bias, d_cb, s_cot = (sm32[53 + q : 54 + q] for q in range(4))
        d_bout = s_cot * scale
        d_ls = jnp.sum(g_out * wout_ref[...].astype(f32), 0, keepdims=True) + bout_ref[...] * s_cot
        dk_ref[...] = dk
        dbin_ref[...] = d_bin
        dgain_ref[...] = d_gain
        dbias_ref[...] = d_bias
        dcb_ref[...] = d_cb
        dbout_ref[...] = d_bout
        dls_ref[...] = d_ls
        squares = jnp.sum(d_win * d_win, 0, keepdims=True) + d_bin * d_bin
        squares = sum(squares[:, q * CH : (q + 1) * CH] for q in range(4))
        squares = squares + jnp.sum(d_wout * d_wout, 0, keepdims=True) + jnp.sum(dk * dk, 0, keepdims=True)
        for part in (d_gain, d_bias, d_cb, d_bout, d_ls):
            squares = squares + part * part
        norm_ref[...] = jnp.sqrt(jnp.sum(squares, 1, keepdims=True))

        for side in range(2):
            copy_h(side).wait_send()
            copy_v(side).wait_send()
        over_b(copy_w1, "done")
        over_a(copy_w2, "done")
        over_b(copy_w3, "done")
        over_a(copy_s1, "done")
        over_b(copy_s2, "done")
        over_a(copy_s3, "done")
        for t in range(TC):
            store(t).wait()

    hbm, vmem, smem = (pl.BlockSpec(memory_space=m) for m in (pl.ANY, pltpu.VMEM, pltpu.SMEM))
    shape = jax.ShapeDtypeStruct
    dma = pltpu.SemaphoreType.DMA
    by_tile = (TC, LAT_ROWS, 8, CH)
    return pl.pallas_call(
        kernel,
        in_specs=[hbm] * 4 + [vmem] * 7 + [smem] + [hbm] * 5,
        out_specs=[hbm] + [vmem] * 10,
        out_shape=RESULTS,
        scratch_shapes=[
            pltpu.VMEM(by_tile, bf16),
            pltpu.VMEM(by_tile, bf16),
            pltpu.VMEM(by_tile, bf16),
            pltpu.VMEM(by_tile, bf16),
            pltpu.VMEM((LAT_ROWS + 6, COLS + 8, CH), f32),
            pltpu.VMEM((TL * TC // 2, FREQ, 2 * CH), bf16),
            pltpu.VMEM((FREQ, N * 16), bf16),
            pltpu.VMEM((FREQ, OUT * OUT), bf16),
            pltpu.VMEM((OUT * OUT, FREQ), bf16),
            pltpu.VMEM((FREQ, 56), f32),
            pltpu.VMEM((56, FREQ), f32),
            pltpu.VMEM((TAPS, CH), f32),
            pltpu.VMEM((56, CH), f32),
            pltpu.VMEM((FREQ, CH), f32),
            pltpu.VMEM((FREQ, CH), f32),
            pltpu.VMEM((2 * CH, HID), f32),
            pltpu.VMEM((8, HID), f32),
            pltpu.VMEM((4, 8, CH), f32),
            pltpu.VMEM((SMALL, CH), f32),
            pltpu.VMEM((2, LAT_ROWS * 4, CH), bf16),
            pltpu.VMEM((2, LAT_ROWS * 4, CH), bf16),
            pltpu.VMEM((2, 192, CH), bf16),
            pltpu.VMEM((2, 192, CH), bf16),
            pltpu.VMEM((nb, wrows, HID), bf16),
            pltpu.VMEM((nb, wrows, HID), bf16),
            pltpu.VMEM((na, wrows, HID), bf16),
            pltpu.VMEM((nb, wrows, HID), bf16),
            pltpu.VMEM((na, srows, CH), f32),
            pltpu.VMEM((na, srows, CH), f32),
            pltpu.VMEM((nb, srows, CH), f32),
            pltpu.VMEM((na, srows, CH), f32),
            dma((3, TC)),
            dma((6,)),
            dma((TC,)),
            dma((2,)),
            dma((2,)),
            dma((2,)),
            dma((2,)),
        ]
        + [dma((n,)) for n in (nb, nb, na, na, nb, nb, na, na, nb, nb, na, na)],
        compiler_params=pltpu.CompilerParams(
            collective_id=0, has_side_effects=True, vmem_limit_bytes=60 * 2**20
        ),
        cost_estimate=pl.CostEstimate(flops=6 * 10**9, bytes_accessed=6 * 10**6, transcendentals=3 * 10**6),
        name="block_backward",
    )


RESULTS = [
    jax.ShapeDtypeStruct(s, t)
    for s, t in (
        ((LAT_ROWS, COLS, CH), bf16),
        ((TAPS, CH), f32),
        ((1, CH), f32),
        ((1, CH), f32),
        ((1, CH), f32),
        ((CH, HID), f32),
        ((1, HID), f32),
        ((HID, CH), f32),
        ((1, CH), f32),
        ((1, CH), f32),
        ((1, 1), f32),
    )
]
BANDS = 6


def hand_on(*refs):
    n = len(RESULTS)
    src, dst, sem = refs[:n], refs[n : 2 * n], refs[2 * n]
    rows = LAT_ROWS // BANDS
    copies = [
        pltpu.make_async_copy(src[0].at[pl.ds(i * rows, rows)], dst[0].at[pl.ds(i * rows, rows)], sem.at[n + i])
        for i in range(BANDS)
    ]
    copies += [pltpu.make_async_copy(src[i], dst[i], sem.at[i]) for i in range(1, n)]
    for copy in copies:
        copy.start()
    for copy in copies:
        copy.wait()


def make_hand_on():
    n = len(RESULTS)
    hbm = pl.BlockSpec(memory_space=pl.ANY)
    return pl.pallas_call(
        hand_on,
        in_specs=[hbm] * n,
        out_specs=[hbm] * n,
        out_shape=RESULTS,
        scratch_shapes=[pltpu.SemaphoreType.DMA((n + BANDS,))],
        name="hand_on",
    )


def solution(mesh):
    nlon, nlat = mesh.shape["lon"], mesh.shape["lat"]
    nz, nx, nyh = (4, 4, 2) if nlon == 32 else (nlon, 1, 1)
    nyl, ncore = nlat // 2, 2
    total_rows, total_cols = LAT_ROWS * nlat, COLS * nlon
    call = make_kernel(nz, nx, nyh, nyl, ncore, total_rows * total_cols)
    finish = make_hand_on()
    fwd, fwd_tile, inv, taps, taps_inv = tables()
    place = (np.arange(total_rows, dtype=np.float32) + np.float32(0.5)) / np.float32(total_rows) - np.float32(0.5)
    weight = np.cos(np.float32(math.pi) * place).astype(np.float32)

    def on_device(field_in, conv_out, cotangent, kernel, ln_gain, ln_bias, w_in, b_in, w_out, b_out, layer_scale):
        line = lambda v: v.reshape(1, -1)
        outs = call(
            conv_out, cotangent, field_in, kernel, line(ln_gain), line(ln_bias), w_in, line(b_in),
            w_out, line(b_out), line(layer_scale), weight, fwd, fwd_tile, inv, taps, taps_inv,
        )
        d_field, d_kernel, d_cb, d_gain, d_bias, d_win, d_bin, d_wout, d_bout, d_ls, norm = finish(*outs)
        wide = lambda v: v.reshape(-1)
        return (
            d_field, d_kernel, wide(d_cb), wide(d_gain), wide(d_bias), d_win, wide(d_bin),
            d_wout, wide(d_bout), wide(d_ls), norm.reshape(()),
        )

    grid = P("lat", "lon", None)
    return jax.shard_map(
        on_device,
        mesh=mesh,
        in_specs=(grid, grid, grid) + (P(),) * 8,
        out_specs=(grid,) + (P(),) * 10,
        check_vma=False,
    )
```

```python
import math

import jax
import jax.numpy as jnp
import ml_dtypes
import numpy as np
from jax import lax
from jax.experimental import pallas as pl
from jax.experimental.pallas import tpu as pltpu
from jax.sharding import PartitionSpec as P

MESH = pl.DeviceIdType.MESH
f32, bf16 = jnp.float32, jnp.bfloat16
EPS = 1e-06
COEF = 0.044715
ROOT = math.sqrt(2.0 / math.pi)

N = 14
OUT = 8
PAIRS = 104
FREQ = 2 * PAIRS
SCALE = 1.828125
LAT_ROWS, COLS, CH, HID, TAPS = 96, 56, 128, 512, 49
TL, TC = LAT_ROWS // OUT, COLS // OUT
SMALL = 64
RIM = ((0, 0, LAT_ROWS), (TC - 1, 0, LAT_ROWS))


def tables():
    own = [(0, 0), (0, 7), (7, 0), (7, 7)]
    seen, pairs = set(own), []
    for k in range(N):
        for l in range(N):
            if (k, l) not in seen:
                seen.add((k, l))
                seen.add(((-k) % N, (-l) % N))
                pairs.append((k, l))
    freq = np.array(own + pairs)
    weight = np.array([1.0] * 4 + [2.0] * 96)[:, None] / (N * N)
    twin = np.array([0.0] * 4 + [1.0] * 96)[:, None]

    def angle(rows, cols, row_off, col_off):
        m, n = np.meshgrid(np.arange(rows) + row_off, np.arange(cols) + col_off, indexing="ij")
        m, n = m.ravel(), n.ravel()
        return 2 * np.pi * ((np.outer(freq[:, 0], m) + np.outer(freq[:, 1], n)) % N) / N

    def interleave(re, im):
        fill = np.zeros((PAIRS - 100, re.shape[1]))
        re, im = np.concatenate([re, fill]), np.concatenate([im, fill])
        shape = (PAIRS // 8, 8, re.shape[1])
        return np.stack([re.reshape(shape), im.reshape(shape)], 1).reshape(FREQ, -1)

    inside = np.tile(np.array([0.0] + [1.0] * 14 + [0.0]), N)
    a = angle(N, 16, 0, -1)
    fwd = interleave(np.cos(a) * inside, -np.sin(a) * inside * twin)
    a = angle(OUT, OUT, 6, 6)
    fwd_tile = interleave(np.cos(a), -np.sin(a) * twin)
    inv = interleave(np.cos(a) * weight, -np.sin(a) * weight * twin).T
    a = angle(7, 7, 0, 0)
    taps = interleave(np.cos(a), -np.sin(a) * twin)
    taps_inv = interleave(np.cos(a) * weight, -np.sin(a) * weight * twin).T
    area = N * N
    return (
        (fwd * SCALE).astype(ml_dtypes.bfloat16),
        (fwd_tile * SCALE).astype(ml_dtypes.bfloat16),
        (inv * area * SCALE).astype(ml_dtypes.bfloat16),
        (np.pad(taps, ((0, 0), (0, 7))) / (area * SCALE * SCALE)).astype(np.float32),
        (np.pad(taps_inv, ((0, 7), (0, 0))) / (SCALE * SCALE)).astype(np.float32),
    )


def dot(a, b):
    return jnp.dot(a, b, preferred_element_type=f32)


def dot_exact(a, b):
    return jnp.dot(a, b, preferred_element_type=f32, precision=lax.Precision.HIGHEST)


def dot_last(a, b):
    return lax.dot_general(a, b, (((1,), (1,)), ((), ())), preferred_element_type=f32)


def dot_rows(a, b):
    return lax.dot_general(a, b, (((0,), (0,)), ((), ())), preferred_element_type=f32)


def rows8(v):
    return jnp.sum(v.reshape(v.shape[0] // 8, 8, v.shape[1]), 0)


def make_kernel(nz, nx, nyh, nyl, ncore, total_cells):
    nlon, nlat = nz * nx * nyh, nyl * ncore
    ny = nyh * nyl
    nb, na = nz * ny, nx * ncore
    wrows = 2 * CH // nb
    factor = float(total_cells) ** (-0.5)

    def kernel(
        x_hbm, c_hbm, f_hbm, ker_hbm, gain_ref, bias_ref, win_ref, bin_ref, wout_ref, bout_ref, ls_ref,
        cos_ref, mf_hbm, mg_hbm, mi_hbm, mk_hbm, md_hbm,
        out_hbm, dk_ref, dcb_ref, dgain_ref, dbias_ref, dwin_ref, dbin_ref, dwout_ref, dbout_ref, dls_ref, norm_ref,
        xv, cv, fv, outv, dup, yb, mf, mg, mi, mk, md, ker, kpad, kh, acc, gw, gbin, small, sm32,
        hs, hr, vs, vr, ws, wr, w2, wf, s1, s2,
        in_sem, const_sem, out_sem, h_send, h_recv, v_send, v_recv,
        w1_send, w1_recv, w2_send, w2_recv, w3_send, w3_recv, s1_send, s1_recv, s2_send, s2_recv,
    ):
        lon, lat = lax.axis_index("lon"), lax.axis_index("lat")
        z, x, yh = lax.div(lon, nx * nyh), lax.rem(lax.div(lon, nyh), nx), lax.rem(lon, nyh)
        yl, core = lax.div(lat, ncore), lax.rem(lat, ncore)
        b_me = z * ny + yh * nyl + yl
        a_me = x * ncore + core

        def b_peer(b):
            bz, by = lax.div(b, ny), lax.rem(b, ny)
            return (bz * (nx * nyh) + x * nyh + lax.div(by, nyl), lax.rem(by, nyl) * ncore + core)

        def a_peer(a):
            return (z * (nx * nyh) + lax.div(a, ncore) * nyh + yh, yl * ncore + lax.rem(a, ncore))

        right, left = lax.rem(lon + 1, nlon), lax.rem(lon + nlon - 1, nlon)
        down, up = lax.rem(lat + 1, nlat), lax.rem(lat + nlat - 1, nlat)

        def load(which, t):
            src, dst = ((x_hbm, xv), (c_hbm, cv), (f_hbm, fv))[which]
            return pltpu.make_async_copy(src.at[:, pl.ds(8 * t, 8), :], dst.at[t], in_sem.at[which, t])

        consts = ((mf_hbm, mf), (mg_hbm, mg), (mk_hbm, mk), (ker_hbm, ker), (md_hbm, md), (mi_hbm, mi))

        def load_const(i):
            return pltpu.make_async_copy(*consts[i], const_sem.at[i])

        for t in (0, TC - 1, *range(1, TC - 1)):
            load(0, t).start()
            load(1, t).start()
        for i in range(len(consts)):
            load_const(i).start()
        for t in range(TC):
            load(2, t).start()

        barrier = pltpu.get_barrier_semaphore()
        for peer in ((right, lat), (left, lat), (lon, down), (lon, up)):
            pl.semaphore_signal(barrier, inc=1, device_id=peer, device_id_type=MESH)

        def greet_b(d, carry):
            pl.semaphore_signal(barrier, inc=1, device_id=b_peer(lax.rem(b_me + d, nb)), device_id_type=MESH)
            return carry

        def greet_a(d, carry):
            pl.semaphore_signal(barrier, inc=1, device_id=a_peer(lax.rem(a_me + d, na)), device_id_type=MESH)
            return carry

        lax.fori_loop(1, nb, greet_b, 0)
        lax.fori_loop(1, na, greet_a, 0)

        third = jnp.full((CH, CH), 1.0 / CH, bf16)
        none = jnp.zeros((CH, CH), bf16)
        mean_two = jnp.concatenate(
            [jnp.concatenate([third, none], 1), jnp.concatenate([none, third], 1)], 0
        )
        gain, bias, scale = gain_ref[...], bias_ref[...], ls_ref[...]
        gw[...] = jnp.zeros_like(gw)
        gbin[...] = jnp.zeros_like(gbin)
        small[...] = jnp.zeros_like(small)
        acc[...] = jnp.zeros_like(acc)
        kpad[...] = jnp.zeros_like(kpad)

        def mlp(parts):
            def cells_of(ref):
                return jnp.concatenate(
                    [ref[t, pl.ds(r0, n)].astype(f32).reshape(n * 8, CH) for t, r0, n in parts], 0
                )

            value = cells_of(xv)
            center = value - dot(value.astype(bf16), third)
            rstd = lax.rsqrt(dot((center * center).astype(bf16), third) + EPS)
            normed = center * rstd
            zed = (normed * gain + bias).astype(bf16)
            cot = cells_of(cv)
            cb = cot.astype(bf16)
            d_out = (cot * scale).astype(bf16)
            acts, dpres = [], []
            g_bin = jnp.zeros((8, HID), f32)
            sub = value.shape[0] // 2
            for s in range(0, value.shape[0], sub):
                h = dot(zed[s : s + sub], win_ref[...]) + bin_ref[...]
                d_act = dot_last(d_out[s : s + sub], wout_ref[...])
                h2 = h * h
                inner = h * (ROOT + (ROOT * COEF) * h2)
                wide = h * (2 * ROOT + (6 * ROOT * COEF) * h2)
                gate = 0.5 * jnp.tanh(inner) + 0.5
                d_pre = d_act * (gate * (1.0 + (1.0 - gate) * wide))
                g_bin = g_bin + rows8(d_pre)
                acts.append((h * gate).astype(bf16))
                dpres.append(d_pre.astype(bf16))
            act, d_pre = jnp.concatenate(acts, 0), jnp.concatenate(dpres, 0)
            gbin[...] += g_bin
            gw[CH:, :] += dot_rows(cb, act)
            gw[:CH, :] += dot_rows(zed, d_pre)
            d_zed = dot_last(d_pre, win_ref[...])
            d_gain = d_zed * normed
            d_norm = d_zed * gain
            means = dot(
                jnp.concatenate([d_norm.astype(bf16), (d_gain * gain).astype(bf16)], 1), mean_two
            )
            du = rstd * (d_norm - means[:, :CH] - normed * means[:, CH:])
            at = 0
            for t, r0, n in parts:
                dup[pl.ds(3 + r0, n), 4 + 8 * t : 12 + 8 * t, :] = du[at : at + 8 * n].reshape(n, 8, CH)
                at += 8 * n
            small[0] += rows8(d_gain)
            small[1] += rows8(d_zed)
            small[2] += rows8(du)
            small[3] += rows8(cot)

        for t in (0, TC - 1):
            load(0, t).wait()
            load(1, t).wait()
        mlp(RIM)

        half = LAT_ROWS // 2
        low = lax.broadcasted_iota(jnp.int32, (half, 8, CH), 1) < 4

        def copy_h(side):
            return pltpu.make_async_remote_copy(
                src_ref=hs.at[side], dst_ref=hr.at[side], send_sem=h_send.at[side], recv_sem=h_recv.at[side],
                device_id=((right, lat), (left, lat))[side], device_id_type=MESH,
            )

        def copy_v(side):
            return pltpu.make_async_remote_copy(
                src_ref=vs.at[side], dst_ref=vr.at[side], send_sem=v_send.at[side], recv_sem=v_recv.at[side],
                device_id=((lon, down), (lon, up))[side], device_id_type=MESH,
            )

        pl.semaphore_wait(barrier, 4 + (nb - 1) + (na - 1))
        first, second = dup[3 : 3 + half, 56:64, :], dup[3 + half : 3 + LAT_ROWS, 56:64, :]
        hs[0] = jnp.where(low, first, pltpu.roll(second, 4, 1)).reshape(half * 8, CH).astype(bf16)
        copy_h(0).start()
        first, second = dup[3 : 3 + half, 0:8, :], dup[3 + half : 3 + LAT_ROWS, 0:8, :]
        hs[1] = jnp.where(low, pltpu.roll(second, 4, 1), first).reshape(half * 8, CH).astype(bf16)
        copy_h(1).start()

        for t in range(1, TC - 1):
            load(0, t).wait()
            load(1, t).wait()

        def mlp_middle(i, carry):
            mlp([(t, i * half, half) for t in range(1, TC - 1)])
            return carry

        lax.fori_loop(0, 2, mlp_middle, 0)

        def copy_w1(b_to, b_from):
            return pltpu.make_async_remote_copy(
                src_ref=ws.at[b_to], dst_ref=wr.at[b_from], send_sem=w1_send.at[b_to], recv_sem=w1_recv.at[b_from],
                device_id=b_peer(b_to), device_id_type=MESH,
            )

        def copy_w2(a_to, a_from):
            return pltpu.make_async_remote_copy(
                src_ref=w2.at[a_me], dst_ref=w2.at[a_from], send_sem=w2_send.at[a_to], recv_sem=w2_recv.at[a_from],
                device_id=a_peer(a_to), device_id_type=MESH,
            )

        def copy_w3(b_to, b_from):
            return pltpu.make_async_remote_copy(
                src_ref=wf.at[b_me], dst_ref=wf.at[b_from], send_sem=w3_send.at[b_to], recv_sem=w3_recv.at[b_from],
                device_id=b_peer(b_to), device_id_type=MESH,
            )

        def copy_s1(a_to, a_from):
            return pltpu.make_async_remote_copy(
                src_ref=s1.at[a_me], dst_ref=s1.at[a_from], send_sem=s1_send.at[a_to], recv_sem=s1_recv.at[a_from],
                device_id=a_peer(a_to), device_id_type=MESH,
            )

        def copy_s2(b_to, b_from):
            return pltpu.make_async_remote_copy(
                src_ref=s2.at[b_me], dst_ref=s2.at[b_from], send_sem=s2_send.at[b_to], recv_sem=s2_recv.at[b_from],
                device_id=b_peer(b_to), device_id_type=MESH,
            )

        def over(copy, act, me, size):
            def body(d, carry):
                peer = lax.rem(me + d, size)
                if act == "send":
                    copy(peer, me).start()
                elif act == "recv":
                    copy(peer, peer).wait_recv()
                else:
                    copy(peer, me).wait_send()
                return carry

            lax.fori_loop(1, size, body, 0)

        def over_a(copy, act):
            over(copy, act, a_me, na)

        def over_b(copy, act):
            over(copy, act, b_me, nb)

        ws[...] = gw[...].astype(bf16).reshape(nb, wrows, HID)
        over_b(copy_w1, "send")

        copy_h(0).wait_recv()
        copy_h(1).wait_recv()
        near = hr[0].astype(f32).reshape(half, 8, CH)
        dup[3 : 3 + half, 0:8, :] = jnp.where(low, near, dup[3 : 3 + half, 0:8, :])
        dup[3 + half : 3 + LAT_ROWS, 0:8, :] = jnp.where(
            low, pltpu.roll(near, 4, 1), dup[3 + half : 3 + LAT_ROWS, 0:8, :]
        )
        near = hr[1].astype(f32).reshape(half, 8, CH)
        dup[3 : 3 + half, 56:64, :] = jnp.where(low, dup[3 : 3 + half, 56:64, :], near)
        dup[3 + half : 3 + LAT_ROWS, 56:64, :] = jnp.where(
            low, dup[3 + half : 3 + LAT_ROWS, 56:64, :], pltpu.roll(near, 4, 1)
        )
        vs[0] = dup[LAT_ROWS : LAT_ROWS + 3].reshape(192, CH).astype(bf16)
        vs[1] = dup[3:6].reshape(192, CH).astype(bf16)
        copy_v(0).start()
        copy_v(1).start()

        for i in range(len(consts)):
            load_const(i).wait()
        for t in range(TC):
            load(2, t).wait()
        kpad[0:TAPS] = ker[...]
        kh[...] = dot_exact(mk[...], kpad[...])

        def tile_pair(slot, i0, i1, t):
            def window(i):
                return dup[pl.ds(i * OUT, N), 8 * t : 8 * t + 16, :].reshape(N * 16, CH).astype(bf16)

            def field(i):
                tile = fv[t, pl.ds(i * OUT, OUT)].astype(f32)
                tile = [tile[r] * cos_ref[lat * LAT_ROWS + i * OUT + r] for r in range(OUT)]
                return jnp.concatenate(tile, 0).astype(bf16)

            shape = (PAIRS // 8, 2, 8, 2 * CH)
            w = dot(mf[...], jnp.concatenate([window(i0), window(i1)], 1)).reshape(shape)
            g = dot(mg[...], jnp.concatenate([field(i0), field(i1)], 1)).reshape(shape)
            k = kh[...].reshape(PAIRS // 8, 2, 8, CH)
            k = jnp.concatenate([k, k], -1)
            w_re, w_im, g_re, g_im, k_re, k_im = w[:, 0], w[:, 1], g[:, 0], g[:, 1], k[:, 0], k[:, 1]
            y = jnp.stack([k_re * w_re - k_im * w_im, k_re * w_im + k_im * w_re], 1)
            yb[slot] = y.reshape(FREQ, 2 * CH).astype(bf16)
            d = jnp.stack([g_re * w_re + g_im * w_im, g_im * w_re - g_re * w_im], 1).reshape(FREQ, 2 * CH)
            acc[...] += d[:, :CH] + d[:, CH:]

        pairs = TL // 2

        def middle(j, carry):
            for t in range(1, TC - 1):
                tile_pair(t * pairs + j, 1 + 2 * j, 2 + 2 * j, t)
            return carry

        def sides(j, carry):
            for t in (0, TC - 1):
                tile_pair(t * pairs + j, 1 + 2 * j, 2 + 2 * j, t)
            return carry

        lax.fori_loop(0, pairs - 1, middle, 0)
        lax.fori_loop(0, pairs - 1, sides, 0)

        copy_v(0).wait_recv()
        copy_v(1).wait_recv()
        zero = jnp.zeros((3, 64, CH), f32)
        dup[0:3] = jnp.where(lat > 0, vr[0].astype(f32).reshape(3, 64, CH), zero)
        dup[LAT_ROWS + 3 : LAT_ROWS + 6] = jnp.where(lat < nlat - 1, vr[1].astype(f32).reshape(3, 64, CH), zero)
        for t in range(TC):
            tile_pair(t * pairs + pairs - 1, 0, TL - 1, t)

        sm32[...] = jnp.zeros_like(sm32)
        sm32[0:56] = dot_exact(md[...], acc[...])
        total = jnp.sum(gbin[...], 0, keepdims=True)
        for q in range(4):
            sm32[49 + q : 50 + q] = total[:, q * CH : (q + 1) * CH]
            sm32[53 + q : 54 + q] = jnp.sum(small[q], 0, keepdims=True)
        s1[a_me] = sm32[...].astype(bf16)
        over_a(copy_s1, "send")

        def store(t):
            return pltpu.make_async_copy(outv.at[t], out_hbm.at[:, pl.ds(8 * t, 8), :], out_sem.at[t])

        def finish(t, carry):
            for j in range(pairs):
                conv = dot(mi[...], yb[t * pairs + j]).reshape(OUT, OUT, 2 * CH)
                ends = (0, TL - 1) if j == pairs - 1 else (1 + 2 * j, 2 + 2 * j)
                for n, i in enumerate(ends):
                    cot = cv[t, i * OUT : (i + 1) * OUT].astype(f32)
                    part = conv[:, :, n * CH : (n + 1) * CH]
                    value = [cot[r] + part[r] * cos_ref[lat * LAT_ROWS + i * OUT + r] for r in range(OUT)]
                    outv[t, i * OUT : (i + 1) * OUT] = jnp.stack(value, 0).astype(bf16)
            store(t).start()
            return carry

        lax.fori_loop(0, 3, finish, 0)
        wr[b_me] = ws[b_me]
        over_b(copy_w1, "recv")
        w2[a_me] = jnp.sum(wr[...].astype(f32), 0).astype(bf16)
        over_a(copy_w2, "send")
        lax.fori_loop(3, TC, finish, 0)
        over_a(copy_s1, "recv")
        s2[b_me] = jnp.sum(s1[...].astype(f32), 0).astype(bf16)
        over_b(copy_s2, "send")
        over_a(copy_w2, "recv")
        wf[b_me] = jnp.sum(w2[...].astype(f32), 0).astype(bf16)
        over_b(copy_w3, "send")

        over_b(copy_s2, "recv")
        sm32[...] = jnp.sum(s2[...].astype(f32), 0) * factor
        dk = sm32[0:TAPS]
        d_bin = jnp.concatenate([sm32[49 + q : 50 + q] for q in range(4)], 1)
        d_gain, d_bias, d_cb, s_cot = (sm32[53 + q : 54 + q] for q in range(4))
        d_bout = s_cot * scale
        dk_ref[...] = dk
        dbin_ref[...] = d_bin
        dgain_ref[...] = d_gain
        dbias_ref[...] = d_bias
        dcb_ref[...] = d_cb
        dbout_ref[...] = d_bout
        over_b(copy_w3, "recv")
        d_win = jnp.concatenate([wf[b].astype(f32) for b in range(nb // 2)], 0) * factor
        dwin_ref[...] = d_win
        g_out = jnp.concatenate([wf[b].astype(f32) for b in range(nb // 2, nb)], 0) * factor
        g_out = g_out.T
        d_wout = g_out * scale
        dwout_ref[...] = d_wout
        d_ls = jnp.sum(g_out * wout_ref[...].astype(f32), 0, keepdims=True) + bout_ref[...] * s_cot
        dls_ref[...] = d_ls
        squares = jnp.sum(d_win * d_win, 0, keepdims=True) + d_bin * d_bin
        squares = sum(squares[:, q * CH : (q + 1) * CH] for q in range(4))
        squares = squares + jnp.sum(d_wout * d_wout, 0, keepdims=True) + jnp.sum(dk * dk, 0, keepdims=True)
        for part in (d_gain, d_bias, d_cb, d_bout, d_ls):
            squares = squares + part * part
        norm_ref[...] = jnp.sqrt(jnp.sum(squares, 1, keepdims=True))

        for side in range(2):
            copy_h(side).wait_send()
            copy_v(side).wait_send()
        over_b(copy_w1, "done")
        over_a(copy_w2, "done")
        over_b(copy_w3, "done")
        over_a(copy_s1, "done")
        over_b(copy_s2, "done")
        for t in range(TC):
            store(t).wait()

    hbm, vmem, smem = (pl.BlockSpec(memory_space=m) for m in (pl.ANY, pltpu.VMEM, pltpu.SMEM))
    shape = jax.ShapeDtypeStruct
    dma = pltpu.SemaphoreType.DMA
    by_tile = (TC, LAT_ROWS, 8, CH)
    return pl.pallas_call(
        kernel,
        in_specs=[hbm] * 4 + [vmem] * 7 + [smem] + [hbm] * 5,
        out_specs=[hbm] + [vmem] * 10,
        out_shape=RESULTS,
        scratch_shapes=[
            pltpu.VMEM(by_tile, bf16),
            pltpu.VMEM(by_tile, bf16),
            pltpu.VMEM(by_tile, bf16),
            pltpu.VMEM(by_tile, bf16),
            pltpu.VMEM((LAT_ROWS + 6, COLS + 8, CH), f32),
            pltpu.VMEM((TL * TC // 2, FREQ, 2 * CH), bf16),
            pltpu.VMEM((FREQ, N * 16), bf16),
            pltpu.VMEM((FREQ, OUT * OUT), bf16),
            pltpu.VMEM((OUT * OUT, FREQ), bf16),
            pltpu.VMEM((FREQ, 56), f32),
            pltpu.VMEM((56, FREQ), f32),
            pltpu.VMEM((TAPS, CH), f32),
            pltpu.VMEM((56, CH), f32),
            pltpu.VMEM((FREQ, CH), f32),
            pltpu.VMEM((FREQ, CH), f32),
            pltpu.VMEM((2 * CH, HID), f32),
            pltpu.VMEM((8, HID), f32),
            pltpu.VMEM((4, 8, CH), f32),
            pltpu.VMEM((SMALL, CH), f32),
            pltpu.VMEM((2, LAT_ROWS * 4, CH), bf16),
            pltpu.VMEM((2, LAT_ROWS * 4, CH), bf16),
            pltpu.VMEM((2, 192, CH), bf16),
            pltpu.VMEM((2, 192, CH), bf16),
            pltpu.VMEM((nb, wrows, HID), bf16),
            pltpu.VMEM((nb, wrows, HID), bf16),
            pltpu.VMEM((na, wrows, HID), bf16),
            pltpu.VMEM((nb, wrows, HID), bf16),
            pltpu.VMEM((na, SMALL, CH), bf16),
            pltpu.VMEM((nb, SMALL, CH), bf16),
            dma((3, TC)),
            dma((6,)),
            dma((TC,)),
            dma((2,)),
            dma((2,)),
            dma((2,)),
            dma((2,)),
        ]
        + [dma((n,)) for n in (nb, nb, na, na, nb, nb, na, na, nb, nb)],
        compiler_params=pltpu.CompilerParams(
            collective_id=0, has_side_effects=True, vmem_limit_bytes=60 * 2**20
        ),
        cost_estimate=pl.CostEstimate(flops=6 * 10**9, bytes_accessed=6 * 10**6, transcendentals=3 * 10**6),
        name="block_backward",
    )


RESULTS = [
    jax.ShapeDtypeStruct(s, t)
    for s, t in (
        ((LAT_ROWS, COLS, CH), bf16),
        ((TAPS, CH), f32),
        ((1, CH), f32),
        ((1, CH), f32),
        ((1, CH), f32),
        ((CH, HID), f32),
        ((1, HID), f32),
        ((HID, CH), f32),
        ((1, CH), f32),
        ((1, CH), f32),
        ((1, 1), f32),
    )
]
BANDS = 6


def hand_on(*refs):
    n = len(RESULTS)
    src, dst, stage, sem_in, sem_out = refs[:n], refs[n : 2 * n], refs[2 * n : 3 * n], refs[3 * n], refs[3 * n + 1]
    rows = LAT_ROWS // BANDS

    def parts(i):
        return [pl.ds(j * rows, rows) for j in range(BANDS)] if i == 0 else [slice(None)]

    hops = []
    for i in range(n):
        for j, part in enumerate(parts(i)):
            slot = n + j if i == 0 else i
            hops.append((
                pltpu.make_async_copy(src[i].at[part], stage[i].at[part], sem_in.at[slot]),
                pltpu.make_async_copy(stage[i].at[part], dst[i].at[part], sem_out.at[slot]),
            ))
    for first, _ in hops:
        first.start()
    for first, second in hops:
        first.wait()
        second.start()
    for _, second in hops:
        second.wait()


def make_hand_on():
    n = len(RESULTS)
    hbm = pl.BlockSpec(memory_space=pltpu.HBM)
    dma = pltpu.SemaphoreType.DMA((n + BANDS,))
    return pl.pallas_call(
        hand_on,
        in_specs=[hbm] * n,
        out_specs=[hbm] * n,
        out_shape=RESULTS,
        scratch_shapes=[pltpu.VMEM(r.shape, r.dtype) for r in RESULTS] + [dma, dma],
        name="hand_on",
    )


def solution(mesh):
    nlon, nlat = mesh.shape["lon"], mesh.shape["lat"]
    nz, nx, nyh = (4, 4, 2) if nlon == 32 else (nlon, 1, 1)
    nyl, ncore = nlat // 2, 2
    total_rows, total_cols = LAT_ROWS * nlat, COLS * nlon
    call = make_kernel(nz, nx, nyh, nyl, ncore, total_rows * total_cols)
    finish = make_hand_on()
    fwd, fwd_tile, inv, taps, taps_inv = tables()
    place = (np.arange(total_rows, dtype=np.float32) + np.float32(0.5)) / np.float32(total_rows) - np.float32(0.5)
    weight = np.cos(np.float32(math.pi) * place).astype(np.float32)

    def on_device(field_in, conv_out, cotangent, kernel, ln_gain, ln_bias, w_in, b_in, w_out, b_out, layer_scale):
        line = lambda v: v.reshape(1, -1)
        outs = call(
            conv_out, cotangent, field_in, kernel, line(ln_gain), line(ln_bias), w_in, line(b_in),
            w_out, line(b_out), line(layer_scale), weight, fwd, fwd_tile, inv, taps, taps_inv,
        )
        d_field, d_kernel, d_cb, d_gain, d_bias, d_win, d_bin, d_wout, d_bout, d_ls, norm = finish(*outs)
        wide = lambda v: v.reshape(-1)
        return (
            d_field, d_kernel, wide(d_cb), wide(d_gain), wide(d_bias), d_win, wide(d_bin),
            d_wout, wide(d_bout), wide(d_ls), norm.reshape(()),
        )

    grid = P("lat", "lon", None)
    return jax.shard_map(
        on_device,
        mesh=mesh,
        in_specs=(grid, grid, grid) + (P(),) * 8,
        out_specs=(grid,) + (P(),) * 10,
        check_vma=False,
    )
```

```python
import math

import jax
import jax.numpy as jnp
import ml_dtypes
import numpy as np
from jax import lax
from jax.experimental import pallas as pl
from jax.experimental.pallas import tpu as pltpu
from jax.sharding import PartitionSpec as P

MESH = pl.DeviceIdType.MESH
f32, bf16 = jnp.float32, jnp.bfloat16
EPS = 1e-06
COEF = 0.044715
ROOT = math.sqrt(2.0 / math.pi)

N = 14
OUT = 8
PAIRS = 104
FREQ = 2 * PAIRS
SCALE = 1.828125
LAT_ROWS, COLS, CH, HID, TAPS = 96, 56, 128, 512, 49
TL, TC = LAT_ROWS // OUT, COLS // OUT
SMALL = 64
RIM = ((0, 0, LAT_ROWS), (TC - 1, 0, LAT_ROWS))


def tables():
    own = [(0, 0), (0, 7), (7, 0), (7, 7)]
    seen, pairs = set(own), []
    for k in range(N):
        for l in range(N):
            if (k, l) not in seen:
                seen.add((k, l))
                seen.add(((-k) % N, (-l) % N))
                pairs.append((k, l))
    freq = np.array(own + pairs)
    weight = np.array([1.0] * 4 + [2.0] * 96)[:, None] / (N * N)
    twin = np.array([0.0] * 4 + [1.0] * 96)[:, None]

    def angle(rows, cols, row_off, col_off):
        m, n = np.meshgrid(np.arange(rows) + row_off, np.arange(cols) + col_off, indexing="ij")
        m, n = m.ravel(), n.ravel()
        return 2 * np.pi * ((np.outer(freq[:, 0], m) + np.outer(freq[:, 1], n)) % N) / N

    def interleave(re, im):
        fill = np.zeros((PAIRS - 100, re.shape[1]))
        re, im = np.concatenate([re, fill]), np.concatenate([im, fill])
        shape = (PAIRS // 8, 8, re.shape[1])
        return np.stack([re.reshape(shape), im.reshape(shape)], 1).reshape(FREQ, -1)

    inside = np.tile(np.array([0.0] + [1.0] * 14 + [0.0]), N)
    a = angle(N, 16, 0, -1)
    fwd = interleave(np.cos(a) * inside, -np.sin(a) * inside * twin)
    a = angle(OUT, OUT, 6, 6)
    fwd_tile = interleave(np.cos(a), -np.sin(a) * twin)
    inv = interleave(np.cos(a) * weight, -np.sin(a) * weight * twin).T
    a = angle(7, 7, 0, 0)
    taps = interleave(np.cos(a), -np.sin(a) * twin)
    taps_inv = interleave(np.cos(a) * weight, -np.sin(a) * weight * twin).T
    area = N * N
    return (
        (fwd * SCALE).astype(ml_dtypes.bfloat16),
        (fwd_tile * SCALE).astype(ml_dtypes.bfloat16),
        (inv * area * SCALE).astype(ml_dtypes.bfloat16),
        (np.pad(taps, ((0, 0), (0, 7))) / (area * SCALE * SCALE)).astype(np.float32),
        (np.pad(taps_inv, ((0, 7), (0, 0))) / (SCALE * SCALE)).astype(np.float32),
    )


def dot(a, b):
    return jnp.dot(a, b, preferred_element_type=f32)


def dot_exact(a, b):
    return jnp.dot(a, b, preferred_element_type=f32, precision=lax.Precision.HIGHEST)


def dot_last(a, b):
    return lax.dot_general(a, b, (((1,), (1,)), ((), ())), preferred_element_type=f32)


def dot_rows(a, b):
    return lax.dot_general(a, b, (((0,), (0,)), ((), ())), preferred_element_type=f32)


def rows8(v):
    return jnp.sum(v.reshape(v.shape[0] // 8, 8, v.shape[1]), 0)


def make_kernel(nz, nx, nyh, nyl, ncore, total_cells):
    nlon, nlat = nz * nx * nyh, nyl * ncore
    ny = nyh * nyl
    nb, na = nz * ny, nx * ncore
    wrows = 2 * CH // nb
    factor = float(total_cells) ** (-0.5)

    def kernel(
        x_hbm, c_hbm, f_hbm, ker_hbm, gain_hbm, bias_hbm, win_hbm, bin_hbm, wout_hbm, bout_hbm, ls_hbm,
        cos_ref, mf_hbm, mg_hbm, mi_hbm, mk_hbm, md_hbm,
        out_hbm, dk_hbm, dcb_hbm, dgain_hbm, dbias_hbm, dwin_hbm, dbin_hbm, dwout_hbm, dbout_hbm, dls_hbm, norm_hbm,
        dk_ref, dcb_ref, dgain_ref, dbias_ref, dwin_ref, dbin_ref, dwout_ref, dbout_ref, dls_ref, norm_ref,
        gain_ref, bias_ref, win_ref, bin_ref, wout_ref, bout_ref, ls_ref, dps, norms, rstds,
        xv, cv, fv, outv, dup, yb, mf, mg, mi, mk, md, ker, kpad, kh, acc, gw, gbin, small, sm32,
        hs, hr, vs, vr, ws, wr, w2, wf, s1, s2,
        in_sem, const_sem, res_sem, out_sem, h_send, h_recv, v_send, v_recv,
        w1_send, w1_recv, w2_send, w2_recv, w3_send, w3_recv, s1_send, s1_recv, s2_send, s2_recv,
    ):
        lon, lat = lax.axis_index("lon"), lax.axis_index("lat")
        z, x, yh = lax.div(lon, nx * nyh), lax.rem(lax.div(lon, nyh), nx), lax.rem(lon, nyh)
        yl, core = lax.div(lat, ncore), lax.rem(lat, ncore)
        b_me = z * ny + yh * nyl + yl
        a_me = x * ncore + core

        def b_peer(b):
            bz, by = lax.div(b, ny), lax.rem(b, ny)
            return (bz * (nx * nyh) + x * nyh + lax.div(by, nyl), lax.rem(by, nyl) * ncore + core)

        def a_peer(a):
            return (z * (nx * nyh) + lax.div(a, ncore) * nyh + yh, yl * ncore + lax.rem(a, ncore))

        right, left = lax.rem(lon + 1, nlon), lax.rem(lon + nlon - 1, nlon)
        down, up = lax.rem(lat + 1, nlat), lax.rem(lat + nlat - 1, nlat)

        def load(which, t):
            src, dst = ((x_hbm, xv), (c_hbm, cv), (f_hbm, fv))[which]
            return pltpu.make_async_copy(src.at[:, pl.ds(8 * t, 8), :], dst.at[t], in_sem.at[which, t])

        consts = (
            (gain_hbm, gain_ref), (bias_hbm, bias_ref), (win_hbm, win_ref), (bin_hbm, bin_ref), (wout_hbm, wout_ref),
            (ls_hbm, ls_ref), (bout_hbm, bout_ref),
            (mf_hbm, mf), (mg_hbm, mg), (mk_hbm, mk), (ker_hbm, ker), (md_hbm, md), (mi_hbm, mi),
        )
        results = (
            (dk_ref, dk_hbm), (dcb_ref, dcb_hbm), (dgain_ref, dgain_hbm), (dbias_ref, dbias_hbm), (dbin_ref, dbin_hbm),
            (dbout_ref, dbout_hbm), (dwin_ref, dwin_hbm), (dwout_ref, dwout_hbm), (dls_ref, dls_hbm), (norm_ref, norm_hbm),
        )

        def give(i):
            return pltpu.make_async_copy(*results[i], res_sem.at[i])

        def load_const(i):
            return pltpu.make_async_copy(*consts[i], const_sem.at[i])

        for t in (0, TC - 1):
            load(0, t).start()
            load(1, t).start()
        for i in range(7):
            load_const(i).start()
        for t in range(1, TC - 1):
            load(0, t).start()
            load(1, t).start()
        for i in range(7, len(consts)):
            load_const(i).start()
        for t in range(TC):
            load(2, t).start()

        barrier = pltpu.get_barrier_semaphore()
        for peer in ((right, lat), (left, lat), (lon, down), (lon, up)):
            pl.semaphore_signal(barrier, inc=1, device_id=peer, device_id_type=MESH)

        def greet_b(d, carry):
            pl.semaphore_signal(barrier, inc=1, device_id=b_peer(lax.rem(b_me + d, nb)), device_id_type=MESH)
            return carry

        def greet_a(d, carry):
            pl.semaphore_signal(barrier, inc=1, device_id=a_peer(lax.rem(a_me + d, na)), device_id_type=MESH)
            return carry

        lax.fori_loop(1, nb, greet_b, 0)
        lax.fori_loop(1, na, greet_a, 0)

        third = jnp.full((CH, CH), 1.0 / CH, bf16)
        none = jnp.zeros((CH, CH), bf16)
        mean_two = jnp.concatenate(
            [jnp.concatenate([third, none], 1), jnp.concatenate([none, third], 1)], 0
        )
        gw[...] = jnp.zeros_like(gw)
        gbin[...] = jnp.zeros_like(gbin)
        small[...] = jnp.zeros_like(small)
        acc[...] = jnp.zeros_like(acc)
        kpad[...] = jnp.zeros_like(kpad)

        for i in range(7):
            load_const(i).wait()
        gain, bias, scale = gain_ref[...], bias_ref[...], ls_ref[...]
        win_half, bin_half = win_ref[...] * jnp.asarray(0.5, bf16), bin_ref[...] * 0.5
        wout_half = wout_ref[...] * jnp.asarray(0.5, bf16)

        def cells_of(ref, parts):
            return jnp.concatenate([ref[t, pl.ds(r0, n)].astype(f32).reshape(n * 8, CH) for t, r0, n in parts], 0)

        def mlp_grads(parts):
            value = cells_of(xv, parts)
            center = value - dot(value.astype(bf16), third)
            rstd = lax.rsqrt(dot((center * center).astype(bf16), third) + EPS)
            normed = center * rstd
            zed = (normed * gain + bias).astype(bf16)
            cot = cells_of(cv, parts)
            cb = cot.astype(bf16)
            d_out = (cot * scale).astype(bf16)
            acts, dpres = [], []
            g_bin = jnp.zeros((8, HID), f32)
            sub = value.shape[0] // 2
            for s in range(0, value.shape[0], sub):
                h = dot(zed[s : s + sub], win_half) + bin_half
                d_act = dot_last(d_out[s : s + sub], wout_half)
                h2 = h * h
                tangent = jnp.tanh(h * (2 * ROOT + (8 * ROOT * COEF) * h2))
                wide = h * (2 * ROOT + (24 * ROOT * COEF) * h2)
                above = 1.0 + tangent
                d_pre = d_act * (above * (1.0 + (1.0 - tangent) * wide))
                g_bin = g_bin + rows8(d_pre)
                acts.append((h * above).astype(bf16))
                dpres.append(d_pre.astype(bf16))
            act, d_pre = jnp.concatenate(acts, 0), jnp.concatenate(dpres, 0)
            gbin[...] += g_bin
            gw[CH:, :] += dot_rows(cb, act)
            gw[:CH, :] += dot_rows(zed, d_pre)
            small[3] += rows8(cot)
            return d_pre, normed, rstd

        def mlp_du(parts, d_pre, normed, rstd):
            d_zed = dot_last(d_pre, win_ref[...])
            d_gain = d_zed * normed
            d_norm = d_zed * gain
            means = dot(
                jnp.concatenate([d_norm.astype(bf16), (d_gain * gain).astype(bf16)], 1), mean_two
            )
            du = rstd * (d_norm - means[:, :CH] - normed * means[:, CH:])
            at = 0
            for t, r0, n in parts:
                dup[pl.ds(3 + r0, n), 4 + 8 * t : 12 + 8 * t, :] = du[at : at + 8 * n].reshape(n, 8, CH)
                at += 8 * n
            small[0] += rows8(d_gain)
            small[1] += rows8(d_zed)
            small[2] += rows8(du)

        for t in (0, TC - 1):
            load(0, t).wait()
            load(1, t).wait()
        mlp_du(RIM, *mlp_grads(RIM))

        half = LAT_ROWS // 2
        low = lax.broadcasted_iota(jnp.int32, (half, 8, CH), 1) < 4

        def copy_h(side):
            return pltpu.make_async_remote_copy(
                src_ref=hs.at[side], dst_ref=hr.at[side], send_sem=h_send.at[side], recv_sem=h_recv.at[side],
                device_id=((right, lat), (left, lat))[side], device_id_type=MESH,
            )

        def copy_v(side):
            return pltpu.make_async_remote_copy(
                src_ref=vs.at[side], dst_ref=vr.at[side], send_sem=v_send.at[side], recv_sem=v_recv.at[side],
                device_id=((lon, down), (lon, up))[side], device_id_type=MESH,
            )

        pl.semaphore_wait(barrier, 4 + (nb - 1) + (na - 1))
        first, second = dup[3 : 3 + half, 56:64, :], dup[3 + half : 3 + LAT_ROWS, 56:64, :]
        hs[0] = jnp.where(low, first, pltpu.roll(second, 4, 1)).reshape(half * 8, CH).astype(bf16)
        copy_h(0).start()
        first, second = dup[3 : 3 + half, 0:8, :], dup[3 + half : 3 + LAT_ROWS, 0:8, :]
        hs[1] = jnp.where(low, pltpu.roll(second, 4, 1), first).reshape(half * 8, CH).astype(bf16)
        copy_h(1).start()

        for t in range(1, TC - 1):
            load(0, t).wait()
            load(1, t).wait()

        def middle_parts(i):
            return [(t, i * half, half) for t in range(1, TC - 1)]

        def middle_grads(i, carry):
            dps[i], norms[i], rstds[i] = mlp_grads(middle_parts(i))
            return carry

        def middle_du(i, carry):
            mlp_du(middle_parts(i), dps[i], norms[i], rstds[i])
            return carry

        lax.fori_loop(0, 2, middle_grads, 0)

        def copy_w1(b_to, b_from):
            return pltpu.make_async_remote_copy(
                src_ref=ws.at[b_to], dst_ref=wr.at[b_from], send_sem=w1_send.at[b_to], recv_sem=w1_recv.at[b_from],
                device_id=b_peer(b_to), device_id_type=MESH,
            )

        def copy_w2(a_to, a_from):
            return pltpu.make_async_remote_copy(
                src_ref=w2.at[a_me], dst_ref=w2.at[a_from], send_sem=w2_send.at[a_to], recv_sem=w2_recv.at[a_from],
                device_id=a_peer(a_to), device_id_type=MESH,
            )

        def copy_w3(b_to, b_from):
            return pltpu.make_async_remote_copy(
                src_ref=wf.at[b_me], dst_ref=wf.at[b_from], send_sem=w3_send.at[b_to], recv_sem=w3_recv.at[b_from],
                device_id=b_peer(b_to), device_id_type=MESH,
            )

        def copy_s1(b_to, b_from):
            return pltpu.make_async_remote_copy(
                src_ref=s1.at[b_me], dst_ref=s1.at[b_from], send_sem=s1_send.at[b_to], recv_sem=s1_recv.at[b_from],
                device_id=b_peer(b_to), device_id_type=MESH,
            )

        def copy_s2(a_to, a_from):
            return pltpu.make_async_remote_copy(
                src_ref=s2.at[a_me], dst_ref=s2.at[a_from], send_sem=s2_send.at[a_to], recv_sem=s2_recv.at[a_from],
                device_id=a_peer(a_to), device_id_type=MESH,
            )

        def over(copy, act, me, size):
            def body(d, carry):
                peer = lax.rem(me + d, size)
                if act == "send":
                    copy(peer, me).start()
                elif act == "recv":
                    copy(peer, peer).wait_recv()
                else:
                    copy(peer, me).wait_send()
                return carry

            lax.fori_loop(1, size, body, 0)

        def over_a(copy, act):
            over(copy, act, a_me, na)

        def over_b(copy, act):
            over(copy, act, b_me, nb)

        ws[...] = gw[...].astype(bf16).reshape(nb, wrows, HID)
        over_b(copy_w1, "send")
        lax.fori_loop(0, 2, middle_du, 0)

        copy_h(0).wait_recv()
        copy_h(1).wait_recv()
        near = hr[0].astype(f32).reshape(half, 8, CH)
        dup[3 : 3 + half, 0:8, :] = jnp.where(low, near, dup[3 : 3 + half, 0:8, :])
        dup[3 + half : 3 + LAT_ROWS, 0:8, :] = jnp.where(
            low, pltpu.roll(near, 4, 1), dup[3 + half : 3 + LAT_ROWS, 0:8, :]
        )
        near = hr[1].astype(f32).reshape(half, 8, CH)
        dup[3 : 3 + half, 56:64, :] = jnp.where(low, dup[3 : 3 + half, 56:64, :], near)
        dup[3 + half : 3 + LAT_ROWS, 56:64, :] = jnp.where(
            low, dup[3 + half : 3 + LAT_ROWS, 56:64, :], pltpu.roll(near, 4, 1)
        )
        vs[0] = dup[LAT_ROWS : LAT_ROWS + 3].reshape(192, CH).astype(bf16)
        vs[1] = dup[3:6].reshape(192, CH).astype(bf16)
        copy_v(0).start()
        copy_v(1).start()

        for i in range(7, len(consts)):
            load_const(i).wait()
        for t in range(TC):
            load(2, t).wait()
        kpad[0:TAPS] = ker[...]
        kh[...] = dot_exact(mk[...], kpad[...])

        def tile_pair(slot, i0, i1, t):
            def window(i):
                return dup[pl.ds(i * OUT, N), 8 * t : 8 * t + 16, :].reshape(N * 16, CH).astype(bf16)

            def field(i):
                tile = fv[t, pl.ds(i * OUT, OUT)].astype(f32)
                tile = [tile[r] * cos_ref[lat * LAT_ROWS + i * OUT + r] for r in range(OUT)]
                return jnp.concatenate(tile, 0).astype(bf16)

            shape = (PAIRS // 8, 2, 8, 2 * CH)
            w = dot(mf[...], jnp.concatenate([window(i0), window(i1)], 1)).reshape(shape)
            g = dot(mg[...], jnp.concatenate([field(i0), field(i1)], 1)).reshape(shape)
            k = kh[...].reshape(PAIRS // 8, 2, 8, CH)
            k = jnp.concatenate([k, k], -1)
            w_re, w_im, g_re, g_im, k_re, k_im = w[:, 0], w[:, 1], g[:, 0], g[:, 1], k[:, 0], k[:, 1]
            y = jnp.stack([k_re * w_re - k_im * w_im, k_re * w_im + k_im * w_re], 1)
            yb[slot] = y.reshape(FREQ, 2 * CH).astype(bf16)
            d = jnp.stack([g_re * w_re + g_im * w_im, g_im * w_re - g_re * w_im], 1).reshape(FREQ, 2 * CH)
            acc[...] += d[:, :CH] + d[:, CH:]

        pairs = TL // 2

        def middle(j, carry):
            for t in range(1, TC - 1):
                tile_pair(t * pairs + j, 1 + 2 * j, 2 + 2 * j, t)
            return carry

        def sides(j, carry):
            for t in (0, TC - 1):
                tile_pair(t * pairs + j, 1 + 2 * j, 2 + 2 * j, t)
            return carry

        lax.fori_loop(0, pairs - 1, middle, 0)
        lax.fori_loop(0, pairs - 1, sides, 0)

        wr[b_me] = ws[b_me]
        over_b(copy_w1, "recv")
        w2[a_me] = jnp.sum(wr[...].astype(f32), 0).astype(bf16)
        over_a(copy_w2, "send")

        copy_v(0).wait_recv()
        copy_v(1).wait_recv()
        zero = jnp.zeros((3, 64, CH), f32)
        dup[0:3] = jnp.where(lat > 0, vr[0].astype(f32).reshape(3, 64, CH), zero)
        dup[LAT_ROWS + 3 : LAT_ROWS + 6] = jnp.where(lat < nlat - 1, vr[1].astype(f32).reshape(3, 64, CH), zero)
        for t in range(TC):
            tile_pair(t * pairs + pairs - 1, 0, TL - 1, t)

        sm32[...] = jnp.zeros_like(sm32)
        sm32[0:56] = dot_exact(md[...], acc[...])
        total = jnp.sum(gbin[...], 0, keepdims=True)
        for q in range(4):
            sm32[49 + q : 50 + q] = total[:, q * CH : (q + 1) * CH]
            sm32[53 + q : 54 + q] = jnp.sum(small[q], 0, keepdims=True)
        s1[b_me] = sm32[...].astype(bf16)
        over_b(copy_s1, "send")

        def store(t):
            return pltpu.make_async_copy(outv.at[t], out_hbm.at[:, pl.ds(8 * t, 8), :], out_sem.at[t])

        def finish(t, carry):
            for j in range(pairs):
                conv = dot(mi[...], yb[t * pairs + j]).reshape(OUT, OUT, 2 * CH)
                ends = (0, TL - 1) if j == pairs - 1 else (1 + 2 * j, 2 + 2 * j)
                for n, i in enumerate(ends):
                    cot = cv[t, i * OUT : (i + 1) * OUT].astype(f32)
                    part = conv[:, :, n * CH : (n + 1) * CH]
                    value = [cot[r] + part[r] * cos_ref[lat * LAT_ROWS + i * OUT + r] for r in range(OUT)]
                    outv[t, i * OUT : (i + 1) * OUT] = jnp.stack(value, 0).astype(bf16)
            store(t).start()
            return carry

        lax.fori_loop(0, TC, finish, 0)
        over_a(copy_w2, "recv")
        wf[b_me] = jnp.sum(w2[...].astype(f32), 0).astype(bf16)
        over_b(copy_w3, "send")
        over_b(copy_s1, "recv")
        s2[a_me] = jnp.sum(s1[...].astype(f32), 0).astype(bf16)
        over_a(copy_s2, "send")

        over_b(copy_w3, "recv")
        d_win = jnp.concatenate([wf[b].astype(f32) for b in range(nb // 2)], 0) * factor
        dwin_ref[...] = d_win
        give(6).start()
        g_out = jnp.concatenate([wf[b].astype(f32) for b in range(nb // 2, nb)], 0) * factor
        g_out = g_out.T
        d_wout = g_out * scale
        dwout_ref[...] = d_wout
        give(7).start()
        squares = jnp.sum(d_win * d_win, 0, keepdims=True)
        squares = sum(squares[:, q * CH : (q + 1) * CH] for q in range(4))
        squares = squares + jnp.sum(d_wout * d_wout, 0, keepdims=True)
        g_ls = jnp.sum(g_out * wout_ref[...].astype(f32), 0, keepdims=True)
        over_a(copy_s2, "recv")
        sm32[...] = jnp.sum(s2[...].astype(f32), 0) * factor
        dk = sm32[0:TAPS]
        d_bin = jnp.concatenate([sm32[49 + q : 50 + q] for q in range(4)], 1)
        d_gain, d_bias, d_cb, s_cot = (sm32[53 + q : 54 + q] for q in range(4))
        d_bout = s_cot * scale
        d_ls = g_ls + bout_ref[...] * s_cot
        dk_ref[...] = dk
        dcb_ref[...] = d_cb
        dgain_ref[...] = d_gain
        dbias_ref[...] = d_bias
        dbin_ref[...] = d_bin
        dbout_ref[...] = d_bout
        dls_ref[...] = d_ls
        for i in (0, 1, 2, 3, 4, 5, 8):
            give(i).start()
        squares = squares + jnp.sum(dk * dk, 0, keepdims=True)
        for q in range(4):
            squares = squares + d_bin[:, q * CH : (q + 1) * CH] * d_bin[:, q * CH : (q + 1) * CH]
        for part in (d_gain, d_bias, d_cb, d_bout, d_ls):
            squares = squares + part * part
        norm_ref[...] = jnp.sqrt(jnp.sum(squares, 1, keepdims=True))
        give(9).start()

        for side in range(2):
            copy_h(side).wait_send()
            copy_v(side).wait_send()
        over_b(copy_w1, "done")
        over_a(copy_w2, "done")
        over_b(copy_w3, "done")
        over_b(copy_s1, "done")
        over_a(copy_s2, "done")
        for t in range(TC):
            store(t).wait()
        for i in range(len(results)):
            give(i).wait()

    hbm, smem = pl.BlockSpec(memory_space=pl.ANY), pl.BlockSpec(memory_space=pltpu.SMEM)
    shape = jax.ShapeDtypeStruct
    dma = pltpu.SemaphoreType.DMA
    by_tile = (TC, LAT_ROWS, 8, CH)
    return pl.pallas_call(
        kernel,
        in_specs=[hbm] * 11 + [smem] + [hbm] * 5,
        out_specs=[hbm] * 11,
        out_shape=RESULTS,
        scratch_shapes=[pltpu.VMEM(r.shape, r.dtype) for r in RESULTS[1:]]
        + [
            pltpu.VMEM((1, CH), f32),
            pltpu.VMEM((1, CH), f32),
            pltpu.VMEM((CH, HID), bf16),
            pltpu.VMEM((1, HID), f32),
            pltpu.VMEM((HID, CH), bf16),
            pltpu.VMEM((1, CH), f32),
            pltpu.VMEM((1, CH), f32),
            pltpu.VMEM((2, LAT_ROWS // 2 * (COLS - 16), HID), bf16),
            pltpu.VMEM((2, LAT_ROWS // 2 * (COLS - 16), CH), f32),
            pltpu.VMEM((2, LAT_ROWS // 2 * (COLS - 16), CH), f32),
            pltpu.VMEM(by_tile, bf16),
            pltpu.VMEM(by_tile, bf16),
            pltpu.VMEM(by_tile, bf16),
            pltpu.VMEM(by_tile, bf16),
            pltpu.VMEM((LAT_ROWS + 6, COLS + 8, CH), f32),
            pltpu.VMEM((TL * TC // 2, FREQ, 2 * CH), bf16),
            pltpu.VMEM((FREQ, N * 16), bf16),
            pltpu.VMEM((FREQ, OUT * OUT), bf16),
            pltpu.VMEM((OUT * OUT, FREQ), bf16),
            pltpu.VMEM((FREQ, 56), f32),
            pltpu.VMEM((56, FREQ), f32),
            pltpu.VMEM((TAPS, CH), f32),
            pltpu.VMEM((56, CH), f32),
            pltpu.VMEM((FREQ, CH), f32),
            pltpu.VMEM((FREQ, CH), f32),
            pltpu.VMEM((2 * CH, HID), f32),
            pltpu.VMEM((8, HID), f32),
            pltpu.VMEM((4, 8, CH), f32),
            pltpu.VMEM((SMALL, CH), f32),
            pltpu.VMEM((2, LAT_ROWS * 4, CH), bf16),
            pltpu.VMEM((2, LAT_ROWS * 4, CH), bf16),
            pltpu.VMEM((2, 192, CH), bf16),
            pltpu.VMEM((2, 192, CH), bf16),
            pltpu.VMEM((nb, wrows, HID), bf16),
            pltpu.VMEM((nb, wrows, HID), bf16),
            pltpu.VMEM((na, wrows, HID), bf16),
            pltpu.VMEM((nb, wrows, HID), bf16),
            pltpu.VMEM((nb, SMALL, CH), bf16),
            pltpu.VMEM((na, SMALL, CH), bf16),
            dma((3, TC)),
            dma((13,)),
            dma((len(RESULTS) - 1,)),
            dma((TC,)),
            dma((2,)),
            dma((2,)),
            dma((2,)),
            dma((2,)),
        ]
        + [dma((n,)) for n in (nb, nb, na, na, nb, nb, nb, nb, na, na)],
        compiler_params=pltpu.CompilerParams(
            collective_id=0, has_side_effects=True, vmem_limit_bytes=60 * 2**20
        ),
        cost_estimate=pl.CostEstimate(flops=6 * 10**9, bytes_accessed=6 * 10**6, transcendentals=3 * 10**6),
        name="block_backward",
    )


RESULTS = [
    jax.ShapeDtypeStruct(s, t)
    for s, t in (
        ((LAT_ROWS, COLS, CH), bf16),
        ((TAPS, CH), f32),
        ((1, CH), f32),
        ((1, CH), f32),
        ((1, CH), f32),
        ((CH, HID), f32),
        ((1, HID), f32),
        ((HID, CH), f32),
        ((1, CH), f32),
        ((1, CH), f32),
        ((1, 1), f32),
    )
]
BANDS = 6


def hand_on(*refs):
    n = len(RESULTS)
    src, dst, stage, sem_in, sem_out = refs[:n], refs[n : 2 * n], refs[2 * n : 3 * n], refs[3 * n], refs[3 * n + 1]
    rows = LAT_ROWS // BANDS

    def parts(i):
        return [pl.ds(j * rows, rows) for j in range(BANDS)] if i == 0 else [slice(None)]

    hops = []
    for i in range(n):
        for j, part in enumerate(parts(i)):
            slot = n + j if i == 0 else i
            hops.append((
                pltpu.make_async_copy(src[i].at[part], stage[i].at[part], sem_in.at[slot]),
                pltpu.make_async_copy(stage[i].at[part], dst[i].at[part], sem_out.at[slot]),
            ))
    for first, _ in hops:
        first.start()
    for first, second in hops:
        first.wait()
        second.start()
    for _, second in hops:
        second.wait()


def make_hand_on():
    n = len(RESULTS)
    hbm = pl.BlockSpec(memory_space=pltpu.HBM)
    dma = pltpu.SemaphoreType.DMA((n + BANDS,))
    return pl.pallas_call(
        hand_on,
        in_specs=[hbm] * n,
        out_specs=[hbm] * n,
        out_shape=RESULTS,
        scratch_shapes=[pltpu.VMEM(r.shape, r.dtype) for r in RESULTS] + [dma, dma],
        name="hand_on",
    )


def solution(mesh):
    nlon, nlat = mesh.shape["lon"], mesh.shape["lat"]
    nz, nx, nyh = (4, 4, 2) if nlon == 32 else (nlon, 1, 1)
    nyl, ncore = nlat // 2, 2
    total_rows, total_cols = LAT_ROWS * nlat, COLS * nlon
    call = make_kernel(nz, nx, nyh, nyl, ncore, total_rows * total_cols)
    finish = make_hand_on()
    fwd, fwd_tile, inv, taps, taps_inv = tables()
    place = (np.arange(total_rows, dtype=np.float32) + np.float32(0.5)) / np.float32(total_rows) - np.float32(0.5)
    weight = np.cos(np.float32(math.pi) * place).astype(np.float32)

    def on_device(field_in, conv_out, cotangent, kernel, ln_gain, ln_bias, w_in, b_in, w_out, b_out, layer_scale):
        line = lambda v: v.reshape(1, -1)
        outs = call(
            conv_out, cotangent, field_in, kernel, line(ln_gain), line(ln_bias), w_in, line(b_in),
            w_out, line(b_out), line(layer_scale), weight, fwd, fwd_tile, inv, taps, taps_inv,
        )
        d_field, d_kernel, d_cb, d_gain, d_bias, d_win, d_bin, d_wout, d_bout, d_ls, norm = finish(*outs)
        wide = lambda v: v.reshape(-1)
        return (
            d_field, d_kernel, wide(d_cb), wide(d_gain), wide(d_bias), d_win, wide(d_bin),
            d_wout, wide(d_bout), wide(d_ls), norm.reshape(()),
        )

    grid = P("lat", "lon", None)
    return jax.shard_map(
        on_device,
        mesh=mesh,
        in_specs=(grid, grid, grid) + (P(),) * 8,
        out_specs=(grid,) + (P(),) * 10,
        check_vma=False,
    )
```

```python
import math

import jax
import jax.numpy as jnp
import ml_dtypes
import numpy as np
from jax import lax
from jax.experimental import pallas as pl
from jax.experimental.pallas import tpu as pltpu
from jax.sharding import PartitionSpec as P

MESH = pl.DeviceIdType.MESH
f32, bf16 = jnp.float32, jnp.bfloat16
EPS = 1e-06
COEF = 0.044715
ROOT = math.sqrt(2.0 / math.pi)

N = 14
OUT = 8
PAIRS = 104
FREQ = 2 * PAIRS
SCALE = 1.828125
LAT_ROWS, COLS, CH, HID, TAPS = 96, 56, 128, 512, 49
TL, TC = LAT_ROWS // OUT, COLS // OUT
SMALL = 64
RIM = ((0, 0, LAT_ROWS), (TC - 1, 0, LAT_ROWS))


def tables():
    own = [(0, 0), (0, 7), (7, 0), (7, 7)]
    seen, pairs = set(own), []
    for k in range(N):
        for l in range(N):
            if (k, l) not in seen:
                seen.add((k, l))
                seen.add(((-k) % N, (-l) % N))
                pairs.append((k, l))
    freq = np.array(own + pairs)
    weight = np.array([1.0] * 4 + [2.0] * 96)[:, None] / (N * N)
    twin = np.array([0.0] * 4 + [1.0] * 96)[:, None]

    def angle(rows, cols, row_off, col_off):
        m, n = np.meshgrid(np.arange(rows) + row_off, np.arange(cols) + col_off, indexing="ij")
        m, n = m.ravel(), n.ravel()
        return 2 * np.pi * ((np.outer(freq[:, 0], m) + np.outer(freq[:, 1], n)) % N) / N

    def interleave(re, im):
        fill = np.zeros((PAIRS - 100, re.shape[1]))
        re, im = np.concatenate([re, fill]), np.concatenate([im, fill])
        shape = (PAIRS // 8, 8, re.shape[1])
        return np.stack([re.reshape(shape), im.reshape(shape)], 1).reshape(FREQ, -1)

    inside = np.tile(np.array([0.0] + [1.0] * 14 + [0.0]), N)
    a = angle(N, 16, 0, -1)
    fwd = interleave(np.cos(a) * inside, -np.sin(a) * inside * twin)
    a = angle(OUT, OUT, 6, 6)
    fwd_tile = interleave(np.cos(a), -np.sin(a) * twin)
    inv = interleave(np.cos(a) * weight, -np.sin(a) * weight * twin).T
    a = angle(7, 7, 0, 0)
    taps = interleave(np.cos(a), -np.sin(a) * twin)
    taps_inv = interleave(np.cos(a) * weight, -np.sin(a) * weight * twin).T
    area = N * N
    low = np.zeros((FREQ + OUT * OUT, 384))
    low[:FREQ, : N * 16] = fwd * SCALE
    low[:FREQ, 256 : 256 + OUT * OUT] = fwd_tile * SCALE
    low[FREQ:, :FREQ] = inv * area * SCALE
    high = np.zeros((FREQ + 56, FREQ))
    high[:FREQ, :TAPS] = taps / (area * SCALE * SCALE)
    high[FREQ : FREQ + TAPS] = taps_inv / (SCALE * SCALE)
    return low.astype(ml_dtypes.bfloat16), high.astype(np.float32)


def dot(a, b):
    return jnp.dot(a, b, preferred_element_type=f32)


def dot_exact(a, b):
    return jnp.dot(a, b, preferred_element_type=f32, precision=lax.Precision.HIGHEST)


def dot_last(a, b):
    return lax.dot_general(a, b, (((1,), (1,)), ((), ())), preferred_element_type=f32)


def dot_rows(a, b):
    return lax.dot_general(a, b, (((0,), (0,)), ((), ())), preferred_element_type=f32)


def rows8(v):
    return jnp.sum(v.reshape(v.shape[0] // 8, 8, v.shape[1]), 0)


def make_kernel(nz, nx, nyh, nyl, ncore, total_cells):
    nlon, nlat = nz * nx * nyh, nyl * ncore
    ny = nyh * nyl
    nb, na = nz * ny, nx * ncore
    wrows = 2 * CH // nb
    factor = float(total_cells) ** (-0.5)

    def kernel(
        x_hbm, c_hbm, f_hbm, ker_hbm, gain_hbm, bias_hbm, win_hbm, bin_hbm, wout_hbm, bout_hbm, ls_hbm,
        cos_ref, low_hbm, high_hbm,
        out_hbm, dwin_hbm, dwout_hbm, rest_hbm,
        dwin_ref, dwout_ref, rest_ref,
        gain_ref, bias_ref, win_ref, bin_ref, wout_ref, bout_ref, ls_ref, dps, norms, rstds,
        xv, cv, fv, outv, dup, yb, low_ref, high_ref, ker, kpad, kh, acc, gw, gbin, small, sm32,
        hs, hr, vs, vr, ws, wr, w2, wf, s1, s2,
        in_sem, const_sem, res_sem, out_sem, h_send, h_recv, v_send, v_recv,
        w1_send, w1_recv, w2_send, w2_recv, w3_send, w3_recv, s1_send, s1_recv, s2_send, s2_recv,
    ):
        lon, lat = lax.axis_index("lon"), lax.axis_index("lat")
        z, x, yh = lax.div(lon, nx * nyh), lax.rem(lax.div(lon, nyh), nx), lax.rem(lon, nyh)
        yl, core = lax.div(lat, ncore), lax.rem(lat, ncore)
        b_me = z * ny + yh * nyl + yl
        a_me = x * ncore + core

        def b_peer(b):
            bz, by = lax.div(b, ny), lax.rem(b, ny)
            return (bz * (nx * nyh) + x * nyh + lax.div(by, nyl), lax.rem(by, nyl) * ncore + core)

        def a_peer(a):
            return (z * (nx * nyh) + lax.div(a, ncore) * nyh + yh, yl * ncore + lax.rem(a, ncore))

        right, left = lax.rem(lon + 1, nlon), lax.rem(lon + nlon - 1, nlon)
        down, up = lax.rem(lat + 1, nlat), lax.rem(lat + nlat - 1, nlat)

        sides_x, middle_x = (pl.ds(0, 8), pl.ds(COLS - 8, 8)), pl.ds(8, COLS - 16)
        loads = [(x_hbm, xv, sides_x[0]), (c_hbm, cv, sides_x[0]), (x_hbm, xv, sides_x[1]), (c_hbm, cv, sides_x[1])]
        loads += [(x_hbm, xv, middle_x), (c_hbm, cv, middle_x), (f_hbm, fv, pl.ds(0, COLS))]

        def load(i):
            src, dst, cols = loads[i]
            return pltpu.make_async_copy(src.at[:, cols, :], dst.at[:, cols, :], in_sem.at[i])

        consts = (
            (gain_hbm, gain_ref), (bias_hbm, bias_ref), (win_hbm, win_ref), (bin_hbm, bin_ref), (wout_hbm, wout_ref),
            (ls_hbm, ls_ref), (bout_hbm, bout_ref),
            (low_hbm, low_ref), (high_hbm, high_ref), (ker_hbm, ker),
        )
        results = ((dwin_ref, dwin_hbm), (dwout_ref, dwout_hbm), (rest_ref, rest_hbm))

        def give(i):
            return pltpu.make_async_copy(*results[i], res_sem.at[i])

        def load_const(i):
            return pltpu.make_async_copy(*consts[i], const_sem.at[i])

        for i in range(4):
            load(i).start()
        for i in range(7):
            load_const(i).start()
        for i in range(4, len(loads)):
            load(i).start()
        for i in range(7, len(consts)):
            load_const(i).start()

        barrier = pltpu.get_barrier_semaphore()
        for peer in ((right, lat), (left, lat), (lon, down), (lon, up)):
            pl.semaphore_signal(barrier, inc=1, device_id=peer, device_id_type=MESH)

        def greet_b(d, carry):
            pl.semaphore_signal(barrier, inc=1, device_id=b_peer(lax.rem(b_me + d, nb)), device_id_type=MESH)
            return carry

        def greet_a(d, carry):
            pl.semaphore_signal(barrier, inc=1, device_id=a_peer(lax.rem(a_me + d, na)), device_id_type=MESH)
            return carry

        lax.fori_loop(1, nb, greet_b, 0)
        lax.fori_loop(1, na, greet_a, 0)

        third = jnp.full((CH, CH), 1.0 / CH, bf16)
        none = jnp.zeros((CH, CH), bf16)
        mean_two = jnp.concatenate(
            [jnp.concatenate([third, none], 1), jnp.concatenate([none, third], 1)], 0
        )
        gw[...] = jnp.zeros_like(gw)
        gbin[...] = jnp.zeros_like(gbin)
        small[...] = jnp.zeros_like(small)
        acc[...] = jnp.zeros_like(acc)
        kpad[...] = jnp.zeros_like(kpad)

        for i in range(7):
            load_const(i).wait()
        gain, bias, scale = gain_ref[...], bias_ref[...], ls_ref[...]
        win_half, bin_half = win_ref[...] * jnp.asarray(0.5, bf16), bin_ref[...] * 0.5
        wout_half = wout_ref[...] * jnp.asarray(0.5, bf16)

        def cells_of(ref, parts):
            return jnp.concatenate([ref[pl.ds(r0, n), 8 * t : 8 * t + 8, :].astype(f32).reshape(n * 8, CH) for t, r0, n in parts], 0)

        def mlp_grads(parts):
            value = cells_of(xv, parts)
            center = value - dot(value.astype(bf16), third)
            rstd = lax.rsqrt(dot((center * center).astype(bf16), third) + EPS)
            normed = center * rstd
            zed = (normed * gain + bias).astype(bf16)
            cot = cells_of(cv, parts)
            cb = cot.astype(bf16)
            d_out = (cot * scale).astype(bf16)
            acts, dpres = [], []
            g_bin = jnp.zeros((8, HID), f32)
            sub = value.shape[0] // 2
            for s in range(0, value.shape[0], sub):
                h = dot(zed[s : s + sub], win_half) + bin_half
                d_act = dot_last(d_out[s : s + sub], wout_half)
                h2 = h * h
                tangent = jnp.tanh(h * (2 * ROOT + (8 * ROOT * COEF) * h2))
                wide = h * (2 * ROOT + (24 * ROOT * COEF) * h2)
                above = 1.0 + tangent
                d_pre = d_act * (above * (1.0 + (1.0 - tangent) * wide))
                g_bin = g_bin + rows8(d_pre)
                acts.append((h * above).astype(bf16))
                dpres.append(d_pre.astype(bf16))
            act, d_pre = jnp.concatenate(acts, 0), jnp.concatenate(dpres, 0)
            gbin[...] += g_bin
            gw[CH:, :] += dot_rows(cb, act)
            gw[:CH, :] += dot_rows(zed, d_pre)
            small[3] += rows8(cot)
            return d_pre, normed, rstd

        def mlp_du(parts, d_pre, normed, rstd):
            d_zed = dot_last(d_pre, win_ref[...])
            d_gain = d_zed * normed
            d_norm = d_zed * gain
            means = dot(
                jnp.concatenate([d_norm.astype(bf16), (d_gain * gain).astype(bf16)], 1), mean_two
            )
            du = rstd * (d_norm - means[:, :CH] - normed * means[:, CH:])
            at = 0
            for t, r0, n in parts:
                dup[pl.ds(3 + r0, n), 4 + 8 * t : 12 + 8 * t, :] = du[at : at + 8 * n].reshape(n, 8, CH)
                at += 8 * n
            small[0] += rows8(d_gain)
            small[1] += rows8(d_zed)
            small[2] += rows8(du)

        for i in range(4):
            load(i).wait()
        mlp_du(RIM, *mlp_grads(RIM))

        half = LAT_ROWS // 2
        low = lax.broadcasted_iota(jnp.int32, (half, 8, CH), 1) < 4

        def copy_h(side):
            return pltpu.make_async_remote_copy(
                src_ref=hs.at[side], dst_ref=hr.at[side], send_sem=h_send.at[side], recv_sem=h_recv.at[side],
                device_id=((right, lat), (left, lat))[side], device_id_type=MESH,
            )

        def copy_v(side):
            return pltpu.make_async_remote_copy(
                src_ref=vs.at[side], dst_ref=vr.at[side], send_sem=v_send.at[side], recv_sem=v_recv.at[side],
                device_id=((lon, down), (lon, up))[side], device_id_type=MESH,
            )

        pl.semaphore_wait(barrier, 4 + (nb - 1) + (na - 1))
        first, second = dup[3 : 3 + half, 56:64, :], dup[3 + half : 3 + LAT_ROWS, 56:64, :]
        hs[0] = jnp.where(low, first, pltpu.roll(second, 4, 1)).reshape(half * 8, CH).astype(bf16)
        copy_h(0).start()
        first, second = dup[3 : 3 + half, 0:8, :], dup[3 + half : 3 + LAT_ROWS, 0:8, :]
        hs[1] = jnp.where(low, pltpu.roll(second, 4, 1), first).reshape(half * 8, CH).astype(bf16)
        copy_h(1).start()

        load(4).wait()
        load(5).wait()

        def middle_parts(i):
            return [(t, i * half, half) for t in range(1, TC - 1)]

        def middle_grads(i, carry):
            dps[i], norms[i], rstds[i] = mlp_grads(middle_parts(i))
            return carry

        def middle_du(i, carry):
            mlp_du(middle_parts(i), dps[i], norms[i], rstds[i])
            return carry

        lax.fori_loop(0, 2, middle_grads, 0)

        def copy_w1(b_to, b_from):
            return pltpu.make_async_remote_copy(
                src_ref=ws.at[b_to], dst_ref=wr.at[b_from], send_sem=w1_send.at[b_to], recv_sem=w1_recv.at[b_from],
                device_id=b_peer(b_to), device_id_type=MESH,
            )

        def copy_w2(a_to, a_from):
            return pltpu.make_async_remote_copy(
                src_ref=w2.at[a_me], dst_ref=w2.at[a_from], send_sem=w2_send.at[a_to], recv_sem=w2_recv.at[a_from],
                device_id=a_peer(a_to), device_id_type=MESH,
            )

        def copy_w3(b_to, b_from):
            return pltpu.make_async_remote_copy(
                src_ref=wf.at[b_me], dst_ref=wf.at[b_from], send_sem=w3_send.at[b_to], recv_sem=w3_recv.at[b_from],
                device_id=b_peer(b_to), device_id_type=MESH,
            )

        def copy_s1(b_to, b_from):
            return pltpu.make_async_remote_copy(
                src_ref=s1.at[b_me], dst_ref=s1.at[b_from], send_sem=s1_send.at[b_to], recv_sem=s1_recv.at[b_from],
                device_id=b_peer(b_to), device_id_type=MESH,
            )

        def copy_s2(a_to, a_from):
            return pltpu.make_async_remote_copy(
                src_ref=s2.at[a_me], dst_ref=s2.at[a_from], send_sem=s2_send.at[a_to], recv_sem=s2_recv.at[a_from],
                device_id=a_peer(a_to), device_id_type=MESH,
            )

        def over(copy, act, me, size):
            def body(d, carry):
                peer = lax.rem(me + d, size)
                if act == "send":
                    copy(peer, me).start()
                elif act == "recv":
                    copy(peer, peer).wait_recv()
                else:
                    copy(peer, me).wait_send()
                return carry

            lax.fori_loop(1, size, body, 0)

        def over_a(copy, act):
            over(copy, act, a_me, na)

        def over_b(copy, act):
            over(copy, act, b_me, nb)

        ws[...] = gw[...].astype(bf16).reshape(nb, wrows, HID)
        over_b(copy_w1, "send")
        lax.fori_loop(0, 2, middle_du, 0)

        copy_h(0).wait_recv()
        copy_h(1).wait_recv()
        near = hr[0].astype(f32).reshape(half, 8, CH)
        dup[3 : 3 + half, 0:8, :] = jnp.where(low, near, dup[3 : 3 + half, 0:8, :])
        dup[3 + half : 3 + LAT_ROWS, 0:8, :] = jnp.where(
            low, pltpu.roll(near, 4, 1), dup[3 + half : 3 + LAT_ROWS, 0:8, :]
        )
        near = hr[1].astype(f32).reshape(half, 8, CH)
        dup[3 : 3 + half, 56:64, :] = jnp.where(low, dup[3 : 3 + half, 56:64, :], near)
        dup[3 + half : 3 + LAT_ROWS, 56:64, :] = jnp.where(
            low, dup[3 + half : 3 + LAT_ROWS, 56:64, :], pltpu.roll(near, 4, 1)
        )
        vs[0] = dup[LAT_ROWS : LAT_ROWS + 3].reshape(192, CH).astype(bf16)
        vs[1] = dup[3:6].reshape(192, CH).astype(bf16)
        copy_v(0).start()
        copy_v(1).start()

        for i in range(7, len(consts)):
            load_const(i).wait()
        load(6).wait()
        kpad[0:TAPS] = ker[...]
        kh[...] = dot_exact(high_ref[0:FREQ, 0:56], kpad[...])

        def tile_pair(slot, i0, i1, t):
            def window(i):
                return dup[pl.ds(i * OUT, N), 8 * t : 8 * t + 16, :].reshape(N * 16, CH).astype(bf16)

            def field(i):
                tile = fv[pl.ds(i * OUT, OUT), 8 * t : 8 * t + 8, :].astype(f32)
                tile = [tile[r] * cos_ref[lat * LAT_ROWS + i * OUT + r] for r in range(OUT)]
                return jnp.concatenate(tile, 0).astype(bf16)

            shape = (PAIRS // 8, 2, 8, 2 * CH)
            w = dot(low_ref[0:FREQ, 0 : N * 16], jnp.concatenate([window(i0), window(i1)], 1)).reshape(shape)
            g = dot(low_ref[0:FREQ, 256 : 256 + OUT * OUT], jnp.concatenate([field(i0), field(i1)], 1)).reshape(shape)
            k = kh[...].reshape(PAIRS // 8, 2, 8, CH)
            k = jnp.concatenate([k, k], -1)
            w_re, w_im, g_re, g_im, k_re, k_im = w[:, 0], w[:, 1], g[:, 0], g[:, 1], k[:, 0], k[:, 1]
            y = jnp.stack([k_re * w_re - k_im * w_im, k_re * w_im + k_im * w_re], 1)
            yb[slot] = y.reshape(FREQ, 2 * CH).astype(bf16)
            d = jnp.stack([g_re * w_re + g_im * w_im, g_im * w_re - g_re * w_im], 1).reshape(FREQ, 2 * CH)
            acc[...] += d[:, :CH] + d[:, CH:]

        pairs = TL // 2

        def middle(j, carry):
            for t in range(1, TC - 1):
                tile_pair(t * pairs + j, 1 + 2 * j, 2 + 2 * j, t)
            return carry

        def sides(j, carry):
            for t in (0, TC - 1):
                tile_pair(t * pairs + j, 1 + 2 * j, 2 + 2 * j, t)
            return carry

        lax.fori_loop(0, pairs - 1, middle, 0)
        lax.fori_loop(0, pairs - 1, sides, 0)

        copy_v(0).wait_recv()
        copy_v(1).wait_recv()
        zero = jnp.zeros((3, 64, CH), f32)
        dup[0:3] = jnp.where(lat > 0, vr[0].astype(f32).reshape(3, 64, CH), zero)
        dup[LAT_ROWS + 3 : LAT_ROWS + 6] = jnp.where(lat < nlat - 1, vr[1].astype(f32).reshape(3, 64, CH), zero)
        for t in range(TC):
            tile_pair(t * pairs + pairs - 1, 0, TL - 1, t)

        sm32[...] = jnp.zeros_like(sm32)
        sm32[0:56] = dot_exact(high_ref[FREQ : FREQ + 56, :], acc[...])
        total = jnp.sum(gbin[...], 0, keepdims=True)
        for q in range(4):
            sm32[49 + q : 50 + q] = total[:, q * CH : (q + 1) * CH]
            sm32[53 + q : 54 + q] = jnp.sum(small[q], 0, keepdims=True)
        s1[b_me] = sm32[...].astype(bf16)
        over_b(copy_s1, "send")

        wr[b_me] = ws[b_me]
        over_b(copy_w1, "recv")
        w2[a_me] = jnp.sum(wr[...].astype(f32), 0).astype(bf16)
        over_a(copy_w2, "send")

        def store(j):
            n = OUT if j >= pairs - 1 else 2 * OUT
            at = (0, LAT_ROWS - OUT)[j - pairs + 1] if j >= pairs - 1 else (1 + 2 * j) * OUT
            return pltpu.make_async_copy(outv.at[pl.ds(at, n)], out_hbm.at[pl.ds(at, n)], out_sem.at[j])

        def finish(j, ends):
            for t in range(TC):
                conv = dot(low_ref[FREQ:, 0:FREQ], yb[t * pairs + j]).reshape(OUT, OUT, 2 * CH)
                for n, i in enumerate(ends):
                    cot = cv[i * OUT : (i + 1) * OUT, 8 * t : 8 * t + 8, :].astype(f32)
                    part = conv[:, :, n * CH : (n + 1) * CH]
                    value = [cot[r] + part[r] * cos_ref[lat * LAT_ROWS + i * OUT + r] for r in range(OUT)]
                    outv[i * OUT : (i + 1) * OUT, 8 * t : 8 * t + 8, :] = jnp.stack(value, 0).astype(bf16)

        for j in range(pairs - 1):
            finish(j, (1 + 2 * j, 2 + 2 * j))
            store(j).start()
        finish(pairs - 1, (0, TL - 1))
        store(pairs - 1).start()
        store(pairs).start()
        over_a(copy_w2, "recv")
        wf[b_me] = jnp.sum(w2[...].astype(f32), 0).astype(bf16)
        over_b(copy_w3, "send")
        over_b(copy_s1, "recv")
        s2[a_me] = jnp.sum(s1[...].astype(f32), 0).astype(bf16)
        over_a(copy_s2, "send")

        over_b(copy_w3, "recv")
        d_win = jnp.concatenate([wf[b].astype(f32) for b in range(nb // 2)], 0) * factor
        dwin_ref[...] = d_win
        give(0).start()
        g_out = jnp.concatenate([wf[b].astype(f32) for b in range(nb // 2, nb)], 0) * factor
        g_out = g_out.T
        d_wout = g_out * scale
        dwout_ref[...] = d_wout
        give(1).start()
        squares = jnp.sum(d_win * d_win, 0, keepdims=True)
        squares = sum(squares[:, q * CH : (q + 1) * CH] for q in range(4))
        squares = squares + jnp.sum(d_wout * d_wout, 0, keepdims=True)
        g_ls = jnp.sum(g_out * wout_ref[...].astype(f32), 0, keepdims=True)
        over_a(copy_s2, "recv")
        sm32[...] = jnp.sum(s2[...].astype(f32), 0) * factor
        dk = sm32[0:TAPS]
        d_bin = jnp.concatenate([sm32[49 + q : 50 + q] for q in range(4)], 1)
        d_gain, d_bias, d_cb, s_cot = (sm32[53 + q : 54 + q] for q in range(4))
        d_bout = s_cot * scale
        d_ls = g_ls + bout_ref[...] * s_cot
        rest_ref[...] = sm32[...]
        rest_ref[56:57] = d_bout
        rest_ref[57:58] = d_ls
        squares = squares + jnp.sum(dk * dk, 0, keepdims=True)
        for q in range(4):
            squares = squares + d_bin[:, q * CH : (q + 1) * CH] * d_bin[:, q * CH : (q + 1) * CH]
        for part in (d_gain, d_bias, d_cb, d_bout, d_ls):
            squares = squares + part * part
        rest_ref[58:59] = jnp.broadcast_to(jnp.sqrt(jnp.sum(squares, 1, keepdims=True)), (1, CH))
        give(2).start()

        for side in range(2):
            copy_h(side).wait_send()
            copy_v(side).wait_send()
        over_b(copy_w1, "done")
        over_a(copy_w2, "done")
        over_b(copy_w3, "done")
        over_b(copy_s1, "done")
        over_a(copy_s2, "done")
        for j in range(pairs + 1):
            store(j).wait()
        for i in range(len(results)):
            give(i).wait()

    hbm, smem = pl.BlockSpec(memory_space=pl.ANY), pl.BlockSpec(memory_space=pltpu.SMEM)
    shape = jax.ShapeDtypeStruct
    dma = pltpu.SemaphoreType.DMA
    field = (LAT_ROWS, COLS, CH)
    return pl.pallas_call(
        kernel,
        in_specs=[hbm] * 11 + [smem] + [hbm] * 2,
        out_specs=[hbm] * 4,
        out_shape=HANDED,
        scratch_shapes=[pltpu.VMEM(r.shape, r.dtype) for r in HANDED[1:]]
        + [
            pltpu.VMEM((1, CH), f32),
            pltpu.VMEM((1, CH), f32),
            pltpu.VMEM((CH, HID), bf16),
            pltpu.VMEM((1, HID), f32),
            pltpu.VMEM((HID, CH), bf16),
            pltpu.VMEM((1, CH), f32),
            pltpu.VMEM((1, CH), f32),
            pltpu.VMEM((2, LAT_ROWS // 2 * (COLS - 16), HID), bf16),
            pltpu.VMEM((2, LAT_ROWS // 2 * (COLS - 16), CH), f32),
            pltpu.VMEM((2, LAT_ROWS // 2 * (COLS - 16), CH), f32),
            pltpu.VMEM(field, bf16),
            pltpu.VMEM(field, bf16),
            pltpu.VMEM(field, bf16),
            pltpu.VMEM(field, bf16),
            pltpu.VMEM((LAT_ROWS + 6, COLS + 8, CH), f32),
            pltpu.VMEM((TL * TC // 2, FREQ, 2 * CH), bf16),
            pltpu.VMEM((FREQ + OUT * OUT, 384), bf16),
            pltpu.VMEM((FREQ + 56, FREQ), f32),
            pltpu.VMEM((TAPS, CH), f32),
            pltpu.VMEM((56, CH), f32),
            pltpu.VMEM((FREQ, CH), f32),
            pltpu.VMEM((FREQ, CH), f32),
            pltpu.VMEM((2 * CH, HID), f32),
            pltpu.VMEM((8, HID), f32),
            pltpu.VMEM((4, 8, CH), f32),
            pltpu.VMEM((SMALL, CH), f32),
            pltpu.VMEM((2, LAT_ROWS * 4, CH), bf16),
            pltpu.VMEM((2, LAT_ROWS * 4, CH), bf16),
            pltpu.VMEM((2, 192, CH), bf16),
            pltpu.VMEM((2, 192, CH), bf16),
            pltpu.VMEM((nb, wrows, HID), bf16),
            pltpu.VMEM((nb, wrows, HID), bf16),
            pltpu.VMEM((na, wrows, HID), bf16),
            pltpu.VMEM((nb, wrows, HID), bf16),
            pltpu.VMEM((nb, SMALL, CH), bf16),
            pltpu.VMEM((na, SMALL, CH), bf16),
            dma((7,)),
            dma((10,)),
            dma((3,)),
            dma((TC,)),
            dma((2,)),
            dma((2,)),
            dma((2,)),
            dma((2,)),
        ]
        + [dma((n,)) for n in (nb, nb, na, na, nb, nb, nb, nb, na, na)],
        compiler_params=pltpu.CompilerParams(
            collective_id=0, has_side_effects=True, vmem_limit_bytes=60 * 2**20
        ),
        cost_estimate=pl.CostEstimate(flops=6 * 10**9, bytes_accessed=6 * 10**6, transcendentals=3 * 10**6),
        name="block_backward",
    )


RESULTS = [
    jax.ShapeDtypeStruct(s, t)
    for s, t in (
        ((LAT_ROWS, COLS, CH), bf16),
        ((TAPS, CH), f32),
        ((1, CH), f32),
        ((1, CH), f32),
        ((1, CH), f32),
        ((CH, HID), f32),
        ((1, HID), f32),
        ((HID, CH), f32),
        ((1, CH), f32),
        ((1, CH), f32),
        ((1, 1), f32),
    )
]
HANDED = [RESULTS[0], RESULTS[5], RESULTS[7], jax.ShapeDtypeStruct((SMALL, CH), f32)]
ROWS = ((2, 55), (3, 53), (4, 54), (8, 56), (9, 57))
BANDS = 4


def hand_on(*refs):
    n, m = len(RESULTS), len(HANDED)
    src, dst = refs[:m], refs[m : m + n]
    stage, lines, sem_in, sem_out = refs[m + n : 2 * m + n], refs[2 * m + n : -2], refs[-2], refs[-1]
    rows = LAT_ROWS // BANDS
    hops = []
    for i, to in enumerate((0, 5, 7)):
        for j in range(BANDS if i == 0 else 1):
            part = pl.ds(j * rows, rows) if i == 0 else slice(None)
            slot = n + j if i == 0 else to
            hops.append((
                pltpu.make_async_copy(src[i].at[part], stage[i].at[part], sem_in.at[slot]),
                pltpu.make_async_copy(stage[i].at[part], dst[to].at[part], sem_out.at[slot]),
            ))
    block_in = pltpu.make_async_copy(src[3], stage[3], sem_in.at[0])
    block_in.start()
    for first, _ in hops:
        first.start()
    block_in.wait()
    block = stage[3]
    lines[0][...] = block[0:TAPS]
    lines[1][...] = jnp.concatenate([block[49 + q : 50 + q] for q in range(4)], 1)
    lines[2][...] = block[58:59, 0:1]
    for line, (_, row) in zip(lines[3:], ROWS):
        line[...] = block[row : row + 1]
    outs = [second for _, second in hops]
    small = [
        pltpu.make_async_copy(line, dst[to], sem_out.at[to])
        for line, to in zip(lines, (1, 6, 10) + tuple(to for to, _ in ROWS))
    ]
    for copy in small:
        copy.start()
    for first, second in hops:
        first.wait()
        second.start()
    for copy in small + outs:
        copy.wait()


def make_hand_on():
    n = len(RESULTS)
    hbm = pl.BlockSpec(memory_space=pltpu.HBM)
    dma = pltpu.SemaphoreType.DMA((n + BANDS,))
    order = (1, 6, 10) + tuple(to for to, _ in ROWS)
    return pl.pallas_call(
        hand_on,
        in_specs=[hbm] * len(HANDED),
        out_specs=[hbm] * n,
        out_shape=RESULTS,
        scratch_shapes=[pltpu.VMEM(r.shape, r.dtype) for r in HANDED + [RESULTS[i] for i in order]] + [dma, dma],
        name="hand_on",
    )


def solution(mesh):
    nlon, nlat = mesh.shape["lon"], mesh.shape["lat"]
    nz, nx, nyh = (4, 4, 2) if nlon == 32 else (nlon, 1, 1)
    nyl, ncore = nlat // 2, 2
    total_rows, total_cols = LAT_ROWS * nlat, COLS * nlon
    call = make_kernel(nz, nx, nyh, nyl, ncore, total_rows * total_cols)
    finish = make_hand_on()
    low, high = tables()
    place = (np.arange(total_rows, dtype=np.float32) + np.float32(0.5)) / np.float32(total_rows) - np.float32(0.5)
    weight = np.cos(np.float32(math.pi) * place).astype(np.float32)

    def on_device(field_in, conv_out, cotangent, kernel, ln_gain, ln_bias, w_in, b_in, w_out, b_out, layer_scale):
        line = lambda v: v.reshape(1, -1)
        outs = call(
            conv_out, cotangent, field_in, kernel, line(ln_gain), line(ln_bias), w_in, line(b_in),
            w_out, line(b_out), line(layer_scale), weight, low, high,
        )
        d_field, d_kernel, d_cb, d_gain, d_bias, d_win, d_bin, d_wout, d_bout, d_ls, norm = finish(*outs)
        wide = lambda v: v.reshape(-1)
        return (
            d_field, d_kernel, wide(d_cb), wide(d_gain), wide(d_bias), d_win, wide(d_bin),
            d_wout, wide(d_bout), wide(d_ls), norm.reshape(()),
        )

    grid = P("lat", "lon", None)
    return jax.shard_map(
        on_device,
        mesh=mesh,
        in_specs=(grid, grid, grid) + (P(),) * 8,
        out_specs=(grid,) + (P(),) * 10,
        check_vma=False,
    )
```

```python
import math

import jax
import jax.numpy as jnp
import ml_dtypes
import numpy as np
from jax import lax
from jax.experimental import pallas as pl
from jax.experimental.pallas import tpu as pltpu
from jax.sharding import PartitionSpec as P

MESH = pl.DeviceIdType.MESH
f32, bf16 = jnp.float32, jnp.bfloat16
EPS = 1e-06
COEF = 0.044715
ROOT = math.sqrt(2.0 / math.pi)

N = 14
OUT = 8
PAIRS = 104
FREQ = 2 * PAIRS
SCALE = 1.828125
LAT_ROWS, COLS, CH, HID, TAPS = 96, 56, 128, 512, 49
TL, TC = LAT_ROWS // OUT, COLS // OUT
SMALL = 64
RIM = ((0, 0, LAT_ROWS), (TC - 1, 0, LAT_ROWS))


def tables():
    own = [(0, 0), (0, 7), (7, 0), (7, 7)]
    seen, pairs = set(own), []
    for k in range(N):
        for l in range(N):
            if (k, l) not in seen:
                seen.add((k, l))
                seen.add(((-k) % N, (-l) % N))
                pairs.append((k, l))
    freq = np.array(own + pairs)
    weight = np.array([1.0] * 4 + [2.0] * 96)[:, None] / (N * N)
    twin = np.array([0.0] * 4 + [1.0] * 96)[:, None]

    def angle(rows, cols, row_off, col_off):
        m, n = np.meshgrid(np.arange(rows) + row_off, np.arange(cols) + col_off, indexing="ij")
        m, n = m.ravel(), n.ravel()
        return 2 * np.pi * ((np.outer(freq[:, 0], m) + np.outer(freq[:, 1], n)) % N) / N

    def interleave(re, im):
        fill = np.zeros((PAIRS - 100, re.shape[1]))
        re, im = np.concatenate([re, fill]), np.concatenate([im, fill])
        shape = (PAIRS // 8, 8, re.shape[1])
        return np.stack([re.reshape(shape), im.reshape(shape)], 1).reshape(FREQ, -1)

    inside = np.tile(np.array([0.0] + [1.0] * 14 + [0.0]), N)
    a = angle(N, 16, 0, -1)
    fwd = interleave(np.cos(a) * inside, -np.sin(a) * inside * twin)
    a = angle(OUT, OUT, 6, 6)
    fwd_tile = interleave(np.cos(a), -np.sin(a) * twin)
    inv = interleave(np.cos(a) * weight, -np.sin(a) * weight * twin).T
    a = angle(7, 7, 0, 0)
    taps = interleave(np.cos(a), -np.sin(a) * twin)
    taps_inv = interleave(np.cos(a) * weight, -np.sin(a) * weight * twin).T
    area = N * N
    low = np.zeros((FREQ + OUT * OUT, 384))
    low[:FREQ, : N * 16] = fwd * SCALE
    low[:FREQ, 256 : 256 + OUT * OUT] = fwd_tile * SCALE
    low[FREQ:, :FREQ] = inv * area * SCALE
    high = np.zeros((FREQ + 56, FREQ))
    high[:FREQ, :TAPS] = taps / (area * SCALE * SCALE)
    high[FREQ : FREQ + TAPS] = taps_inv / (SCALE * SCALE)
    return low.astype(ml_dtypes.bfloat16), high.astype(np.float32)


def dot(a, b):
    return jnp.dot(a, b, preferred_element_type=f32)


def dot_exact(a, b):
    return jnp.dot(a, b, preferred_element_type=f32, precision=lax.Precision.HIGHEST)


def dot_last(a, b):
    return lax.dot_general(a, b, (((1,), (1,)), ((), ())), preferred_element_type=f32)


def dot_rows(a, b):
    return lax.dot_general(a, b, (((0,), (0,)), ((), ())), preferred_element_type=f32)


def rows8(v):
    return jnp.sum(v.reshape(v.shape[0] // 8, 8, v.shape[1]), 0)


def make_kernel(nz, nx, nyh, nyl, ncore, total_cells):
    nlon, nlat = nz * nx * nyh, nyl * ncore
    ny = nyh * nyl
    nb, na = nz * ny, nx * ncore
    wrows = 2 * CH // nb
    factor = float(total_cells) ** (-0.5)

    def kernel(
        x_hbm, c_hbm, f_hbm, ker_hbm, gain_hbm, bias_hbm, win_hbm, bin_hbm, wout_hbm, bout_hbm, ls_hbm,
        cos_ref, low_hbm, high_hbm,
        out_hbm, dwin_hbm, dwout_hbm, rest_hbm,
        dwin_ref, dwout_ref, rest_ref,
        gain_ref, bias_ref, win_ref, bin_ref, wout_ref, bout_ref, ls_ref, dps, norms, rstds,
        xv, cv, fv, outv, dup, yb, low_ref, high_ref, ker, kpad, kh, acc, gw, gbin, small, sm32,
        hs, hr, vs, vr, ws, wr, w2, wf, s1, s2,
        in_sem, const_sem, res_sem, out_sem, h_send, h_recv, v_send, v_recv,
        w1_send, w1_recv, w2_send, w2_recv, w3_send, w3_recv, s1_send, s1_recv, s2_send, s2_recv,
    ):
        lon, lat = lax.axis_index("lon"), lax.axis_index("lat")
        z, x, yh = lax.div(lon, nx * nyh), lax.rem(lax.div(lon, nyh), nx), lax.rem(lon, nyh)
        yl, core = lax.div(lat, ncore), lax.rem(lat, ncore)
        b_me = z * ny + yh * nyl + yl
        a_me = x * ncore + core

        def b_peer(b):
            bz, by = lax.div(b, ny), lax.rem(b, ny)
            return (bz * (nx * nyh) + x * nyh + lax.div(by, nyl), lax.rem(by, nyl) * ncore + core)

        def a_peer(a):
            return (z * (nx * nyh) + lax.div(a, ncore) * nyh + yh, yl * ncore + lax.rem(a, ncore))

        right, left = lax.rem(lon + 1, nlon), lax.rem(lon + nlon - 1, nlon)
        down, up = lax.rem(lat + 1, nlat), lax.rem(lat + nlat - 1, nlat)

        sides_x, middle_x = (pl.ds(0, 8), pl.ds(COLS - 8, 8)), pl.ds(8, COLS - 16)
        loads = [(x_hbm, xv, sides_x[0]), (c_hbm, cv, sides_x[0]), (x_hbm, xv, sides_x[1]), (c_hbm, cv, sides_x[1])]
        loads += [(x_hbm, xv, middle_x), (c_hbm, cv, middle_x), (f_hbm, fv, pl.ds(0, COLS))]

        def load(i):
            src, dst, cols = loads[i]
            return pltpu.make_async_copy(src.at[:, cols, :], dst.at[:, cols, :], in_sem.at[i])

        consts = (
            (gain_hbm, gain_ref), (bias_hbm, bias_ref), (win_hbm, win_ref), (bin_hbm, bin_ref), (wout_hbm, wout_ref),
            (ls_hbm, ls_ref), (bout_hbm, bout_ref),
            (low_hbm, low_ref), (high_hbm, high_ref), (ker_hbm, ker),
        )
        results = ((dwin_ref, dwin_hbm), (dwout_ref, dwout_hbm), (rest_ref, rest_hbm))

        def give(i):
            return pltpu.make_async_copy(*results[i], res_sem.at[i])

        def load_const(i):
            return pltpu.make_async_copy(*consts[i], const_sem.at[i])

        for i in range(4):
            load(i).start()
        for i in range(7):
            load_const(i).start()
        for i in range(4, len(loads)):
            load(i).start()
        for i in range(7, len(consts)):
            load_const(i).start()

        barrier = pltpu.get_barrier_semaphore()
        for peer in ((right, lat), (left, lat), (lon, down), (lon, up)):
            pl.semaphore_signal(barrier, inc=1, device_id=peer, device_id_type=MESH)

        def greet_b(d, carry):
            pl.semaphore_signal(barrier, inc=1, device_id=b_peer(lax.rem(b_me + d, nb)), device_id_type=MESH)
            return carry

        def greet_a(d, carry):
            pl.semaphore_signal(barrier, inc=1, device_id=a_peer(lax.rem(a_me + d, na)), device_id_type=MESH)
            return carry

        lax.fori_loop(1, nb, greet_b, 0)
        lax.fori_loop(1, na, greet_a, 0)

        third = jnp.full((CH, CH), 1.0 / CH, bf16)
        none = jnp.zeros((CH, CH), bf16)
        mean_two = jnp.concatenate(
            [jnp.concatenate([third, none], 1), jnp.concatenate([none, third], 1)], 0
        )
        gw[...] = jnp.zeros_like(gw)
        gbin[...] = jnp.zeros_like(gbin)
        small[...] = jnp.zeros_like(small)
        acc[...] = jnp.zeros_like(acc)
        kpad[...] = jnp.zeros_like(kpad)

        for i in range(7):
            load_const(i).wait()
        gain, bias, scale = gain_ref[...], bias_ref[...], ls_ref[...]
        win_half, bin_half = win_ref[...] * jnp.asarray(0.5, bf16), bin_ref[...] * 0.5
        wout_half = wout_ref[...] * jnp.asarray(0.5, bf16)

        def cells_of(ref, parts):
            return jnp.concatenate([ref[pl.ds(r0, n), 8 * t : 8 * t + 8, :].astype(f32).reshape(n * 8, CH) for t, r0, n in parts], 0)

        def mlp_grads(parts):
            value = cells_of(xv, parts)
            center = value - dot(value.astype(bf16), third)
            rstd = lax.rsqrt(dot((center * center).astype(bf16), third) + EPS)
            normed = center * rstd
            zed = (normed * gain + bias).astype(bf16)
            cot = cells_of(cv, parts)
            cb = cot.astype(bf16)
            d_out = (cot * scale).astype(bf16)
            acts, dpres = [], []
            g_bin = jnp.zeros((8, HID), f32)
            sub = value.shape[0] // 2
            for s in range(0, value.shape[0], sub):
                h = dot(zed[s : s + sub], win_half) + bin_half
                d_act = dot_last(d_out[s : s + sub], wout_half)
                h2 = h * h
                tangent = jnp.tanh(h * (2 * ROOT + (8 * ROOT * COEF) * h2))
                wide = h * (2 * ROOT + (24 * ROOT * COEF) * h2)
                above = 1.0 + tangent
                d_pre = d_act * (above * (1.0 + (1.0 - tangent) * wide))
                g_bin = g_bin + rows8(d_pre)
                acts.append((h * above).astype(bf16))
                dpres.append(d_pre.astype(bf16))
            act, d_pre = jnp.concatenate(acts, 0), jnp.concatenate(dpres, 0)
            gbin[...] += g_bin
            gw[CH:, :] += dot_rows(cb, act)
            gw[:CH, :] += dot_rows(zed, d_pre)
            small[3] += rows8(cot)
            return d_pre, normed, rstd

        def mlp_du(parts, d_pre, normed, rstd):
            d_zed = dot_last(d_pre, win_ref[...])
            d_gain = d_zed * normed
            d_norm = d_zed * gain
            means = dot(
                jnp.concatenate([d_norm.astype(bf16), (d_gain * gain).astype(bf16)], 1), mean_two
            )
            du = rstd * (d_norm - means[:, :CH] - normed * means[:, CH:])
            at = 0
            for t, r0, n in parts:
                dup[pl.ds(3 + r0, n), 4 + 8 * t : 12 + 8 * t, :] = du[at : at + 8 * n].reshape(n, 8, CH)
                at += 8 * n
            small[0] += rows8(d_gain)
            small[1] += rows8(d_zed)
            small[2] += rows8(du)

        for i in range(4):
            load(i).wait()
        mlp_du(RIM, *mlp_grads(RIM))

        half = LAT_ROWS // 2
        low = lax.broadcasted_iota(jnp.int32, (half, 8, CH), 1) < 4

        def copy_h(side):
            return pltpu.make_async_remote_copy(
                src_ref=hs.at[side], dst_ref=hr.at[side], send_sem=h_send.at[side], recv_sem=h_recv.at[side],
                device_id=((right, lat), (left, lat))[side], device_id_type=MESH,
            )

        def copy_v(side):
            return pltpu.make_async_remote_copy(
                src_ref=vs.at[side], dst_ref=vr.at[side], send_sem=v_send.at[side], recv_sem=v_recv.at[side],
                device_id=((lon, down), (lon, up))[side], device_id_type=MESH,
            )

        pl.semaphore_wait(barrier, 4 + (nb - 1) + (na - 1))
        first, second = dup[3 : 3 + half, 56:64, :], dup[3 + half : 3 + LAT_ROWS, 56:64, :]
        hs[0] = jnp.where(low, first, pltpu.roll(second, 4, 1)).reshape(half * 8, CH).astype(bf16)
        copy_h(0).start()
        first, second = dup[3 : 3 + half, 0:8, :], dup[3 + half : 3 + LAT_ROWS, 0:8, :]
        hs[1] = jnp.where(low, pltpu.roll(second, 4, 1), first).reshape(half * 8, CH).astype(bf16)
        copy_h(1).start()

        load(4).wait()
        load(5).wait()

        def middle_parts(i):
            return [(t, i * half, half) for t in range(1, TC - 1)]

        def middle_grads(i, carry):
            dps[i], norms[i], rstds[i] = mlp_grads(middle_parts(i))
            return carry

        def middle_du(i, carry):
            mlp_du(middle_parts(i), dps[i], norms[i], rstds[i])
            return carry

        lax.fori_loop(0, 2, middle_grads, 0)

        def copy_w1(b_to, b_from):
            return pltpu.make_async_remote_copy(
                src_ref=ws.at[b_to], dst_ref=wr.at[b_from], send_sem=w1_send.at[0], recv_sem=w1_recv.at[0],
                device_id=b_peer(b_to), device_id_type=MESH,
            )

        def copy_w2(a_to, a_from):
            return pltpu.make_async_remote_copy(
                src_ref=w2.at[a_me], dst_ref=w2.at[a_from], send_sem=w2_send.at[0], recv_sem=w2_recv.at[0],
                device_id=a_peer(a_to), device_id_type=MESH,
            )

        def copy_w3(b_to, b_from):
            return pltpu.make_async_remote_copy(
                src_ref=wf.at[b_me], dst_ref=wf.at[b_from], send_sem=w3_send.at[0], recv_sem=w3_recv.at[0],
                device_id=b_peer(b_to), device_id_type=MESH,
            )

        def copy_s1(b_to, b_from):
            return pltpu.make_async_remote_copy(
                src_ref=s1.at[b_me], dst_ref=s1.at[b_from], send_sem=s1_send.at[0], recv_sem=s1_recv.at[0],
                device_id=b_peer(b_to), device_id_type=MESH,
            )

        def copy_s2(a_to, a_from):
            return pltpu.make_async_remote_copy(
                src_ref=s2.at[a_me], dst_ref=s2.at[a_from], send_sem=s2_send.at[0], recv_sem=s2_recv.at[0],
                device_id=a_peer(a_to), device_id_type=MESH,
            )

        ends = {
            copy_w1: (wr, w1_send, w1_recv), copy_w2: (w2, w2_send, w2_recv), copy_w3: (wf, w3_send, w3_recv),
            copy_s1: (s1, s1_send, s1_recv), copy_s2: (s2, s2_send, s2_recv),
        }

        def over(copy, act, me, size):
            if act == "send":

                def body(d, carry):
                    copy(lax.rem(me + d, size), me).start()
                    return carry

                lax.fori_loop(1, size, body, 0)
            else:
                buf, sent, received = ends[copy]
                others = buf.at[pl.ds(0, size - 1)]
                sem = received if act == "recv" else sent
                pltpu.make_async_copy(others, others, sem.at[0]).wait()

        def over_a(copy, act):
            over(copy, act, a_me, na)

        def over_b(copy, act):
            over(copy, act, b_me, nb)

        ws[...] = gw[...].astype(bf16).reshape(nb, wrows, HID)
        over_b(copy_w1, "send")
        lax.fori_loop(0, 2, middle_du, 0)

        copy_h(0).wait_recv()
        copy_h(1).wait_recv()
        near = hr[0].astype(f32).reshape(half, 8, CH)
        dup[3 : 3 + half, 0:8, :] = jnp.where(low, near, dup[3 : 3 + half, 0:8, :])
        dup[3 + half : 3 + LAT_ROWS, 0:8, :] = jnp.where(
            low, pltpu.roll(near, 4, 1), dup[3 + half : 3 + LAT_ROWS, 0:8, :]
        )
        near = hr[1].astype(f32).reshape(half, 8, CH)
        dup[3 : 3 + half, 56:64, :] = jnp.where(low, dup[3 : 3 + half, 56:64, :], near)
        dup[3 + half : 3 + LAT_ROWS, 56:64, :] = jnp.where(
            low, dup[3 + half : 3 + LAT_ROWS, 56:64, :], pltpu.roll(near, 4, 1)
        )
        vs[0] = dup[LAT_ROWS : LAT_ROWS + 3].reshape(192, CH).astype(bf16)
        vs[1] = dup[3:6].reshape(192, CH).astype(bf16)
        copy_v(0).start()
        copy_v(1).start()

        for i in range(7, len(consts)):
            load_const(i).wait()
        load(6).wait()
        kpad[0:TAPS] = ker[...]
        kh[...] = dot_exact(high_ref[0:FREQ, 0:56], kpad[...])

        def tile_pair(slot, i0, i1, t):
            def window(i):
                return dup[pl.ds(i * OUT, N), 8 * t : 8 * t + 16, :].reshape(N * 16, CH).astype(bf16)

            def field(i):
                tile = fv[pl.ds(i * OUT, OUT), 8 * t : 8 * t + 8, :].astype(f32)
                tile = [tile[r] * cos_ref[lat * LAT_ROWS + i * OUT + r] for r in range(OUT)]
                return jnp.concatenate(tile, 0).astype(bf16)

            shape = (PAIRS // 8, 2, 8, 2 * CH)
            w = dot(low_ref[0:FREQ, 0 : N * 16], jnp.concatenate([window(i0), window(i1)], 1)).reshape(shape)
            g = dot(low_ref[0:FREQ, 256 : 256 + OUT * OUT], jnp.concatenate([field(i0), field(i1)], 1)).reshape(shape)
            k = kh[...].reshape(PAIRS // 8, 2, 8, CH)
            k = jnp.concatenate([k, k], -1)
            w_re, w_im, g_re, g_im, k_re, k_im = w[:, 0], w[:, 1], g[:, 0], g[:, 1], k[:, 0], k[:, 1]
            y = jnp.stack([k_re * w_re - k_im * w_im, k_re * w_im + k_im * w_re], 1)
            yb[slot] = y.reshape(FREQ, 2 * CH).astype(bf16)
            d = jnp.stack([g_re * w_re + g_im * w_im, g_im * w_re - g_re * w_im], 1).reshape(FREQ, 2 * CH)
            acc[...] += d[:, :CH] + d[:, CH:]

        pairs = TL // 2

        def middle(j, carry):
            for t in range(1, TC - 1):
                tile_pair(t * pairs + j, 1 + 2 * j, 2 + 2 * j, t)
            return carry

        def sides(j, carry):
            for t in (0, TC - 1):
                tile_pair(t * pairs + j, 1 + 2 * j, 2 + 2 * j, t)
            return carry

        lax.fori_loop(0, pairs - 1, middle, 0)
        lax.fori_loop(0, pairs - 1, sides, 0)

        copy_v(0).wait_recv()
        copy_v(1).wait_recv()
        zero = jnp.zeros((3, 64, CH), f32)
        dup[0:3] = jnp.where(lat > 0, vr[0].astype(f32).reshape(3, 64, CH), zero)
        dup[LAT_ROWS + 3 : LAT_ROWS + 6] = jnp.where(lat < nlat - 1, vr[1].astype(f32).reshape(3, 64, CH), zero)
        for t in range(TC):
            tile_pair(t * pairs + pairs - 1, 0, TL - 1, t)

        sm32[...] = jnp.zeros_like(sm32)
        sm32[0:56] = dot_exact(high_ref[FREQ : FREQ + 56, :], acc[...])
        total = jnp.sum(gbin[...], 0, keepdims=True)
        for q in range(4):
            sm32[49 + q : 50 + q] = total[:, q * CH : (q + 1) * CH]
            sm32[53 + q : 54 + q] = jnp.sum(small[q], 0, keepdims=True)
        s1[b_me] = sm32[...].astype(bf16)
        over_b(copy_s1, "send")

        wr[b_me] = ws[b_me]
        over_b(copy_w1, "recv")
        w2[a_me] = jnp.sum(wr[...].astype(f32), 0).astype(bf16)
        over_a(copy_w2, "send")

        def store(j):
            n = OUT if j >= pairs - 1 else 2 * OUT
            at = (0, LAT_ROWS - OUT)[j - pairs + 1] if j >= pairs - 1 else (1 + 2 * j) * OUT
            return pltpu.make_async_copy(outv.at[pl.ds(at, n)], out_hbm.at[pl.ds(at, n)], out_sem.at[j])

        def finish(j, ends):
            for t in range(TC):
                conv = dot(low_ref[FREQ:, 0:FREQ], yb[t * pairs + j]).reshape(OUT, OUT, 2 * CH)
                for n, i in enumerate(ends):
                    cot = cv[i * OUT : (i + 1) * OUT, 8 * t : 8 * t + 8, :].astype(f32)
                    part = conv[:, :, n * CH : (n + 1) * CH]
                    value = [cot[r] + part[r] * cos_ref[lat * LAT_ROWS + i * OUT + r] for r in range(OUT)]
                    outv[i * OUT : (i + 1) * OUT, 8 * t : 8 * t + 8, :] = jnp.stack(value, 0).astype(bf16)

        for j in range(pairs - 1):
            finish(j, (1 + 2 * j, 2 + 2 * j))
            store(j).start()
        finish(pairs - 1, (0, TL - 1))
        store(pairs - 1).start()
        store(pairs).start()
        for side in range(2):
            copy_h(side).wait_send()
            copy_v(side).wait_send()
        over_b(copy_w1, "done")
        over_b(copy_s1, "done")
        over_a(copy_w2, "done")
        over_a(copy_w2, "recv")
        wf[b_me] = jnp.sum(w2[...].astype(f32), 0).astype(bf16)
        over_b(copy_w3, "send")
        over_b(copy_s1, "recv")
        s2[a_me] = jnp.sum(s1[...].astype(f32), 0).astype(bf16)
        over_a(copy_s2, "send")

        for j in range(pairs + 1):
            store(j).wait()
        over_b(copy_w3, "done")
        over_b(copy_w3, "recv")
        d_win = jnp.concatenate([wf[b].astype(f32) for b in range(nb // 2)], 0) * factor
        dwin_ref[...] = d_win
        give(0).start()
        g_out = jnp.concatenate([wf[b].astype(f32) for b in range(nb // 2, nb)], 0) * factor
        g_out = g_out.T
        d_wout = g_out * scale
        dwout_ref[...] = d_wout
        give(1).start()
        squares = jnp.sum(d_win * d_win, 0, keepdims=True)
        squares = sum(squares[:, q * CH : (q + 1) * CH] for q in range(4))
        squares = squares + jnp.sum(d_wout * d_wout, 0, keepdims=True)
        g_ls = jnp.sum(g_out * wout_ref[...].astype(f32), 0, keepdims=True)
        over_a(copy_s2, "recv")
        sm32[...] = jnp.sum(s2[...].astype(f32), 0) * factor
        dk = sm32[0:TAPS]
        d_bin = jnp.concatenate([sm32[49 + q : 50 + q] for q in range(4)], 1)
        d_gain, d_bias, d_cb, s_cot = (sm32[53 + q : 54 + q] for q in range(4))
        d_bout = s_cot * scale
        d_ls = g_ls + bout_ref[...] * s_cot
        rest_ref[...] = sm32[...]
        rest_ref[56:57] = d_bout
        rest_ref[57:58] = d_ls
        squares = squares + jnp.sum(dk * dk, 0, keepdims=True)
        for q in range(4):
            squares = squares + d_bin[:, q * CH : (q + 1) * CH] * d_bin[:, q * CH : (q + 1) * CH]
        for part in (d_gain, d_bias, d_cb, d_bout, d_ls):
            squares = squares + part * part
        rest_ref[58:59] = jnp.broadcast_to(jnp.sqrt(jnp.sum(squares, 1, keepdims=True)), (1, CH))
        give(2).start()

        over_a(copy_s2, "done")
        for i in range(len(results)):
            give(i).wait()

    hbm, smem = pl.BlockSpec(memory_space=pl.ANY), pl.BlockSpec(memory_space=pltpu.SMEM)
    shape = jax.ShapeDtypeStruct
    dma = pltpu.SemaphoreType.DMA
    field = (LAT_ROWS, COLS, CH)
    return pl.pallas_call(
        kernel,
        in_specs=[hbm] * 11 + [smem] + [hbm] * 2,
        out_specs=[hbm] * 4,
        out_shape=HANDED,
        scratch_shapes=[pltpu.VMEM(r.shape, r.dtype) for r in HANDED[1:]]
        + [
            pltpu.VMEM((1, CH), f32),
            pltpu.VMEM((1, CH), f32),
            pltpu.VMEM((CH, HID), bf16),
            pltpu.VMEM((1, HID), f32),
            pltpu.VMEM((HID, CH), bf16),
            pltpu.VMEM((1, CH), f32),
            pltpu.VMEM((1, CH), f32),
            pltpu.VMEM((2, LAT_ROWS // 2 * (COLS - 16), HID), bf16),
            pltpu.VMEM((2, LAT_ROWS // 2 * (COLS - 16), CH), f32),
            pltpu.VMEM((2, LAT_ROWS // 2 * (COLS - 16), CH), f32),
            pltpu.VMEM(field, bf16),
            pltpu.VMEM(field, bf16),
            pltpu.VMEM(field, bf16),
            pltpu.VMEM(field, bf16),
            pltpu.VMEM((LAT_ROWS + 6, COLS + 8, CH), f32),
            pltpu.VMEM((TL * TC // 2, FREQ, 2 * CH), bf16),
            pltpu.VMEM((FREQ + OUT * OUT, 384), bf16),
            pltpu.VMEM((FREQ + 56, FREQ), f32),
            pltpu.VMEM((TAPS, CH), f32),
            pltpu.VMEM((56, CH), f32),
            pltpu.VMEM((FREQ, CH), f32),
            pltpu.VMEM((FREQ, CH), f32),
            pltpu.VMEM((2 * CH, HID), f32),
            pltpu.VMEM((8, HID), f32),
            pltpu.VMEM((4, 8, CH), f32),
            pltpu.VMEM((SMALL, CH), f32),
            pltpu.VMEM((2, LAT_ROWS * 4, CH), bf16),
            pltpu.VMEM((2, LAT_ROWS * 4, CH), bf16),
            pltpu.VMEM((2, 192, CH), bf16),
            pltpu.VMEM((2, 192, CH), bf16),
            pltpu.VMEM((nb, wrows, HID), bf16),
            pltpu.VMEM((nb, wrows, HID), bf16),
            pltpu.VMEM((na, wrows, HID), bf16),
            pltpu.VMEM((nb, wrows, HID), bf16),
            pltpu.VMEM((nb, SMALL, CH), bf16),
            pltpu.VMEM((na, SMALL, CH), bf16),
            dma((7,)),
            dma((10,)),
            dma((3,)),
            dma((TC,)),
            dma((2,)),
            dma((2,)),
            dma((2,)),
            dma((2,)),
        ]
        + [dma((1,)) for _ in range(10)],
        compiler_params=pltpu.CompilerParams(
            collective_id=0, has_side_effects=True, vmem_limit_bytes=60 * 2**20
        ),
        cost_estimate=pl.CostEstimate(flops=6 * 10**9, bytes_accessed=6 * 10**6, transcendentals=3 * 10**6),
        name="block_backward",
    )


RESULTS = [
    jax.ShapeDtypeStruct(s, t)
    for s, t in (
        ((LAT_ROWS, COLS, CH), bf16),
        ((TAPS, CH), f32),
        ((1, CH), f32),
        ((1, CH), f32),
        ((1, CH), f32),
        ((CH, HID), f32),
        ((1, HID), f32),
        ((HID, CH), f32),
        ((1, CH), f32),
        ((1, CH), f32),
        ((1, 1), f32),
    )
]
HANDED = [RESULTS[0], RESULTS[5], RESULTS[7], jax.ShapeDtypeStruct((SMALL, CH), f32)]
ROWS = ((2, 55), (3, 53), (4, 54), (8, 56), (9, 57))
BANDS = 4


def hand_on(*refs):
    n, m = len(RESULTS), len(HANDED)
    src, dst = refs[:m], refs[m : m + n]
    stage, lines, sem_in, sem_out = refs[m + n : 2 * m + n], refs[2 * m + n : -2], refs[-2], refs[-1]
    rows = LAT_ROWS // BANDS
    hops = []
    for i, to in enumerate((0, 5, 7)):
        for j in range(BANDS if i == 0 else 1):
            part = pl.ds(j * rows, rows) if i == 0 else slice(None)
            slot = n + j if i == 0 else to
            hops.append((
                pltpu.make_async_copy(src[i].at[part], stage[i].at[part], sem_in.at[slot]),
                pltpu.make_async_copy(stage[i].at[part], dst[to].at[part], sem_out.at[slot]),
            ))
    block_in = pltpu.make_async_copy(src[3], stage[3], sem_in.at[0])
    block_in.start()
    for first, _ in hops:
        first.start()
    block_in.wait()
    block = stage[3]
    lines[0][...] = block[0:TAPS]
    lines[1][...] = jnp.concatenate([block[49 + q : 50 + q] for q in range(4)], 1)
    lines[2][...] = block[58:59, 0:1]
    for line, (_, row) in zip(lines[3:], ROWS):
        line[...] = block[row : row + 1]
    outs = [second for _, second in hops]
    small = [
        pltpu.make_async_copy(line, dst[to], sem_out.at[to])
        for line, to in zip(lines, (1, 6, 10) + tuple(to for to, _ in ROWS))
    ]
    for copy in small:
        copy.start()
    for first, second in hops:
        first.wait()
        second.start()
    for copy in small + outs:
        copy.wait()


def make_hand_on():
    n = len(RESULTS)
    hbm = pl.BlockSpec(memory_space=pltpu.HBM)
    dma = pltpu.SemaphoreType.DMA((n + BANDS,))
    order = (1, 6, 10) + tuple(to for to, _ in ROWS)
    return pl.pallas_call(
        hand_on,
        in_specs=[hbm] * len(HANDED),
        out_specs=[hbm] * n,
        out_shape=RESULTS,
        scratch_shapes=[pltpu.VMEM(r.shape, r.dtype) for r in HANDED + [RESULTS[i] for i in order]] + [dma, dma],
        name="hand_on",
    )


def solution(mesh):
    nlon, nlat = mesh.shape["lon"], mesh.shape["lat"]
    nz, nx, nyh = (4, 4, 2) if nlon == 32 else (nlon, 1, 1)
    nyl, ncore = nlat // 2, 2
    total_rows, total_cols = LAT_ROWS * nlat, COLS * nlon
    call = make_kernel(nz, nx, nyh, nyl, ncore, total_rows * total_cols)
    finish = make_hand_on()
    low, high = tables()
    place = (np.arange(total_rows, dtype=np.float32) + np.float32(0.5)) / np.float32(total_rows) - np.float32(0.5)
    weight = np.cos(np.float32(math.pi) * place).astype(np.float32)

    def on_device(field_in, conv_out, cotangent, kernel, ln_gain, ln_bias, w_in, b_in, w_out, b_out, layer_scale):
        line = lambda v: v.reshape(1, -1)
        outs = call(
            conv_out, cotangent, field_in, kernel, line(ln_gain), line(ln_bias), w_in, line(b_in),
            w_out, line(b_out), line(layer_scale), weight, low, high,
        )
        d_field, d_kernel, d_cb, d_gain, d_bias, d_win, d_bin, d_wout, d_bout, d_ls, norm = finish(*outs)
        wide = lambda v: v.reshape(-1)
        return (
            d_field, d_kernel, wide(d_cb), wide(d_gain), wide(d_bias), d_win, wide(d_bin),
            d_wout, wide(d_bout), wide(d_ls), norm.reshape(()),
        )

    grid = P("lat", "lon", None)
    return jax.shard_map(
        on_device,
        mesh=mesh,
        in_specs=(grid, grid, grid) + (P(),) * 8,
        out_specs=(grid,) + (P(),) * 10,
        check_vma=False,
    )
```

```python
import math

import jax
import jax.numpy as jnp
import ml_dtypes
import numpy as np
from jax import lax
from jax.experimental import pallas as pl
from jax.experimental.pallas import tpu as pltpu
from jax.sharding import PartitionSpec as P

MESH = pl.DeviceIdType.MESH
f32, bf16 = jnp.float32, jnp.bfloat16
EPS = 1e-06
COEF = 0.044715
ROOT = math.sqrt(2.0 / math.pi)

N = 14
OUT = 8
PAIRS = 104
FREQ = 2 * PAIRS
SCALE = 1.828125
LAT_ROWS, COLS, CH, HID, TAPS = 96, 56, 128, 512, 49
TL, TC = LAT_ROWS // OUT, COLS // OUT
SMALL = 64
RIM = ((0, 0, LAT_ROWS), (TC - 1, 0, LAT_ROWS))


def tables():
    own = [(0, 0), (0, 7), (7, 0), (7, 7)]
    seen, pairs = set(own), []
    for k in range(N):
        for l in range(N):
            if (k, l) not in seen:
                seen.add((k, l))
                seen.add(((-k) % N, (-l) % N))
                pairs.append((k, l))
    freq = np.array(own + pairs)
    weight = np.array([1.0] * 4 + [2.0] * 96)[:, None] / (N * N)
    twin = np.array([0.0] * 4 + [1.0] * 96)[:, None]

    def angle(rows, cols, row_off, col_off):
        m, n = np.meshgrid(np.arange(rows) + row_off, np.arange(cols) + col_off, indexing="ij")
        m, n = m.ravel(), n.ravel()
        return 2 * np.pi * ((np.outer(freq[:, 0], m) + np.outer(freq[:, 1], n)) % N) / N

    def interleave(re, im):
        fill = np.zeros((PAIRS - 100, re.shape[1]))
        re, im = np.concatenate([re, fill]), np.concatenate([im, fill])
        shape = (PAIRS // 8, 8, re.shape[1])
        return np.stack([re.reshape(shape), im.reshape(shape)], 1).reshape(FREQ, -1)

    inside = np.tile(np.array([0.0] + [1.0] * 14 + [0.0]), N)
    a = angle(N, 16, 0, -1)
    fwd = interleave(np.cos(a) * inside, -np.sin(a) * inside * twin)
    a = angle(OUT, OUT, 6, 6)
    fwd_tile = interleave(np.cos(a), -np.sin(a) * twin)
    inv = interleave(np.cos(a) * weight, -np.sin(a) * weight * twin).T
    a = angle(7, 7, 0, 0)
    taps = interleave(np.cos(a), -np.sin(a) * twin)
    taps_inv = interleave(np.cos(a) * weight, -np.sin(a) * weight * twin).T
    area = N * N
    low = np.zeros((FREQ + OUT * OUT, 384))
    low[:FREQ, : N * 16] = fwd * SCALE
    low[:FREQ, 256 : 256 + OUT * OUT] = fwd_tile * SCALE
    low[FREQ:, :FREQ] = inv * area * SCALE
    high = np.zeros((FREQ + 56, FREQ))
    high[:FREQ, :TAPS] = taps / (area * SCALE * SCALE)
    high[FREQ : FREQ + TAPS] = taps_inv / (SCALE * SCALE)
    return low.astype(ml_dtypes.bfloat16), high.astype(np.float32)


def dot(a, b):
    return jnp.dot(a, b, preferred_element_type=f32)


def dot_exact(a, b):
    return jnp.dot(a, b, preferred_element_type=f32, precision=lax.Precision.HIGHEST)


def dot_last(a, b):
    return lax.dot_general(a, b, (((1,), (1,)), ((), ())), preferred_element_type=f32)


def dot_rows(a, b):
    return lax.dot_general(a, b, (((0,), (0,)), ((), ())), preferred_element_type=f32)


def rows8(v):
    return jnp.sum(v.reshape(v.shape[0] // 8, 8, v.shape[1]), 0)


def make_kernel(nz, nx, nyh, nyl, ncore, total_cells):
    nlon, nlat = nz * nx * nyh, nyl * ncore
    ny = nyh * nyl
    nb, na = nz * ny, nx * ncore
    wrows = 2 * CH // nb
    factor = float(total_cells) ** (-0.5)

    def kernel(
        x_hbm, c_hbm, f_hbm, ker_hbm, gain_hbm, bias_hbm, win_hbm, bin_hbm, wout_hbm, bout_hbm, ls_hbm,
        cos_ref, low_hbm, high_hbm,
        out_hbm, dwin_hbm, dwout_hbm, rest_hbm,
        dwin_ref, dwout_ref, rest_ref,
        gain_ref, bias_ref, win_ref, bin_ref, wout_ref, bout_ref, ls_ref, dps, norms, rstds,
        xv, cv, fv, outv, dup, yb, low_ref, high_ref, ker, kpad, kh, acc, gw, gbin, small, sm32,
        hs, hr, vs, vr, ws, wr, w2, wf, s1, s2,
        in_sem, const_sem, res_sem, out_sem, h_send, h_recv, v_send, v_recv,
        w1_send, w1_recv, w2_send, w2_recv, w3_send, w3_recv, s1_send, s1_recv, s2_send, s2_recv,
    ):
        lon, lat = lax.axis_index("lon"), lax.axis_index("lat")
        z, x, yh = lax.div(lon, nx * nyh), lax.rem(lax.div(lon, nyh), nx), lax.rem(lon, nyh)
        yl, core = lax.div(lat, ncore), lax.rem(lat, ncore)
        b_me = z * ny + yh * nyl + yl
        a_me = x * ncore + core

        def b_peer(b):
            bz, by = lax.div(b, ny), lax.rem(b, ny)
            return (bz * (nx * nyh) + x * nyh + lax.div(by, nyl), lax.rem(by, nyl) * ncore + core)

        def a_peer(a):
            return (z * (nx * nyh) + lax.div(a, ncore) * nyh + yh, yl * ncore + lax.rem(a, ncore))

        right, left = lax.rem(lon + 1, nlon), lax.rem(lon + nlon - 1, nlon)
        down, up = lax.rem(lat + 1, nlat), lax.rem(lat + nlat - 1, nlat)

        sides_x, middle_x = (pl.ds(0, 8), pl.ds(COLS - 8, 8)), pl.ds(8, COLS - 16)
        loads = [(x_hbm, xv, sides_x[0]), (c_hbm, cv, sides_x[0]), (x_hbm, xv, sides_x[1]), (c_hbm, cv, sides_x[1])]
        loads += [(x_hbm, xv, middle_x), (c_hbm, cv, middle_x), (f_hbm, fv, pl.ds(0, COLS))]

        def load(i):
            src, dst, cols = loads[i]
            return pltpu.make_async_copy(src.at[:, cols, :], dst.at[:, cols, :], in_sem.at[i])

        consts = (
            (gain_hbm, gain_ref), (bias_hbm, bias_ref), (win_hbm, win_ref), (bin_hbm, bin_ref), (wout_hbm, wout_ref),
            (ls_hbm, ls_ref), (bout_hbm, bout_ref),
            (low_hbm, low_ref), (high_hbm, high_ref), (ker_hbm, ker),
        )
        results = ((dwin_ref, dwin_hbm), (dwout_ref, dwout_hbm), (rest_ref, rest_hbm))

        def give(i):
            return pltpu.make_async_copy(*results[i], res_sem.at[i])

        def load_const(i):
            return pltpu.make_async_copy(*consts[i], const_sem.at[i])

        for i in range(4):
            load(i).start()
        for i in range(7):
            load_const(i).start()
        for i in range(4, len(loads)):
            load(i).start()
        for i in range(7, len(consts)):
            load_const(i).start()

        barrier = pltpu.get_barrier_semaphore()
        for peer in ((right, lat), (left, lat), (lon, down), (lon, up)):
            pl.semaphore_signal(barrier, inc=1, device_id=peer, device_id_type=MESH)

        def greet_b(d, carry):
            pl.semaphore_signal(barrier, inc=1, device_id=b_peer(lax.rem(b_me + d, nb)), device_id_type=MESH)
            return carry

        def greet_a(d, carry):
            pl.semaphore_signal(barrier, inc=1, device_id=a_peer(lax.rem(a_me + d, na)), device_id_type=MESH)
            return carry

        lax.fori_loop(1, nb, greet_b, 0)
        lax.fori_loop(1, na, greet_a, 0)

        third = jnp.full((CH, CH), 1.0 / CH, bf16)
        none = jnp.zeros((CH, CH), bf16)
        mean_two = jnp.concatenate(
            [jnp.concatenate([third, none], 1), jnp.concatenate([none, third], 1)], 0
        )
        acc[...] = jnp.zeros_like(acc)
        kpad[...] = jnp.zeros_like(kpad)

        for i in range(7):
            load_const(i).wait()
        gain, bias, scale = gain_ref[...], bias_ref[...], ls_ref[...]
        win_half, bin_half = win_ref[...] * jnp.asarray(0.5, bf16), bin_ref[...] * 0.5
        wout_half = wout_ref[...] * jnp.asarray(0.5, bf16)

        def cells_of(ref, parts):
            return jnp.concatenate([ref[pl.ds(r0, n), 8 * t : 8 * t + 8, :].astype(f32).reshape(n * 8, CH) for t, r0, n in parts], 0)

        def add(ref, at, value, first):
            ref[at] = value if first else ref[at] + value

        def mlp_grads(parts, first=False):
            value = cells_of(xv, parts)
            center = value - dot(value.astype(bf16), third)
            rstd = lax.rsqrt(dot((center * center).astype(bf16), third) + EPS)
            normed = center * rstd
            zed = (normed * gain + bias).astype(bf16)
            cot = cells_of(cv, parts)
            cb = cot.astype(bf16)
            d_out = (cot * scale).astype(bf16)
            acts, dpres = [], []
            g_bin = jnp.zeros((8, HID), f32)
            sub = value.shape[0] // 2
            for s in range(0, value.shape[0], sub):
                h = dot(zed[s : s + sub], win_half) + bin_half
                d_act = dot_last(d_out[s : s + sub], wout_half)
                h2 = h * h
                tangent = jnp.tanh(h * (2 * ROOT + (8 * ROOT * COEF) * h2))
                wide = h * (2 * ROOT + (24 * ROOT * COEF) * h2)
                above = 1.0 + tangent
                d_pre = d_act * (above * (1.0 + (1.0 - tangent) * wide))
                g_bin = g_bin + rows8(d_pre)
                acts.append((h * above).astype(bf16))
                dpres.append(d_pre.astype(bf16))
            act, d_pre = jnp.concatenate(acts, 0), jnp.concatenate(dpres, 0)
            add(gbin, ..., g_bin, first)
            add(gw, slice(CH, 2 * CH), dot_rows(cb, act), first)
            add(gw, slice(0, CH), dot_rows(zed, d_pre), first)
            add(small, 3, rows8(cot), first)
            return d_pre, normed, rstd

        def mlp_du(parts, d_pre, normed, rstd, first=False):
            d_zed = dot_last(d_pre, win_ref[...])
            d_gain = d_zed * normed
            d_norm = d_zed * gain
            means = dot(
                jnp.concatenate([d_norm.astype(bf16), (d_gain * gain).astype(bf16)], 1), mean_two
            )
            du = rstd * (d_norm - means[:, :CH] - normed * means[:, CH:])
            at = 0
            for t, r0, n in parts:
                dup[pl.ds(3 + r0, n), 4 + 8 * t : 12 + 8 * t, :] = du[at : at + 8 * n].reshape(n, 8, CH)
                at += 8 * n
            for q, value in enumerate((d_gain, d_zed, du)):
                add(small, q, rows8(value), first)

        for i in range(4):
            load(i).wait()
        mlp_du(RIM, *mlp_grads(RIM, True), first=True)

        half = LAT_ROWS // 2
        low = lax.broadcasted_iota(jnp.int32, (half, 8, CH), 1) < 4

        def copy_h(side):
            return pltpu.make_async_remote_copy(
                src_ref=hs.at[side], dst_ref=hr.at[side], send_sem=h_send.at[side], recv_sem=h_recv.at[side],
                device_id=((right, lat), (left, lat))[side], device_id_type=MESH,
            )

        def copy_v(side):
            return pltpu.make_async_remote_copy(
                src_ref=vs.at[side], dst_ref=vr.at[side], send_sem=v_send.at[side], recv_sem=v_recv.at[side],
                device_id=((lon, down), (lon, up))[side], device_id_type=MESH,
            )

        pl.semaphore_wait(barrier, 4 + (nb - 1) + (na - 1))
        first, second = dup[3 : 3 + half, 56:64, :], dup[3 + half : 3 + LAT_ROWS, 56:64, :]
        hs[0] = jnp.where(low, first, pltpu.roll(second, 4, 1)).reshape(half * 8, CH).astype(bf16)
        copy_h(0).start()
        first, second = dup[3 : 3 + half, 0:8, :], dup[3 + half : 3 + LAT_ROWS, 0:8, :]
        hs[1] = jnp.where(low, pltpu.roll(second, 4, 1), first).reshape(half * 8, CH).astype(bf16)
        copy_h(1).start()

        load(4).wait()
        load(5).wait()

        def middle_parts(i):
            return [(t, i * half, half) for t in range(1, TC - 1)]

        def middle_grads(i, carry):
            dps[i], norms[i], rstds[i] = mlp_grads(middle_parts(i))
            return carry

        def middle_du(i, carry):
            mlp_du(middle_parts(i), dps[i], norms[i], rstds[i])
            return carry

        lax.fori_loop(0, 2, middle_grads, 0)

        def copy_w1(b_to, b_from):
            return pltpu.make_async_remote_copy(
                src_ref=ws.at[b_to], dst_ref=wr.at[b_from], send_sem=w1_send.at[0], recv_sem=w1_recv.at[0],
                device_id=b_peer(b_to), device_id_type=MESH,
            )

        def copy_w2(a_to, a_from):
            return pltpu.make_async_remote_copy(
                src_ref=w2.at[a_me], dst_ref=w2.at[a_from], send_sem=w2_send.at[0], recv_sem=w2_recv.at[0],
                device_id=a_peer(a_to), device_id_type=MESH,
            )

        def copy_w3(b_to, b_from):
            return pltpu.make_async_remote_copy(
                src_ref=wf.at[b_me], dst_ref=wf.at[b_from], send_sem=w3_send.at[0], recv_sem=w3_recv.at[0],
                device_id=b_peer(b_to), device_id_type=MESH,
            )

        def copy_s1(b_to, b_from):
            return pltpu.make_async_remote_copy(
                src_ref=s1.at[b_me], dst_ref=s1.at[b_from], send_sem=s1_send.at[0], recv_sem=s1_recv.at[0],
                device_id=b_peer(b_to), device_id_type=MESH,
            )

        def copy_s2(a_to, a_from):
            return pltpu.make_async_remote_copy(
                src_ref=s2.at[a_me], dst_ref=s2.at[a_from], send_sem=s2_send.at[0], recv_sem=s2_recv.at[0],
                device_id=a_peer(a_to), device_id_type=MESH,
            )

        ends = {
            copy_w1: (wr, w1_send, w1_recv), copy_w2: (w2, w2_send, w2_recv), copy_w3: (wf, w3_send, w3_recv),
            copy_s1: (s1, s1_send, s1_recv), copy_s2: (s2, s2_send, s2_recv),
        }

        def over(copy, act, me, size):
            if act == "send":

                def body(d, carry):
                    copy(lax.rem(me + d, size), me).start()
                    return carry

                lax.fori_loop(1, size, body, 0)
            else:
                buf, sent, received = ends[copy]
                others = buf.at[pl.ds(0, size - 1)]
                sem = received if act == "recv" else sent
                pltpu.make_async_copy(others, others, sem.at[0]).wait()

        def over_a(copy, act):
            over(copy, act, a_me, na)

        def over_b(copy, act):
            over(copy, act, b_me, nb)

        ws[...] = gw[...].astype(bf16).reshape(nb, wrows, HID)
        over_b(copy_w1, "send")
        lax.fori_loop(0, 2, middle_du, 0)

        copy_h(0).wait_recv()
        copy_h(1).wait_recv()
        near = hr[0].astype(f32).reshape(half, 8, CH)
        dup[3 : 3 + half, 0:8, :] = jnp.where(low, near, dup[3 : 3 + half, 0:8, :])
        dup[3 + half : 3 + LAT_ROWS, 0:8, :] = jnp.where(
            low, pltpu.roll(near, 4, 1), dup[3 + half : 3 + LAT_ROWS, 0:8, :]
        )
        near = hr[1].astype(f32).reshape(half, 8, CH)
        dup[3 : 3 + half, 56:64, :] = jnp.where(low, dup[3 : 3 + half, 56:64, :], near)
        dup[3 + half : 3 + LAT_ROWS, 56:64, :] = jnp.where(
            low, dup[3 + half : 3 + LAT_ROWS, 56:64, :], pltpu.roll(near, 4, 1)
        )
        vs[0] = dup[LAT_ROWS : LAT_ROWS + 3].reshape(192, CH).astype(bf16)
        vs[1] = dup[3:6].reshape(192, CH).astype(bf16)
        copy_v(0).start()
        copy_v(1).start()

        for i in range(7, len(consts)):
            load_const(i).wait()
        load(6).wait()
        kpad[0:TAPS] = ker[...]
        kh[...] = dot_exact(high_ref[0:FREQ, 0:56], kpad[...])

        def tile_pair(slot, i0, i1, t):
            def window(i):
                return dup[pl.ds(i * OUT, N), 8 * t : 8 * t + 16, :].reshape(N * 16, CH).astype(bf16)

            def field(i):
                tile = fv[pl.ds(i * OUT, OUT), 8 * t : 8 * t + 8, :].astype(f32)
                tile = [tile[r] * cos_ref[lat * LAT_ROWS + i * OUT + r] for r in range(OUT)]
                return jnp.concatenate(tile, 0).astype(bf16)

            shape = (PAIRS // 8, 2, 8, 2 * CH)
            w = dot(low_ref[0:FREQ, 0 : N * 16], jnp.concatenate([window(i0), window(i1)], 1)).reshape(shape)
            g = dot(low_ref[0:FREQ, 256 : 256 + OUT * OUT], jnp.concatenate([field(i0), field(i1)], 1)).reshape(shape)
            k = kh[...].reshape(PAIRS // 8, 2, 8, CH)
            k = jnp.concatenate([k, k], -1)
            w_re, w_im, g_re, g_im, k_re, k_im = w[:, 0], w[:, 1], g[:, 0], g[:, 1], k[:, 0], k[:, 1]
            y = jnp.stack([k_re * w_re - k_im * w_im, k_re * w_im + k_im * w_re], 1)
            yb[slot] = y.reshape(FREQ, 2 * CH).astype(bf16)
            d = jnp.stack([g_re * w_re + g_im * w_im, g_im * w_re - g_re * w_im], 1).reshape(FREQ, 2 * CH)
            acc[...] += d[:, :CH] + d[:, CH:]

        pairs = TL // 2

        def middle(j, carry):
            for t in range(1, TC - 1):
                tile_pair(t * pairs + j, 1 + 2 * j, 2 + 2 * j, t)
            return carry

        def sides(j, carry):
            for t in (0, TC - 1):
                tile_pair(t * pairs + j, 1 + 2 * j, 2 + 2 * j, t)
            return carry

        lax.fori_loop(0, pairs - 1, middle, 0)
        lax.fori_loop(0, pairs - 1, sides, 0)

        copy_v(0).wait_recv()
        copy_v(1).wait_recv()
        zero = jnp.zeros((3, 64, CH), f32)
        dup[0:3] = jnp.where(lat > 0, vr[0].astype(f32).reshape(3, 64, CH), zero)
        dup[LAT_ROWS + 3 : LAT_ROWS + 6] = jnp.where(lat < nlat - 1, vr[1].astype(f32).reshape(3, 64, CH), zero)
        for t in range(TC):
            tile_pair(t * pairs + pairs - 1, 0, TL - 1, t)

        sm32[...] = jnp.zeros_like(sm32)
        sm32[0:56] = dot_exact(high_ref[FREQ : FREQ + 56, :], acc[...])
        total = jnp.sum(gbin[...], 0, keepdims=True)
        for q in range(4):
            sm32[49 + q : 50 + q] = total[:, q * CH : (q + 1) * CH]
            sm32[53 + q : 54 + q] = jnp.sum(small[q], 0, keepdims=True)
        s1[b_me] = sm32[...].astype(bf16)
        over_b(copy_s1, "send")

        wr[b_me] = ws[b_me]
        over_b(copy_w1, "recv")
        w2[a_me] = jnp.sum(wr[...].astype(f32), 0).astype(bf16)
        over_a(copy_w2, "send")

        def store(j):
            n = OUT if j >= pairs - 1 else 2 * OUT
            at = (0, LAT_ROWS - OUT)[j - pairs + 1] if j >= pairs - 1 else (1 + 2 * j) * OUT
            return pltpu.make_async_copy(outv.at[pl.ds(at, n)], out_hbm.at[pl.ds(at, n)], out_sem.at[j])

        def finish(j, ends):
            for t in range(TC):
                conv = dot(low_ref[FREQ:, 0:FREQ], yb[t * pairs + j]).reshape(OUT, OUT, 2 * CH)
                for n, i in enumerate(ends):
                    cot = cv[i * OUT : (i + 1) * OUT, 8 * t : 8 * t + 8, :].astype(f32)
                    part = conv[:, :, n * CH : (n + 1) * CH]
                    value = [cot[r] + part[r] * cos_ref[lat * LAT_ROWS + i * OUT + r] for r in range(OUT)]
                    outv[i * OUT : (i + 1) * OUT, 8 * t : 8 * t + 8, :] = jnp.stack(value, 0).astype(bf16)

        for j in range(pairs - 1):
            finish(j, (1 + 2 * j, 2 + 2 * j))
            store(j).start()
        finish(pairs - 1, (0, TL - 1))
        store(pairs - 1).start()
        store(pairs).start()
        for side in range(2):
            copy_h(side).wait_send()
            copy_v(side).wait_send()
        over_b(copy_w1, "done")
        over_b(copy_s1, "done")
        over_a(copy_w2, "done")
        over_a(copy_w2, "recv")
        wf[b_me] = jnp.sum(w2[...].astype(f32), 0).astype(bf16)
        over_b(copy_w3, "send")
        over_b(copy_s1, "recv")
        s2[a_me] = jnp.sum(s1[...].astype(f32), 0).astype(bf16)
        over_a(copy_s2, "send")

        for j in range(pairs + 1):
            store(j).wait()
        over_b(copy_w3, "done")
        over_b(copy_w3, "recv")
        d_win = jnp.concatenate([wf[b].astype(f32) for b in range(nb // 2)], 0) * factor
        dwin_ref[...] = d_win
        give(0).start()
        g_out = jnp.concatenate([wf[b].astype(f32) for b in range(nb // 2, nb)], 0) * factor
        g_out = g_out.T
        d_wout = g_out * scale
        dwout_ref[...] = d_wout
        give(1).start()
        squares = jnp.sum(d_win * d_win, 0, keepdims=True)
        squares = sum(squares[:, q * CH : (q + 1) * CH] for q in range(4))
        squares = squares + jnp.sum(d_wout * d_wout, 0, keepdims=True)
        g_ls = jnp.sum(g_out * wout_ref[...].astype(f32), 0, keepdims=True)
        over_a(copy_s2, "recv")
        sm32[...] = jnp.sum(s2[...].astype(f32), 0) * factor
        dk = sm32[0:TAPS]
        d_bin = jnp.concatenate([sm32[49 + q : 50 + q] for q in range(4)], 1)
        d_gain, d_bias, d_cb, s_cot = (sm32[53 + q : 54 + q] for q in range(4))
        d_bout = s_cot * scale
        d_ls = g_ls + bout_ref[...] * s_cot
        rest_ref[...] = sm32[...]
        rest_ref[56:57] = d_bout
        rest_ref[57:58] = d_ls
        squares = squares + jnp.sum(dk * dk, 0, keepdims=True)
        for q in range(4):
            squares = squares + d_bin[:, q * CH : (q + 1) * CH] * d_bin[:, q * CH : (q + 1) * CH]
        for part in (d_gain, d_bias, d_cb, d_bout, d_ls):
            squares = squares + part * part
        rest_ref[58:59] = jnp.broadcast_to(jnp.sqrt(jnp.sum(squares, 1, keepdims=True)), (1, CH))
        give(2).start()

        over_a(copy_s2, "done")
        for i in range(len(results)):
            give(i).wait()

    hbm, smem = pl.BlockSpec(memory_space=pl.ANY), pl.BlockSpec(memory_space=pltpu.SMEM)
    shape = jax.ShapeDtypeStruct
    dma = pltpu.SemaphoreType.DMA
    field = (LAT_ROWS, COLS, CH)
    return pl.pallas_call(
        kernel,
        in_specs=[hbm] * 11 + [smem] + [hbm] * 2,
        out_specs=[hbm] * 4,
        out_shape=HANDED,
        scratch_shapes=[pltpu.VMEM(r.shape, r.dtype) for r in HANDED[1:]]
        + [
            pltpu.VMEM((1, CH), f32),
            pltpu.VMEM((1, CH), f32),
            pltpu.VMEM((CH, HID), bf16),
            pltpu.VMEM((1, HID), f32),
            pltpu.VMEM((HID, CH), bf16),
            pltpu.VMEM((1, CH), f32),
            pltpu.VMEM((1, CH), f32),
            pltpu.VMEM((2, LAT_ROWS // 2 * (COLS - 16), HID), bf16),
            pltpu.VMEM((2, LAT_ROWS // 2 * (COLS - 16), CH), f32),
            pltpu.VMEM((2, LAT_ROWS // 2 * (COLS - 16), CH), f32),
            pltpu.VMEM(field, bf16),
            pltpu.VMEM(field, bf16),
            pltpu.VMEM(field, bf16),
            pltpu.VMEM(field, bf16),
            pltpu.VMEM((LAT_ROWS + 6, COLS + 8, CH), f32),
            pltpu.VMEM((TL * TC // 2, FREQ, 2 * CH), bf16),
            pltpu.VMEM((FREQ + OUT * OUT, 384), bf16),
            pltpu.VMEM((FREQ + 56, FREQ), f32),
            pltpu.VMEM((TAPS, CH), f32),
            pltpu.VMEM((56, CH), f32),
            pltpu.VMEM((FREQ, CH), f32),
            pltpu.VMEM((FREQ, CH), f32),
            pltpu.VMEM((2 * CH, HID), f32),
            pltpu.VMEM((8, HID), f32),
            pltpu.VMEM((4, 8, CH), f32),
            pltpu.VMEM((SMALL, CH), f32),
            pltpu.VMEM((2, LAT_ROWS * 4, CH), bf16),
            pltpu.VMEM((2, LAT_ROWS * 4, CH), bf16),
            pltpu.VMEM((2, 192, CH), bf16),
            pltpu.VMEM((2, 192, CH), bf16),
            pltpu.VMEM((nb, wrows, HID), bf16),
            pltpu.VMEM((nb, wrows, HID), bf16),
            pltpu.VMEM((na, wrows, HID), bf16),
            pltpu.VMEM((nb, wrows, HID), bf16),
            pltpu.VMEM((nb, SMALL, CH), bf16),
            pltpu.VMEM((na, SMALL, CH), bf16),
            dma((7,)),
            dma((10,)),
            dma((3,)),
            dma((TC,)),
            dma((2,)),
            dma((2,)),
            dma((2,)),
            dma((2,)),
        ]
        + [dma((1,)) for _ in range(10)],
        compiler_params=pltpu.CompilerParams(
            collective_id=0, has_side_effects=True, vmem_limit_bytes=60 * 2**20
        ),
        cost_estimate=pl.CostEstimate(flops=6 * 10**9, bytes_accessed=6 * 10**6, transcendentals=3 * 10**6),
        name="block_backward",
    )


RESULTS = [
    jax.ShapeDtypeStruct(s, t)
    for s, t in (
        ((LAT_ROWS, COLS, CH), bf16),
        ((TAPS, CH), f32),
        ((1, CH), f32),
        ((1, CH), f32),
        ((1, CH), f32),
        ((CH, HID), f32),
        ((1, HID), f32),
        ((HID, CH), f32),
        ((1, CH), f32),
        ((1, CH), f32),
        ((1, 1), f32),
    )
]
HANDED = [RESULTS[0], RESULTS[5], RESULTS[7], jax.ShapeDtypeStruct((SMALL, CH), f32)]
ROWS = ((2, 55), (3, 53), (4, 54), (8, 56), (9, 57))
BANDS = 2


def hand_on(*refs):
    n, m = len(RESULTS), len(HANDED)
    src, dst = refs[:m], refs[m : m + n]
    stage, lines, sem_in, sem_out = refs[m + n : 2 * m + n], refs[2 * m + n : -2], refs[-2], refs[-1]
    rows = LAT_ROWS // BANDS
    hops = []
    for i, to in enumerate((0, 5, 7)):
        for j in range(BANDS if i == 0 else 1):
            part = pl.ds(j * rows, rows) if i == 0 else slice(None)
            slot = n + j if i == 0 else to
            hops.append((
                pltpu.make_async_copy(src[i].at[part], stage[i].at[part], sem_in.at[slot]),
                pltpu.make_async_copy(stage[i].at[part], dst[to].at[part], sem_out.at[slot]),
            ))
    block_in = pltpu.make_async_copy(src[3], stage[3], sem_in.at[0])
    block_in.start()
    for first, _ in hops:
        first.start()
    block_in.wait()
    block = stage[3]
    lines[0][...] = block[0:TAPS]
    lines[1][...] = jnp.concatenate([block[49 + q : 50 + q] for q in range(4)], 1)
    lines[2][...] = block[58:59, 0:1]
    for line, (_, row) in zip(lines[3:], ROWS):
        line[...] = block[row : row + 1]
    outs = [second for _, second in hops]
    small = [
        pltpu.make_async_copy(line, dst[to], sem_out.at[to])
        for line, to in zip(lines, (1, 6, 10) + tuple(to for to, _ in ROWS))
    ]
    for copy in small:
        copy.start()
    for first, second in hops:
        first.wait()
        second.start()
    for copy in small + outs:
        copy.wait()


def make_hand_on():
    n = len(RESULTS)
    hbm = pl.BlockSpec(memory_space=pltpu.HBM)
    dma = pltpu.SemaphoreType.DMA((n + BANDS,))
    order = (1, 6, 10) + tuple(to for to, _ in ROWS)
    return pl.pallas_call(
        hand_on,
        in_specs=[hbm] * len(HANDED),
        out_specs=[hbm] * n,
        out_shape=RESULTS,
        scratch_shapes=[pltpu.VMEM(r.shape, r.dtype) for r in HANDED + [RESULTS[i] for i in order]] + [dma, dma],
        name="hand_on",
    )


def solution(mesh):
    nlon, nlat = mesh.shape["lon"], mesh.shape["lat"]
    nz, nx, nyh = (4, 4, 2) if nlon == 32 else (nlon, 1, 1)
    nyl, ncore = nlat // 2, 2
    total_rows, total_cols = LAT_ROWS * nlat, COLS * nlon
    call = make_kernel(nz, nx, nyh, nyl, ncore, total_rows * total_cols)
    finish = make_hand_on()
    low, high = tables()
    place = (np.arange(total_rows, dtype=np.float32) + np.float32(0.5)) / np.float32(total_rows) - np.float32(0.5)
    weight = np.cos(np.float32(math.pi) * place).astype(np.float32)

    def on_device(field_in, conv_out, cotangent, kernel, ln_gain, ln_bias, w_in, b_in, w_out, b_out, layer_scale):
        line = lambda v: v.reshape(1, -1)
        outs = call(
            conv_out, cotangent, field_in, kernel, line(ln_gain), line(ln_bias), w_in, line(b_in),
            w_out, line(b_out), line(layer_scale), weight, low, high,
        )
        d_field, d_kernel, d_cb, d_gain, d_bias, d_win, d_bin, d_wout, d_bout, d_ls, norm = finish(*outs)
        wide = lambda v: v.reshape(-1)
        return (
            d_field, d_kernel, wide(d_cb), wide(d_gain), wide(d_bias), d_win, wide(d_bin),
            d_wout, wide(d_bout), wide(d_ls), norm.reshape(()),
        )

    grid = P("lat", "lon", None)
    return jax.shard_map(
        on_device,
        mesh=mesh,
        in_specs=(grid, grid, grid) + (P(),) * 8,
        out_specs=(grid,) + (P(),) * 10,
        check_vma=False,
    )
```
